32 devices in a mesh: dp: 8 (over z, x), chan: 4 (over y, core).
Axes of the slice: x: 2, y: 2, z: 4, core: 2. Of those that a mesh axis runs over, the one named last changes fastest.
Arguments:
- features: bfloat16 [12800, 512], P('dp', 'chan'), may hold values from -6 to 6
- shortcut: bfloat16 [12800, 2048], P('dp', 'chan'), may hold values from -6 to 6
- valid_masks: int32 [128, 100], P('dp'), may hold values from 0 to 1, as said below
- labels: int32 [128], P('dp'), may hold values from 0 to 999
- w_conv: float32 [4608, 512], P('dp', 'chan'), may hold values from -0.09375 to 0.09375
- w_proj: float32 [512, 2048], P('dp', 'chan'), may hold values from -0.25 to 0.25
- w_cls: float32 [2048, 1000], P(('chan', 'dp')), may hold values from -0.25 to 0.25
- cls_bias: float32 [1000], replicated, may hold values from -1.5 to 1.5
- norm_one: float32 [2, 512], P(None, 'chan'), may hold values from -0.6 to 1.5
- norm_two: float32 [2, 2048], P(None, 'chan'), may hold values from -0.6 to 1.5
- conv_moment: float32 [4608, 512], P('dp', 'chan'), may hold values from -0.0048828125 to 0.0048828125
- conv_second: float32 [4608, 512], P('dp', 'chan'), may hold values from 6.1035155e-07 to 2.4414062e-06
- proj_moment: float32 [512, 2048], P('dp', 'chan'), may hold values from -0.0078125 to 0.0078125
- proj_second: float32 [512, 2048], P('dp', 'chan'), may hold values from 1.8692017e-06 to 7.476807e-06
- cls_moment: float32 [2048, 1000], P(('chan', 'dp')), may hold values from -0.0234375 to 0.0234375
- cls_second: float32 [2048, 1000], P(('chan', 'dp')), may hold values from 1.7578124e-05 to 7.03125e-05
- bias_moment: float32 [1000], replicated, may hold values from -0.0390625 to 0.0390625
- bias_second: float32 [1000], replicated, may hold values from 4.8828126e-05 to 0.0001953125
- one_moment: float32 [2, 512], P(None, 'chan'), may hold values from -0.00140625 to 0.00140625
- one_second: float32 [2, 512], P(None, 'chan'), may hold values from 4.943848e-07 to 1.9775391e-06
- two_moment: float32 [2, 2048], P(None, 'chan'), may hold values from -0.0048828125 to 0.0048828125
- two_second: float32 [2, 2048], P(None, 'chan'), may hold values from 3.0899048e-06 to 2.3841858e-05
Outputs:
- new_w_conv: float32 [4608, 512], P('dp', 'chan')
- new_conv_moment: float32 [4608, 512], P('dp', 'chan')
- new_conv_second: float32 [4608, 512], P('dp', 'chan')
- new_w_proj: float32 [512, 2048], P('dp', 'chan')
- new_proj_moment: float32 [512, 2048], P('dp', 'chan')
- new_proj_second: float32 [512, 2048], P('dp', 'chan')
- new_w_cls: float32 [2048, 1000], P(('chan', 'dp'))
- new_cls_moment: float32 [2048, 1000], P(('chan', 'dp'))
- new_cls_second: float32 [2048, 1000], P(('chan', 'dp'))
- new_cls_bias: float32 [1000], replicated
- new_bias_moment: float32 [1000], replicated
- new_bias_second: float32 [1000], replicated
- new_norm_one: float32 [2, 512], P(None, 'chan')
- new_one_moment: float32 [2, 512], P(None, 'chan')
- new_one_second: float32 [2, 512], P(None, 'chan')
- new_norm_two: float32 [2, 2048], P(None, 'chan')
- new_two_moment: float32 [2, 2048], P(None, 'chan')
- new_two_second: float32 [2, 2048], P(None, 'chan')
- conv_copy: bfloat16 [4608, 512], P('dp', 'chan')
- proj_copy: bfloat16 [512, 2048], P('dp', 'chan')
- cls_copy: bfloat16 [2048, 1000], P(('chan', 'dp'))
- train_loss: float32 [], replicated
The draws below stay inside these ranges and needn't reach their ends.
Inputs may be any that keep to these rules, and one draw needn't show every extreme that they name: `valid_masks`: each image's valid pixels form a rectangle of 6 to 10 rows by 6 to 10 columns at the top left of its buffer.
All inputs are finite; a program needn't handle non-finite values.
Results may differ from the reference program's by a relative error of at most 0.015.
Values may be sent and summed in bfloat16 or wider, within the bound.
A program may use at most 128 MiB of HBM per device.

```python
import math
import jax
import jax.numpy as jnp
from jax import lax

C1 = 512
C2 = 2048
CLASSES = 1000
SIDE = 10
MICRO = 4
STEP = 3
IMG_DEV = 16
IMAGES = 128
N_DP = 8


def draw_shortcut(key, part):
    key = jax.random.fold_in(key, 51)
    first, second = jax.random.split(key)
    pixel = jax.random.normal(first, (IMAGES, SIDE * SIDE, C2), jnp.float32)
    image = jax.random.normal(second, (IMAGES, 1, C2), jnp.float32)
    total = jnp.clip(pixel + image, -6.0, 6.0)
    return total.reshape(IMAGES * SIDE * SIDE, C2).astype(jnp.bfloat16)


def draw_valid_masks(key, part):
    first, second = jax.random.split(jax.random.fold_in(key, 11))
    heights = jax.random.randint(first, (IMAGES, 1, 1), 6, SIDE + 1)
    widths = jax.random.randint(second, (IMAGES, 1, 1), 6, SIDE + 1)
    rows = jnp.arange(SIDE).reshape(1, SIDE, 1)
    across = jnp.arange(SIDE).reshape(1, 1, SIDE)
    inside = (rows < heights) & (across < widths)
    return inside.astype(jnp.int32).reshape(IMAGES, SIDE * SIDE)


def norm_params(key, count):
    first, second = jax.random.split(key)
    gains = jax.random.uniform(first, (1, count), jnp.float32, 0.5, 1.5)
    biases = jax.random.uniform(second, (1, count), jnp.float32, -0.6, 0.6)
    return jnp.concatenate([gains, biases], axis=0)


def norm_moment(key, count, gain_scale, bias_scale):
    scales = jnp.array([[gain_scale], [bias_scale]], jnp.float32) / jnp.sqrt(jnp.float32(count * IMAGES))
    return scales * jax.random.uniform(key, (2, count), jnp.float32, -2.0, 2.0)


def norm_second(key, count, gain_scale, bias_scale):
    scales = jnp.array([[gain_scale * gain_scale], [bias_scale * bias_scale]], jnp.float32) / jnp.float32(count * IMAGES)
    factor = jnp.exp(jax.random.uniform(key, (2, count), jnp.float32, 0.0, 1.3862944))
    return scales * factor


def draw_norm_one(key, part):
    return norm_params(jax.random.fold_in(key, 21), C1)


def draw_norm_two(key, part):
    return norm_params(jax.random.fold_in(key, 22), C2)


def draw_one_moment(key, part):
    return norm_moment(jax.random.fold_in(key, 31), C1, 0.18, 0.18)


def draw_two_moment(key, part):
    return norm_moment(jax.random.fold_in(key, 32), C2, 0.9, 1.25)


def draw_one_second(key, part):
    return norm_second(jax.random.fold_in(key, 41), C1, 0.18, 0.18)


def draw_two_second(key, part):
    return norm_second(jax.random.fold_in(key, 42), C2, 0.9, 1.25)


def plant(values, key, smallest, largest):
    longest = values.shape.index(max(values.shape))
    spots = []
    for shift in (0, 1):
        where = [jax.random.randint(jax.random.fold_in(key, axis), (), 0, length) for axis, length in enumerate(values.shape)]
        where[longest] = (where[longest] + shift) % values.shape[longest]
        spots.append(tuple(where))
    return values.at[spots[0]].set(smallest).at[spots[1]].set(largest)


def levels(rng, extent, cuts, least, top_value):
    gain, own = 1.0, jax.random.fold_in(rng, 6)
    for dim, blocks in cuts:
        draws = jnp.exp(jax.random.uniform(jax.random.fold_in(own, dim), (blocks,), jnp.float32, least / len(cuts), top_value / len(cuts)))
        gain = gain * jnp.repeat(draws, extent[dim] // blocks).reshape([-1 if axis == dim else 1 for axis in range(len(extent))])
    return gain


def bell_draw(key, shape, scale, bound, cuts=(), held_as=jnp.bfloat16):
    values = jax.random.normal(key, shape, jnp.float32) * scale
    if len(cuts) > 0:
        values = levels(key, shape, cuts, -0.22, 0.18) * values
    return jnp.clip(values, min=-bound, max=bound).astype(held_as)


def setup_inputs(seed: int = 0) -> dict:
    arg_keys = jax.random.split(jax.random.key(seed), 23)
    features = bell_draw(arg_keys[0], (IMAGES * SIDE * SIDE, C1), 1.0, 6.0, ((0, 8), (1, 4)))
    shortcut = draw_shortcut(jax.random.fold_in(arg_keys[22], 71), 0)
    valid_masks = draw_valid_masks(jax.random.fold_in(arg_keys[22], 71), 0)
    labels = plant(jax.random.randint(arg_keys[3], (IMAGES,), 0, CLASSES), jax.random.fold_in(arg_keys[3], 1), 0, CLASSES - 1).astype(jnp.int32)
    w_conv = bell_draw(arg_keys[4], (9 * C1, C1), (9 * C1) ** -0.5, 0.09375, ((0, 8), (1, 4)), jnp.float32)
    w_proj = bell_draw(arg_keys[5], (C1, C2), C1 ** -0.5, 0.25, ((0, 8), (1, 4)), jnp.float32)
    w_cls = bell_draw(arg_keys[6], (C2, CLASSES), (C2 // 4) ** -0.5, 0.25, ((0, 32),), jnp.float32)
    cls_bias = bell_draw(arg_keys[7], (CLASSES,), 0.3, 1.5, (), jnp.float32)
    norm_one = draw_norm_one(jax.random.fold_in(arg_keys[22], 71), 0)
    norm_two = draw_norm_two(jax.random.fold_in(arg_keys[22], 71), 0)
    conv_moment = bell_draw(arg_keys[10], (9 * C1, C1), (0.2 / (C1 * IMAGES) ** 0.5), 0.0048828125, ((0, 8), (1, 4)), jnp.float32)
    conv_second = jnp.clip(jnp.exp(math.log(2.441406195430318e-06) - 1.3862944 * jax.random.uniform(arg_keys[11], (9 * C1, C1), jnp.float32) ** levels(arg_keys[11], (9 * C1, C1), ((0, 8), (1, 4)), -0.2, 0.2)), 6.103515488575795e-07, 2.441406195430318e-06)
    proj_moment = bell_draw(arg_keys[12], (C1, C2), (0.7 / (C2 * IMAGES) ** 0.5), 0.0078125, ((0, 8), (1, 4)), jnp.float32)
    proj_second = jnp.clip(jnp.exp(math.log(7.476806786144152e-06) - 1.3862944 * jax.random.uniform(arg_keys[13], (C1, C2), jnp.float32) ** levels(arg_keys[13], (C1, C2), ((0, 8), (1, 4)), -0.2, 0.2)), 1.869201696536038e-06, 7.476806786144152e-06)
    cls_moment = bell_draw(arg_keys[14], (C2, CLASSES), (1.5 / (CLASSES * IMAGES) ** 0.5), 0.0234375, ((0, 32),), jnp.float32)
    cls_second = jnp.clip(jnp.exp(math.log(7.031249697320163e-05) - 1.3862944 * jax.random.uniform(arg_keys[15], (C2, CLASSES), jnp.float32) ** levels(arg_keys[15], (C2, CLASSES), ((0, 32),), -0.2, 0.2)), 1.7578124243300408e-05, 7.031249697320163e-05)
    bias_moment = bell_draw(arg_keys[16], (CLASSES,), (2.5 / (CLASSES * IMAGES) ** 0.5), 0.0390625, (), jnp.float32)
    bias_second = jnp.clip(jnp.exp(jax.random.uniform(arg_keys[17], (CLASSES,), jnp.float32, math.log(4.882812572759576e-05), math.log(0.0001953125))), 4.882812572759576e-05, 0.0001953125)
    one_moment = draw_one_moment(jax.random.fold_in(arg_keys[22], 71), 0)
    one_second = draw_one_second(jax.random.fold_in(arg_keys[22], 71), 0)
    two_moment = draw_two_moment(jax.random.fold_in(arg_keys[22], 71), 0)
    two_second = draw_two_second(jax.random.fold_in(arg_keys[22], 71), 0)
    return dict(features=features, shortcut=shortcut, valid_masks=valid_masks, labels=labels, w_conv=w_conv, w_proj=w_proj, w_cls=w_cls, cls_bias=cls_bias, norm_one=norm_one, norm_two=norm_two, conv_moment=conv_moment, conv_second=conv_second, proj_moment=proj_moment, proj_second=proj_second, cls_moment=cls_moment, cls_second=cls_second, bias_moment=bias_moment, bias_second=bias_second, one_moment=one_moment, one_second=one_second, two_moment=two_moment, two_second=two_second)


highest = lax.Precision.HIGHEST
norm_eps = 1e-05
adam_eps = 1e-08
beta_decay = 0.5
rate_matrix = 0.02
rate_small = 0.5
weight_decay = 0.01

@jax.custom_vjp
def low(v):
    return lax.optimization_barrier(v.astype(jnp.bfloat16)).astype(jnp.float32)

@jax.custom_vjp
def low_back(v):
    return v

def low_keep(v):
    return (low(v), None)

def low_pass(kept, grad):
    return (grad,)

def back_keep(v):
    return (v, None)

def back_low(kept, grad):
    return (low(grad),)
low.defvjp(low_keep, low_pass)
low_back.defvjp(back_keep, back_low)

def batch_norm(hidden, weights, params):
    count = jnp.sum(weights)
    center = lax.optimization_barrier(jnp.sum(hidden * weights, axis=(0, 1, 2))) / count
    spread = lax.optimization_barrier(jnp.sum(hidden * hidden * weights, axis=(0, 1, 2))) / count - center * center
    return params[0] * (hidden - center) * lax.rsqrt(spread + norm_eps) + params[1]

def forward(params, feat_blocks, short_blocks, mask_blocks, label_blocks):
    w_conv, w_proj, w_cls, cls_bias, norm_one, norm_two = params
    kernel = low(w_conv).reshape(3, 3, C1, C1)
    project = low(w_proj)
    classify = low(w_cls)
    total = jnp.zeros((), jnp.float32)
    for block in range(MICRO):
        weights = mask_blocks[block]
        hidden = lax.conv_general_dilated(feat_blocks[block] * weights, kernel, (1, 1), 'SAME', dimension_numbers=('NHWC', 'HWIO', 'NHWC'), precision=highest)
        hidden = low_back(hidden)
        active = low(jax.nn.silu(batch_norm(hidden, weights, norm_one)) * weights)
        second = low_back(jnp.einsum('nhwc,cd->nhwd', active, project, precision=highest))
        summed = batch_norm(second, weights, norm_two) + short_blocks[block]
        output = jax.nn.silu(summed) * weights
        pooled = low(lax.optimization_barrier(jnp.sum(output, axis=(1, 2))) / lax.optimization_barrier(jnp.sum(weights, axis=(1, 2))))
        logits = low_back(jnp.dot(pooled, classify, precision=highest) + cls_bias)
        picked = jnp.take_along_axis(logits, label_blocks[block][:, None], axis=1)[:, 0]
        total = total + jnp.sum(jax.nn.logsumexp(logits, axis=1) - picked)
    return total / IMAGES

def split_blocks(array, trailing):
    shaped = array.reshape((N_DP, MICRO, IMG_DEV // MICRO) + trailing)
    return [shaped[:, block].reshape((-1,) + trailing) for block in range(MICRO)]

def adam_step(weight, moment, second, grad, rate, decay):
    moment = beta_decay * moment + (1.0 - beta_decay) * grad
    second = beta_decay * second + (1.0 - beta_decay) * grad * grad
    correct = 1.0 - beta_decay ** STEP
    weight = weight - rate * (moment / correct / (jnp.sqrt(second / correct) + adam_eps) + decay * weight)
    return (weight, moment, second)

def reference(features, shortcut, valid_masks, labels, w_conv, w_proj, w_cls, cls_bias, norm_one, norm_two, conv_moment, conv_second, proj_moment, proj_second, cls_moment, cls_second, bias_moment, bias_second, one_moment, one_second, two_moment, two_second):
    feat_blocks = split_blocks(features.astype(jnp.float32), (SIDE, SIDE, C1))
    short_blocks = split_blocks(shortcut.astype(jnp.float32), (SIDE, SIDE, C2))
    mask_blocks = split_blocks(valid_masks.astype(jnp.float32), (SIDE, SIDE, 1))
    label_blocks = split_blocks(labels, ())
    params = (w_conv, w_proj, w_cls, cls_bias, norm_one, norm_two)
    loss_value, pullback = jax.vjp(lambda p: forward(p, feat_blocks, short_blocks, mask_blocks, label_blocks), params)
    grads = pullback(jnp.ones((), jnp.float32))[0]
    conv_w, conv_m, conv_v = adam_step(w_conv, conv_moment, conv_second, grads[0], rate_matrix, weight_decay)
    proj_w, proj_m, proj_v = adam_step(w_proj, proj_moment, proj_second, grads[1], rate_matrix, weight_decay)
    cls_w, cls_m, cls_v = adam_step(w_cls, cls_moment, cls_second, grads[2], rate_matrix, weight_decay)
    bias_w, bias_m, bias_v = adam_step(cls_bias, bias_moment, bias_second, grads[3], rate_small, 0.0)
    one_w, one_m, one_v = adam_step(norm_one, one_moment, one_second, grads[4], rate_small, 0.0)
    two_w, two_m, two_v = adam_step(norm_two, two_moment, two_second, grads[5], rate_small, 0.0)
    return (conv_w, conv_m, conv_v, proj_w, proj_m, proj_v, cls_w, cls_m, cls_v, bias_w, bias_m, bias_v, one_w, one_m, one_v, two_w, two_m, two_v, conv_w.astype(jnp.bfloat16), proj_w.astype(jnp.bfloat16), cls_w.astype(jnp.bfloat16), loss_value)
```

```python
import jax
import jax.numpy as jnp
from jax import lax
from jax.sharding import PartitionSpec as P

SIDE = 10
MICRO = 4
STEP = 3


norm_eps = 1e-05
adam_eps = 1e-08
beta_decay = 0.5
rate_matrix = 0.02
rate_small = 0.5
weight_decay = 0.01


def tap_columns(flat, images):
    width = flat.shape[1]
    grid = flat.reshape(images, SIDE, SIDE, width)
    padded = jnp.pad(grid, ((0, 0), (1, 1), (1, 1), (0, 0)))
    pieces = [
        padded[:, down : down + SIDE, across : across + SIDE, :]
        for down in range(3)
        for across in range(3)
    ]
    return jnp.concatenate(pieces, axis=3).reshape(images * SIDE * SIDE, 9 * width)


def silu_slope(value):
    sigma = jax.nn.sigmoid(value)
    return sigma * (1.0 + value * (1.0 - sigma))


def norm_forward(hidden, weights, params):
    sums, squares, count = lax.psum(
        (
            jnp.sum(hidden * weights, axis=1),
            jnp.sum(hidden * hidden * weights, axis=1),
            jnp.sum(weights, axis=1),
        ),
        "dp",
    )
    center = sums / count
    scale = lax.rsqrt(squares / count - center * center + norm_eps)
    normed = (hidden - center[:, None]) * scale[:, None]
    return (params[0] * normed + params[1], normed, scale[:, None], count[:, None])


def norm_backward(upstream, normed, scale, count, weights, params):
    total, along = lax.psum((jnp.sum(upstream, axis=1), jnp.sum(upstream * normed, axis=1)), "dp")
    grad = (
        weights
        * params[0]
        * scale
        * (upstream - (total[:, None] + normed * along[:, None]) / count)
    )
    return (grad, jnp.stack([jnp.sum(along, axis=0), jnp.sum(total, axis=0)]))


def contract_rows(left, right):
    return lax.dot_general(
        left, right, (((0,), (0,)), ((), ())), preferred_element_type=jnp.float32
    )


def contract_cols(left, right):
    return lax.dot_general(
        left, right, (((1,), (1,)), ((), ())), preferred_element_type=jnp.float32
    )


def adam_step(weight, moment, second, grad, rate, decay):
    moment = beta_decay * moment + (1.0 - beta_decay) * grad
    second = beta_decay * second + (1.0 - beta_decay) * grad * grad
    correct = 1.0 - beta_decay**STEP
    weight = weight - rate * (
        moment / correct / (jnp.sqrt(second / correct) + adam_eps) + decay * weight
    )
    return (weight, moment, second)


def per_device(
    features,
    shortcut,
    valid_masks,
    labels,
    w_conv,
    w_proj,
    w_cls,
    cls_bias,
    norm_one,
    norm_two,
    conv_moment,
    conv_second,
    proj_moment,
    proj_second,
    cls_moment,
    cls_second,
    bias_moment,
    bias_second,
    one_moment,
    one_second,
    two_moment,
    two_second,
):
    images = valid_masks.shape[0]
    area = SIDE * SIDE
    pixels = images * area
    total_images = images * lax.axis_size("dp")
    classes = w_cls.shape[1]
    conv_full, proj_full, cls_full = (
        lax.all_gather(w_conv.astype(jnp.bfloat16), "dp", axis=0, tiled=True),
        lax.all_gather(w_proj.astype(jnp.bfloat16), "dp", axis=0, tiled=True),
        lax.all_gather(w_cls.astype(jnp.bfloat16), "dp", axis=0, tiled=True),
    )

    def split(flat):
        return flat.reshape((MICRO, -1) + flat.shape[1:])

    def join(parts):
        return parts.reshape((-1,) + parts.shape[2:])

    image_mask = valid_masks.astype(jnp.float32)
    pixel_counts = jnp.sum(image_mask, axis=1)
    weights = split(image_mask.reshape(pixels, 1))
    masked = features * join(weights).astype(jnp.bfloat16)
    gathered = lax.all_gather(masked, "chan", axis=1, tiled=True)
    columns = tap_columns(gathered, images)
    hidden = jnp.dot(columns, conv_full, preferred_element_type=jnp.float32)
    shifted, normed_one, scale_one, count = norm_forward(split(hidden), weights, norm_one)
    active = join((jax.nn.silu(shifted) * weights).astype(jnp.bfloat16))
    active_full = lax.all_gather(active, "chan", axis=1, tiled=True)
    second = jnp.dot(active_full, proj_full, preferred_element_type=jnp.float32)
    shifted_two, normed_two, scale_two, _ = norm_forward(split(second), weights, norm_two)
    summed = shifted_two + split(shortcut.astype(jnp.float32))
    output = jax.nn.silu(summed) * weights
    channels = shortcut.shape[1]
    pooled = (
        jnp.sum(output.reshape(images, area, channels), axis=1) / pixel_counts[:, None]
    ).astype(jnp.bfloat16)
    partial_value = jnp.dot(pooled, cls_full, preferred_element_type=jnp.float32)
    logits = lax.psum(partial_value, "chan") + cls_bias
    top = jnp.max(logits, axis=1, keepdims=True)
    expo = jnp.exp(logits - top)
    expo_sum = jnp.sum(expo, axis=1, keepdims=True)
    onehot = (labels[:, None] == jnp.arange(classes)[None, :]).astype(jnp.float32)
    picked = jnp.sum(logits * onehot, axis=1)
    loss_sum = jnp.sum(top[:, 0] + jnp.log(expo_sum[:, 0]) - picked)
    dlogits = ((expo / expo_sum - onehot) / total_images).astype(jnp.bfloat16)
    grad_bias = jnp.sum(dlogits.astype(jnp.float32), axis=0)
    local_cls = contract_rows(pooled, dlogits)
    grad_pool = contract_cols(dlogits, cls_full)
    spread_back = jnp.broadcast_to(
        (grad_pool / pixel_counts[:, None])[:, None, :], (images, area, channels)
    ).reshape(MICRO, -1, channels)
    upstream_two = spread_back * weights * silu_slope(summed)
    grad_second, grad_two = norm_backward(
        upstream_two, normed_two, scale_two, count, weights, norm_two
    )
    grad_second = join(grad_second.astype(jnp.bfloat16))
    local_proj = contract_rows(active_full, grad_second)
    partial_act = contract_cols(grad_second, proj_full)
    grad_active = lax.psum_scatter(
        partial_act.astype(jnp.bfloat16), "chan", scatter_dimension=1, tiled=True
    ).astype(jnp.float32)
    upstream_one = split(grad_active) * weights * silu_slope(shifted)
    grad_hidden, grad_one = norm_backward(
        upstream_one, normed_one, scale_one, count, weights, norm_one
    )
    local_conv = contract_rows(columns, join(grad_hidden.astype(jnp.bfloat16)))
    sum_conv, sum_proj, sum_cls = (
        lax.psum_scatter(
            local_conv.astype(jnp.bfloat16), "dp", scatter_dimension=0, tiled=True
        ).astype(jnp.float32),
        lax.psum_scatter(
            local_proj.astype(jnp.bfloat16), "dp", scatter_dimension=0, tiled=True
        ).astype(jnp.float32),
        lax.psum_scatter(
            local_cls.astype(jnp.bfloat16), "dp", scatter_dimension=0, tiled=True
        ).astype(jnp.float32),
    )
    loss_total, bias_total = lax.psum((loss_sum, grad_bias), "dp")
    train_loss = loss_total / total_images
    conv_w, conv_m, conv_v = adam_step(
        w_conv, conv_moment, conv_second, sum_conv, rate_matrix, weight_decay
    )
    proj_w, proj_m, proj_v = adam_step(
        w_proj, proj_moment, proj_second, sum_proj, rate_matrix, weight_decay
    )
    cls_w, cls_m, cls_v = adam_step(
        w_cls, cls_moment, cls_second, sum_cls, rate_matrix, weight_decay
    )
    bias_w, bias_m, bias_v = adam_step(
        cls_bias, bias_moment, bias_second, bias_total, rate_small, 0.0
    )
    one_w, one_m, one_v = adam_step(norm_one, one_moment, one_second, grad_one, rate_small, 0.0)
    two_w, two_m, two_v = adam_step(norm_two, two_moment, two_second, grad_two, rate_small, 0.0)
    return (
        conv_w,
        conv_m,
        conv_v,
        proj_w,
        proj_m,
        proj_v,
        cls_w,
        cls_m,
        cls_v,
        bias_w,
        bias_m,
        bias_v,
        one_w,
        one_m,
        one_v,
        two_w,
        two_m,
        two_v,
        conv_w.astype(jnp.bfloat16),
        proj_w.astype(jnp.bfloat16),
        cls_w.astype(jnp.bfloat16),
        train_loss,
    )


def solution(mesh):
    placed = (
        P("dp", "chan"),
        P("dp", "chan"),
        P("dp", None),
        P("dp"),
        P("dp", "chan"),
        P("dp", "chan"),
        P(("chan", "dp"), None),
        P(),
        P(None, "chan"),
        P(None, "chan"),
        P("dp", "chan"),
        P("dp", "chan"),
        P("dp", "chan"),
        P("dp", "chan"),
        P(("chan", "dp"), None),
        P(("chan", "dp"), None),
        P(),
        P(),
        P(None, "chan"),
        P(None, "chan"),
        P(None, "chan"),
        P(None, "chan"),
    )
    return jax.shard_map(
        per_device,
        mesh=mesh,
        in_specs=placed,
        out_specs=(
            P("dp", "chan"),
            P("dp", "chan"),
            P("dp", "chan"),
            P("dp", "chan"),
            P("dp", "chan"),
            P("dp", "chan"),
            P(("chan", "dp"), None),
            P(("chan", "dp"), None),
            P(("chan", "dp"), None),
            P(),
            P(),
            P(),
            P(None, "chan"),
            P(None, "chan"),
            P(None, "chan"),
            P(None, "chan"),
            P(None, "chan"),
            P(None, "chan"),
            P("dp", "chan"),
            P("dp", "chan"),
            P(("chan", "dp"), None),
            P(),
        ),
        check_vma=False,
    )
```

```python
import functools

import jax
import jax.numpy as jnp
from jax import lax
from jax.experimental import pallas as pl
from jax.experimental.pallas import tpu as pltpu
from jax.sharding import PartitionSpec as P

SIDE = 10
MICRO = 4
STEP = 3


norm_eps = 1e-05
adam_eps = 1e-08
beta_decay = 0.5
rate_matrix = 0.02
rate_small = 0.5
weight_decay = 0.01


def tap_columns(flat, images):
    width = flat.shape[1]
    grid = flat.reshape(images, SIDE, SIDE, width)
    padded = jnp.pad(grid, ((0, 0), (1, 1), (1, 1), (0, 0)))
    pieces = [
        padded[:, down : down + SIDE, across : across + SIDE, :]
        for down in range(3)
        for across in range(3)
    ]
    return jnp.concatenate(pieces, axis=3).reshape(images * SIDE * SIDE, 9 * width)


def silu_slope(value):
    sigma = jax.nn.sigmoid(value)
    return sigma * (1.0 + value * (1.0 - sigma))


def norm_forward(hidden, weights, params):
    sums, squares, count = lax.psum(
        (
            jnp.sum(hidden * weights, axis=1),
            jnp.sum(hidden * hidden * weights, axis=1),
            jnp.sum(weights, axis=1),
        ),
        "dp",
    )
    center = sums / count
    scale = lax.rsqrt(squares / count - center * center + norm_eps)
    normed = (hidden - center[:, None]) * scale[:, None]
    return (params[0] * normed + params[1], normed, scale[:, None], count[:, None])


def norm_backward(upstream, normed, scale, count, weights, params):
    total, along = lax.psum((jnp.sum(upstream, axis=1), jnp.sum(upstream * normed, axis=1)), "dp")
    grad = (
        weights
        * params[0]
        * scale
        * (upstream - (total[:, None] + normed * along[:, None]) / count)
    )
    return (grad, jnp.stack([jnp.sum(along, axis=0), jnp.sum(total, axis=0)]))


def contract_rows(left, right):
    return lax.dot_general(
        left, right, (((0,), (0,)), ((), ())), preferred_element_type=jnp.float32
    )


def contract_cols(left, right):
    return lax.dot_general(
        left, right, (((1,), (1,)), ((), ())), preferred_element_type=jnp.float32
    )


def adam_step(weight, moment, second, grad, rate, decay):
    moment = beta_decay * moment + (1.0 - beta_decay) * grad
    second = beta_decay * second + (1.0 - beta_decay) * grad * grad
    correct = 1.0 - beta_decay**STEP
    weight = weight - rate * (
        moment / correct / (jnp.sqrt(second / correct) + adam_eps) + decay * weight
    )
    return (weight, moment, second)


def per_device(
    features,
    shortcut,
    valid_masks,
    labels,
    w_conv,
    w_proj,
    w_cls,
    cls_bias,
    norm_one,
    norm_two,
    conv_moment,
    conv_second,
    proj_moment,
    proj_second,
    cls_moment,
    cls_second,
    bias_moment,
    bias_second,
    one_moment,
    one_second,
    two_moment,
    two_second,
):
    images = valid_masks.shape[0]
    area = SIDE * SIDE
    pixels = images * area
    total_images = images * lax.axis_size("dp")
    classes = w_cls.shape[1]
    conv_full, proj_full, cls_full = (
        lax.all_gather(w_conv.astype(jnp.bfloat16), "dp", axis=0, tiled=True),
        lax.all_gather(w_proj.astype(jnp.bfloat16), "dp", axis=0, tiled=True),
        lax.all_gather(w_cls.astype(jnp.bfloat16), "dp", axis=0, tiled=True),
    )

    def split(flat):
        return flat.reshape((MICRO, -1) + flat.shape[1:])

    def join(parts):
        return parts.reshape((-1,) + parts.shape[2:])

    image_mask = valid_masks.astype(jnp.float32)
    pixel_counts = jnp.sum(image_mask, axis=1)
    weights = split(image_mask.reshape(pixels, 1))
    masked = features * join(weights).astype(jnp.bfloat16)
    gathered = lax.all_gather(masked, "chan", axis=1, tiled=True)
    columns = tap_columns(gathered, images)
    hidden = jnp.dot(columns, conv_full, preferred_element_type=jnp.float32)
    shifted, normed_one, scale_one, count = norm_forward(split(hidden), weights, norm_one)
    active = join((jax.nn.silu(shifted) * weights).astype(jnp.bfloat16))
    active_full = lax.all_gather(active, "chan", axis=1, tiled=True)
    second = jnp.dot(active_full, proj_full, preferred_element_type=jnp.float32)
    shifted_two, normed_two, scale_two, _ = norm_forward(split(second), weights, norm_two)
    summed = shifted_two + split(shortcut.astype(jnp.float32))
    output = jax.nn.silu(summed) * weights
    channels = shortcut.shape[1]
    pooled = (
        jnp.sum(output.reshape(images, area, channels), axis=1) / pixel_counts[:, None]
    ).astype(jnp.bfloat16)
    partial_value = jnp.dot(pooled, cls_full, preferred_element_type=jnp.float32)
    logits = lax.psum(partial_value, "chan") + cls_bias
    top = jnp.max(logits, axis=1, keepdims=True)
    expo = jnp.exp(logits - top)
    expo_sum = jnp.sum(expo, axis=1, keepdims=True)
    onehot = (labels[:, None] == jnp.arange(classes)[None, :]).astype(jnp.float32)
    picked = jnp.sum(logits * onehot, axis=1)
    loss_sum = jnp.sum(top[:, 0] + jnp.log(expo_sum[:, 0]) - picked)
    dlogits = ((expo / expo_sum - onehot) / total_images).astype(jnp.bfloat16)
    grad_bias = jnp.sum(dlogits.astype(jnp.float32), axis=0)
    local_cls = contract_rows(pooled, dlogits)
    grad_pool = contract_cols(dlogits, cls_full)
    spread_back = jnp.broadcast_to(
        (grad_pool / pixel_counts[:, None])[:, None, :], (images, area, channels)
    ).reshape(MICRO, -1, channels)
    upstream_two = spread_back * weights * silu_slope(summed)
    grad_second, grad_two = norm_backward(
        upstream_two, normed_two, scale_two, count, weights, norm_two
    )
    grad_second = join(grad_second.astype(jnp.bfloat16))
    local_proj = contract_rows(active_full, grad_second)
    partial_act = contract_cols(grad_second, proj_full)
    grad_active = lax.psum_scatter(
        partial_act.astype(jnp.bfloat16), "chan", scatter_dimension=1, tiled=True
    ).astype(jnp.float32)
    upstream_one = split(grad_active) * weights * silu_slope(shifted)
    grad_hidden, grad_one = norm_backward(
        upstream_one, normed_one, scale_one, count, weights, norm_one
    )
    local_conv = contract_rows(columns, join(grad_hidden.astype(jnp.bfloat16)))
    sum_conv, sum_proj, sum_cls = (
        lax.psum_scatter(
            local_conv.astype(jnp.bfloat16), "dp", scatter_dimension=0, tiled=True
        ).astype(jnp.float32),
        lax.psum_scatter(
            local_proj.astype(jnp.bfloat16), "dp", scatter_dimension=0, tiled=True
        ).astype(jnp.float32),
        lax.psum_scatter(
            local_cls.astype(jnp.bfloat16), "dp", scatter_dimension=0, tiled=True
        ).astype(jnp.float32),
    )
    loss_total, bias_total = lax.psum((loss_sum, grad_bias), "dp")
    train_loss = loss_total / total_images
    conv_w, conv_m, conv_v = adam_step(
        w_conv, conv_moment, conv_second, sum_conv, rate_matrix, weight_decay
    )
    proj_w, proj_m, proj_v = adam_step(
        w_proj, proj_moment, proj_second, sum_proj, rate_matrix, weight_decay
    )
    cls_w, cls_m, cls_v = adam_step(
        w_cls, cls_moment, cls_second, sum_cls, rate_matrix, weight_decay
    )
    bias_w, bias_m, bias_v = adam_step(
        cls_bias, bias_moment, bias_second, bias_total, rate_small, 0.0
    )
    one_w, one_m, one_v = adam_step(norm_one, one_moment, one_second, grad_one, rate_small, 0.0)
    two_w, two_m, two_v = adam_step(norm_two, two_moment, two_second, grad_two, rate_small, 0.0)
    return (
        conv_w,
        conv_m,
        conv_v,
        proj_w,
        proj_m,
        proj_v,
        cls_w,
        cls_m,
        cls_v,
        bias_w,
        bias_m,
        bias_v,
        one_w,
        one_m,
        one_v,
        two_w,
        two_m,
        two_v,
        conv_w.astype(jnp.bfloat16),
        proj_w.astype(jnp.bfloat16),
        cls_w.astype(jnp.bfloat16),
        train_loss,
    )


MESH = pl.DeviceIdType.MESH
AREA = SIDE * SIDE
PAD = 16
BF = jnp.bfloat16
F32 = jnp.float32


def flip(value, bits):
    bit = 1
    while bit <= bits:
        if bits & bit:
            value = value + bit - 2 * bit * (lax.div(value, bit) % 2)
        bit *= 2
    return value


def nt_dot(left, right):
    return lax.dot_general(left, right, (((1,), (1,)), ((), ())), preferred_element_type=F32)


def mm(left, right):
    return jnp.dot(left, right, preferred_element_type=F32)


def sigmoid(value):
    return 1.0 / (1.0 + jnp.exp(-value))


def row_iota(shape):
    return lax.broadcasted_iota(jnp.int32, shape, 0)


def lane_iota(shape):
    return lax.broadcasted_iota(jnp.int32, shape, 1)


def fused_kernel(dims, *refs):
    nd, nc, pm, imb, c1l, c2l, r1, rp, rc, classes, total_images = dims
    (
        feat, short, masks, labels, wconv, wproj, wcls, cbias, n1, n2,
        gconv, gproj, gcls, gbias, gone, gtwo, gloss,
        wf, pf, cf, wfull, pfull, cfull, xv, sv, xm, xt, yb, hid, mk, edge, cntm, cnti,
        af, at, sec, slp, bn1, bn2, tsum, pool, lgt, dlm, dpd, dsb, da, dab, sr, es, er,
        du, dhp, acc, pacc, st0, st1, st2, st3, st4,
        gcs, gcx, gcz, gcr, gps, gpx, gpz, gpr, dla, pla, plt,
        ld_s, cw_s, cw_r, pw_s, pw_r, kw_s, kw_r, fx_s, fx_r, af_s, af_r, s0_s, s0_r, s1_s, s1_r,
        s2_s, s2_r, s3_s, s3_r, s4_s, s4_r, lg_s, lg_r, sr_s, sr_r, er_s, er_r,
        dl_s, dl_r, pl_s, pl_r, gcx_s, gcx_r, gcz_s, gcz_r, gpx_s, gpx_r, gpz_s, gpz_r,
    ) = refs
    nz = nd // 2
    c1 = c1l * nc
    nq = c2l // 128
    d = lax.axis_index("dp")
    c = lax.axis_index("chan")
    z, x = lax.div(d, 2), d % 2
    y, k = lax.div(c, 2), c % 2
    sib = y * 2 + 1 - k
    opp = (1 - y) * 2 + k
    dia = (1 - y) * 2 + 1 - k
    xdev = (z * 2 + 1 - x, c)
    sibdev = (d, sib)
    oppdev = (d, opp)

    def zdev(j):
        return (flip(z, j) * 2 + x, c)

    def remote(src, dst, ssem, rsem, dev):
        return pltpu.make_async_remote_copy(
            src_ref=src, dst_ref=dst, send_sem=ssem, recv_sem=rsem,
            device_id=dev, device_id_type=MESH,
        )

    def unit(buf, u, rows):
        return buf.at[pl.ds(pl.multiple_of(u * rows, rows), rows)]

    def gather_start(buf, rows, ss, rr):
        mine = unit(buf, d, rows)
        remote(mine, mine, ss.at[0], rr.at[d], xdev).start()
        for j in range(1, nz):
            remote(mine, mine, ss.at[j], rr.at[d], zdev(j)).start()

    def gather_forward(buf, rows, ss, rr, j):
        u = flip(z, j) * 2 + x
        got = unit(buf, u, rows)
        copy = remote(got, got, ss.at[nz + j], rr.at[u], xdev)
        copy.wait_recv()
        copy.start()

    def gather_finish(buf, rows, ss, rr):
        for j in range(nz):
            u = flip(z, j) * 2 + 1 - x
            got = unit(buf, u, rows)
            remote(got, got, ss.at[0], rr.at[u], xdev).wait_recv()

    def gather_drain(buf, rows, ss, rr):
        mine = unit(buf, d, rows)
        for j in range(2 * nz):
            if j != nz:
                remote(mine, mine, ss.at[j], rr.at[d], xdev).wait_send()

    def peers():
        return [flip(d, p) for p in range(1, nd)]

    def stats_send(buf, ss, rr):
        for p in range(1, nd):
            u = flip(d, p)
            remote(buf.at[d], buf.at[d], ss.at[p], rr.at[d], (u, c)).start()

    def stats_wait(buf, ss, rr):
        for p in range(1, nd):
            u = flip(d, p)
            remote(buf.at[u], buf.at[u], ss.at[p], rr.at[u], (u, c)).wait_recv()

    def stats_sum(buf):
        total = buf[0]
        for p in range(1, nd):
            total = total + buf[p]
        return total

    def stats_drain(buf, ss, rr):
        for p in range(1, nd):
            u = flip(d, p)
            remote(buf.at[d], buf.at[d], ss.at[p], rr.at[d], (u, c)).wait_send()

    def rows(m):
        return pl.ds(pl.multiple_of(m * pm, pm), pm)

    def lanes(chunk):
        return pl.ds(pl.multiple_of(chunk * c1l, c1l), c1l)

    def part(buf, m, chunk):
        return buf.at[rows(m), lanes(chunk)]

    def local(src, dst, i):
        return pltpu.make_async_copy(src, dst, ld_s.at[i])

    loads = [
        local(wconv, wf, 0),
        local(wproj, pf, 1),
        local(wcls, cf, 2),
        local(feat, xv.at[:, lanes(c)], 3),
        local(short, sv, 4),
    ]
    for load in loads:
        load.start()

    barrier = pltpu.get_barrier_semaphore()
    others = [(u, c) for u in peers()] + [sibdev, oppdev, (d, dia)]
    for dev in others:
        pl.semaphore_signal(barrier, inc=1, device_id=dev, device_id_type=MESH)
    loads[0].wait()
    wfull[pl.ds(pl.multiple_of(d * r1, r1), r1), :] = wf[...].astype(BF)
    pl.semaphore_wait(barrier, len(others))

    gather_start(wfull, r1, cw_s, cw_r)
    for m in range(MICRO):
        src = feat.at[pl.ds(m * pm, pm)]
        remote(src, part(xv, m, c), fx_s.at[0, m], fx_r.at[c, m], oppdev).start()
        remote(src, part(xv, m, c), fx_s.at[1, m], fx_r.at[c, m], sibdev).start()

    loads[1].wait()
    pfull[pl.ds(pl.multiple_of(d * rp, rp), rp), :] = pf[...].astype(BF)
    loads[2].wait()
    cfull[pl.ds(pl.multiple_of(d * rc, rc), rc), :] = cf[...].astype(BF)

    pixel = row_iota((pm, 128))
    image = jnp.zeros((pm, 128), jnp.int32)
    for i in range(1, imb):
        image = image + (pixel >= AREA * i).astype(jnp.int32)
    pixel = pixel - AREA * image
    line = jnp.zeros((pm, 128), jnp.int32)
    for i in range(1, SIDE):
        line = line + (pixel >= SIDE * i).astype(jnp.int32)
    across = pixel - SIDE * line
    edge[0] = (line > 0).astype(F32)
    edge[1] = (line < SIDE - 1).astype(F32)
    edge[2] = (across > 0).astype(F32)
    edge[3] = (across < SIDE - 1).astype(F32)
    mask_bf = masks[...].astype(F32).astype(BF)
    images = imb * MICRO
    chosen = (pixel[:, :AREA] == lane_iota((pm, AREA))).astype(F32)
    ones = jnp.ones((AREA, 128), BF)
    image_count = jnp.sum(masks[...].astype(F32), axis=1, keepdims=True)
    for m in range(MICRO):
        away = row_iota((pm, images)) - AREA * (lane_iota((pm, images)) - imb * m)
        owner = jnp.where((away >= 0) & (away < AREA), 1.0, 0.0).astype(BF)
        spread = mm((mm(owner, mask_bf) * chosen).astype(BF), ones)
        mk[m] = spread
        cntm[m] = jnp.sum(spread, axis=0, keepdims=True)
        cnti[m] = jnp.broadcast_to(image_count[m * imb : (m + 1) * imb], (imb, 128))
        st0[d, m : m + 1, :] = cntm[m]
    stats_send(st0, s0_s, s0_r)

    yb[:, 0:PAD, :] = jnp.zeros((9, PAD, c1l), F32)
    yb[:, PAD + pm :, :] = jnp.zeros((9, PAD, c1l), F32)
    dhp[0:PAD, :] = jnp.zeros((PAD, c1l), F32)
    dhp[PAD + pm :, :] = jnp.zeros((PAD, c1l), F32)

    for m in range(MICRO):
        got = part(xv, m, opp)
        copy = remote(got, got, fx_s.at[2, m], fx_r.at[opp, m], sibdev)
        copy.wait_recv()
        copy.start()
        if 1 <= m < nz:
            gather_forward(wfull, r1, cw_s, cw_r, m)
    for j in range(MICRO, nz):
        gather_forward(wfull, r1, cw_s, cw_r, j)
    loads[3].wait()

    def take_features(m, carry):
        for chunk in (sib, dia):
            got = part(xv, m, chunk)
            remote(got, got, fx_s.at[2, m], fx_r.at[chunk, m], sibdev).wait_recv()
        flat_mask = mk[m].astype(BF)
        for q in range(nc):
            piece = xv[rows(m), q * c1l : (q + 1) * c1l] * flat_mask
            xm[m, :, q * c1l : (q + 1) * c1l] = piece
            xt[m, q * c1l : (q + 1) * c1l, :] = piece.T
        return carry

    lax.fori_loop(0, MICRO, take_features, 0)
    gather_finish(wfull, r1, cw_s, cw_r)
    gather_start(pfull, rp, pw_s, pw_r)

    def tap(t):
        return wfull[t * c1 : (t + 1) * c1, :]

    def edges(ky, kx):
        found = None
        if ky == 0:
            found = edge[0]
        if ky == 2:
            found = edge[1]
        if kx == 0:
            found = edge[2] if found is None else found * edge[2]
        if kx == 2:
            found = edge[3] if found is None else found * edge[3]
        return found

    def conv(m, carry):
        inputs = xm[m]
        for t in range(0, 9, 2):
            if t < 8:
                pair = mm(inputs, jnp.concatenate([tap(t), tap(t + 1)], axis=1))
                yb[t, PAD : PAD + pm, :] = pair[:, :c1l]
                yb[t + 1, PAD : PAD + pm, :] = pair[:, c1l:]
            else:
                yb[t, PAD : PAD + pm, :] = mm(inputs, tap(t))
        hidden = None
        for kx in range(3):
            column = None
            for ky in range(3):
                off = PAD + (ky - 1) * SIDE + kx - 1
                value = yb[3 * ky + kx, off : off + pm, :]
                if ky != 1:
                    value = value * edge[0 if ky == 0 else 1]
                column = value if column is None else column + value
            if kx != 1:
                column = column * edge[2 if kx == 0 else 3]
            hidden = column if hidden is None else hidden + column
        hid[m] = hidden
        valid = hidden * mk[m]
        st1[d, pl.ds(m, 1), :] = jnp.sum(valid, axis=0, keepdims=True)
        st1[d, pl.ds(MICRO + m, 1), :] = jnp.sum(valid * hidden, axis=0, keepdims=True)
        return carry

    lax.fori_loop(0, MICRO, conv, 0)
    stats_send(st1, s1_s, s1_r)
    for j in range(1, nz):
        gather_forward(pfull, rp, pw_s, pw_r, j)
    acc[...] = jnp.zeros_like(acc)
    pacc[...] = jnp.zeros_like(pacc)

    stats_wait(st0, s0_s, s0_r)
    counts = stats_sum(st0)
    stats_wait(st1, s1_s, s1_r)
    totals = stats_sum(st1)
    for m in range(MICRO):
        n = counts[m : m + 1, :]
        cntm[m] = n
        center = totals[m : m + 1, :] / n
        spread = totals[MICRO + m : MICRO + m + 1, :] / n - center * center
        bn1[m, 0:1, :] = center
        bn1[m, 1:2, :] = lax.rsqrt(spread + norm_eps)

    def activate(m, carry):
        normed = (hid[m] - bn1[m, 0:1, :]) * bn1[m, 1:2, :]
        shifted = n1[0:1, :] * normed + n1[1:2, :]
        active = (shifted * sigmoid(shifted) * mk[m]).astype(BF)
        mine = part(af, m, c)
        mine[...] = active
        remote(mine, mine, af_s.at[0, m], af_r.at[c, m], oppdev).start()
        remote(mine, mine, af_s.at[1, m], af_r.at[c, m], sibdev).start()
        return carry

    lax.fori_loop(0, MICRO, activate, 0)
    gather_start(cfull, rc, kw_s, kw_r)
    gather_finish(pfull, rp, pw_s, pw_r)
    loads[4].wait()

    def turn(m, chunk):
        at[m, lanes_sub(chunk), :] = part(af, m, chunk)[...].T

    def lanes_sub(chunk):
        return pl.ds(pl.multiple_of(chunk * c1l, c1l), c1l)

    def stage_a(m):
        got = part(af, m, opp)
        copy = remote(got, got, af_s.at[2, m], af_r.at[opp, m], sibdev)
        copy.wait_recv()
        copy.start()
        turn(m, c)
        turn(m, opp)
        got = part(af, m, sib)
        remote(got, got, af_s.at[2, m], af_r.at[sib, m], sibdev).wait_recv()
        turn(m, sib)
        got = part(af, m, dia)
        remote(got, got, af_s.at[2, m], af_r.at[dia, m], sibdev).wait_recv()
        turn(m, dia)
        second = mm(af[rows(m), :], pfull[...])
        sec[m] = second
        mask = mk[m]
        for q in range(nq):
            piece = second[:, q * 128 : (q + 1) * 128]
            valid = piece * mask
            st2[m, d, q : q + 1, :] = jnp.sum(valid, axis=0, keepdims=True)
            st2[m, d, nq + q : nq + q + 1, :] = jnp.sum(valid * piece, axis=0, keepdims=True)
        stats_send(st2.at[m], s2_s.at[m], s2_r.at[m])

    low_half = row_iota((2, 8, 128)) * 0 + lax.broadcasted_iota(jnp.int32, (2, 8, 128), 1)
    tiles = AREA // 4
    half = tiles // 2

    def image_sums(value):
        value = value.reshape(imb // 2, tiles, 8, 128)
        middle = value[:, half]
        first = jnp.sum(value[:, :half], axis=1) + jnp.where(low_half < 4, middle, 0.0)
        last = jnp.sum(value[:, half + 1 :], axis=1) + jnp.where(low_half < 4, 0.0, middle)
        first = jnp.sum(first, axis=1)
        last = jnp.sum(last, axis=1)
        found = []
        for i in range(imb // 2):
            found += [first[i : i + 1], last[i : i + 1]]
        return jnp.concatenate(found, axis=0)

    def image_spread(value):
        pieces = []
        for i in range(imb // 2):
            first = jnp.broadcast_to(value[2 * i : 2 * i + 1], (8, 128))
            last = jnp.broadcast_to(value[2 * i + 1 : 2 * i + 2], (8, 128))
            middle = jnp.where(low_half[0] < 4, first, last)
            pieces.append(jnp.broadcast_to(first[None], (half, 8, 128)))
            pieces.append(middle[None])
            pieces.append(jnp.broadcast_to(last[None], (half, 8, 128)))
        return jnp.concatenate(pieces, axis=0).reshape(pm, 128)

    def stage_b(m):
        stats_wait(st2.at[m], s2_s.at[m], s2_r.at[m])
        total = stats_sum(st2.at[m])
        n = cntm[m]
        mask = mk[m]
        for q in range(nq):
            at_q = slice(q * 128, (q + 1) * 128)
            center = total[q : q + 1] / n
            spread = total[nq + q : nq + q + 1] / n - center * center
            scale = lax.rsqrt(spread + norm_eps)
            bn2[m, 0:1, at_q] = scale
            normed = (sec[m, :, at_q] - center) * scale
            sec[m, :, at_q] = normed
            summed = n2[0:1, at_q] * normed + n2[1:2, at_q]
            summed = summed + sv[rows(m), at_q].astype(F32)
            sigma = sigmoid(summed)
            slope = sigma * (1.0 + summed * (1.0 - sigma)) * mask
            slp[m, :, at_q] = slope
            pool[m, :, at_q] = (image_sums(summed * sigma * mask) / cnti[m]).astype(BF).astype(F32)
            tsum[m, 0, :, at_q] = image_sums(slope)
            tsum[m, 1, :, at_q] = image_sums(slope * normed)
        lgt[m, c] = mm(pool[m].astype(BF), cfull[...])
        for dev, i in ((sibdev, 0), (oppdev, 1), ((d, dia), 2)):
            remote(lgt.at[m, c], lgt.at[m, c], lg_s.at[i, m], lg_r.at[c, m], dev).start()

    def stage_c(m):
        for i, chunk in enumerate((sib, opp, dia)):
            got = lgt.at[m, chunk]
            remote(got, got, lg_s.at[i, m], lg_r.at[chunk, m], sibdev).wait_recv()
        logits = lgt[m, 0]
        for q in range(1, nc):
            logits = logits + lgt[m, q]
        logits = logits + cbias[...]
        top = jnp.max(logits, axis=1, keepdims=True)
        expo = jnp.exp(logits - top)
        expo_sum = jnp.sum(expo, axis=1, keepdims=True)
        image_row = row_iota((imb, classes))
        target = jnp.zeros((imb, classes), jnp.int32)
        for i in range(imb):
            target = jnp.where(image_row == i, labels[m * imb + i], target)
        onehot = (target == lane_iota((imb, classes))).astype(F32)
        picked = jnp.sum(logits * onehot, axis=1, keepdims=True)
        loss = jnp.sum(top + jnp.log(expo_sum) - picked, axis=0, keepdims=True)
        st4[m, d, 2:3, :] = jnp.broadcast_to(loss, (1, 128))
        dlogits = ((expo / expo_sum - onehot) / total_images).astype(BF)
        dlm[m] = dlogits.astype(F32)
        spread = nt_dot(dlogits, cfull[...])
        for q in range(nq):
            at_q = slice(q * 128, (q + 1) * 128)
            value = spread[:, at_q] / cnti[m]
            dpd[m, :, at_q] = value
            st3[m, d, q : q + 1, :] = jnp.sum(value * tsum[m, 0, :, at_q], axis=0, keepdims=True)
            st3[m, d, nq + q : nq + q + 1, :] = jnp.sum(
                value * tsum[m, 1, :, at_q], axis=0, keepdims=True
            )
        stats_send(st3.at[m], s3_s.at[m], s3_r.at[m])

    def stage_d(m):
        stats_wait(st3.at[m], s3_s.at[m], s3_r.at[m])
        total = stats_sum(st3.at[m])
        n = cntm[m]
        mask = mk[m]
        for q in range(nq):
            at_q = slice(q * 128, (q + 1) * 128)
            gain = n2[0:1, at_q] * bn2[m, 0:1, at_q]
            base = gain * total[q : q + 1] / n
            ramp = gain * total[nq + q : nq + q + 1] / n
            value = image_spread(gain * dpd[m, :, at_q]) * slp[m, :, at_q]
            value = value - mask * (base + ramp * sec[m, :, at_q])
            dsb[:, at_q] = value.astype(BF)
        for q in range(nq):
            at_q = slice(q * 128, (q + 1) * 128)
            bn2[m, 1:2, at_q] = total[nq + q : nq + q + 1]
            bn2[m, 2:3, at_q] = total[q : q + 1]
        back = nt_dot(dsb[...], pfull[...])
        for q in range(nc):
            piece = back[:, q * c1l : (q + 1) * c1l]
            da[m, q] = piece
            dab[m, q] = piece.astype(BF)
        for i, chunk in ((0, sib), (1, dia)):
            remote(dab.at[m, chunk], sr.at[m, i], sr_s.at[i, m], sr_r.at[i, m], sibdev).start()
        pacc[...] += mm(at[m], dsb[...])

    def stage_e(m):
        for i in (1, 0):
            remote(sr.at[m, i], sr.at[m, i], sr_s.at[i, m], sr_r.at[i, m], sibdev).wait_recv()
            if i == 1:
                es[m] = (da[m, opp] + sr[m, 1].astype(F32)).astype(BF)
                remote(es.at[m], er.at[m], er_s.at[m], er_r.at[m], oppdev).start()
        da[m, c] = da[m, c] + sr[m, 0].astype(F32)

    def stage_f(m):
        remote(es.at[m], er.at[m], er_s.at[m], er_r.at[m], oppdev).wait_recv()
        upstream = da[m, c] + er[m].astype(F32)
        normed = (hid[m] - bn1[m, 0:1, :]) * bn1[m, 1:2, :]
        shifted = n1[0:1, :] * normed + n1[1:2, :]
        sigma = sigmoid(shifted)
        upstream = upstream * mk[m] * (sigma * (1.0 + shifted * (1.0 - sigma)))
        du[m] = upstream
        st4[m, d, 0:1, :] = jnp.sum(upstream, axis=0, keepdims=True)
        st4[m, d, 1:2, :] = jnp.sum(upstream * normed, axis=0, keepdims=True)
        stats_send(st4.at[m], s4_s.at[m], s4_r.at[m])

    def stage_g(m):
        stats_wait(st4.at[m], s4_s.at[m], s4_r.at[m])
        total = stats_sum(st4.at[m])
        n = cntm[m]
        bn1[m, 2:3, :] = total[1:2]
        bn1[m, 3:4, :] = total[0:1]
        bn1[m, 4:5, :] = total[2:3]
        normed = (hid[m] - bn1[m, 0:1, :]) * bn1[m, 1:2, :]
        gain = n1[0:1, :] * bn1[m, 1:2, :]
        value = mk[m] * gain * (du[m] - (total[0:1] + normed * total[1:2]) / n)
        dhp[PAD : PAD + pm, :] = value.astype(BF).astype(F32)

        def shifted(t):
            ky, kx = t // 3, t % 3
            off = PAD - (ky - 1) * SIDE - (kx - 1)
            piece = dhp[off : off + pm, :]
            found = edges(2 - ky, 2 - kx)
            return (piece if found is None else piece * found).astype(BF)

        left = xt[m]
        for t in range(0, 9, 2):
            if t < 8:
                pair = mm(left, jnp.concatenate([shifted(t), shifted(t + 1)], axis=1))
                acc[t * c1 : (t + 1) * c1, :] += pair[:, :c1l]
                acc[(t + 1) * c1 : (t + 2) * c1, :] += pair[:, c1l:]
            else:
                acc[t * c1 : (t + 1) * c1, :] += mm(left, shifted(t))

    def scatter_start(total, height, sbuf, xbuf, ss, rr):
        for j in range(nz):
            u = flip(z, j) * 2 + 1 - x
            sbuf[j] = total[pl.ds(pl.multiple_of(u * height, height), height), :].astype(BF)
            remote(sbuf.at[j], xbuf.at[j], ss.at[j], rr.at[j], xdev).start()

    def scatter_middle(total, height, xbuf, zbuf, rbuf, xs, xr, zs, zr):
        for j in list(range(1, nz)) + [0]:
            remote(xbuf.at[j], xbuf.at[j], xs.at[j], xr.at[j], xdev).wait_recv()
            u = flip(z, j) * 2 + x
            found = total[pl.ds(pl.multiple_of(u * height, height), height), :]
            found = found + xbuf[j].astype(F32)
            if j == 0:
                return found
            zbuf[j] = found.astype(BF)
            remote(zbuf.at[j], rbuf.at[j], zs.at[j], zr.at[j], zdev(j)).start()

    def scatter_finish(found, rbuf, zs, zr):
        for j in range(1, nz):
            remote(rbuf.at[j], rbuf.at[j], zs.at[j], zr.at[j], zdev(j)).wait_recv()
            found = found + rbuf[j].astype(F32)
        return found

    def scatter_drain(sbuf, zbuf, xs, xr, zs, zr):
        for j in range(nz):
            remote(sbuf.at[j], sbuf.at[j], xs.at[j], xr.at[j], xdev).wait_send()
            if j > 0:
                remote(zbuf.at[j], zbuf.at[j], zs.at[j], zr.at[j], xdev).wait_send()

    stages = (stage_a, stage_b, stage_c, stage_d, stage_e, stage_f, stage_g)

    def step(s, carry):
        for i in reversed(range(len(stages))):
            @pl.when((s >= i) & (s < i + MICRO))
            def run(i=i):
                stages[i](s - i)

            if i == 3:
                @pl.when(s == MICRO + 2)
                def start_proj():
                    scatter_start(pacc, rp, gps, gpx, gpx_s, gpx_r)

            if i == 2:
                @pl.when(s == MICRO + 1)
                def share_cls():
                    mine = dla.at[pl.ds(pl.multiple_of(d * images, images), images)]
                    mine[...] = jnp.concatenate([dlm[q] for q in range(MICRO)], axis=0).astype(BF)
                    pooled = pla.at[pl.ds(pl.multiple_of(d * images, images), images)]
                    pooled[...] = jnp.concatenate([pool[q] for q in range(MICRO)], axis=0).astype(BF)
                    gather_start(dla, images, dl_s, dl_r)
                    gather_start(pla, images, pl_s, pl_r)

            if i == 0:
                @pl.when(s == 0)
                def move_cls():
                    for j in range(1, nz):
                        gather_forward(cfull, rc, kw_s, kw_r, j)
                    gather_finish(cfull, rc, kw_s, kw_r)

        return carry

    lax.fori_loop(0, MICRO + len(stages) - 1, step, 0)

    scatter_start(acc, r1, gcs, gcx, gcx_s, gcx_r)

    for j in range(1, nz):
        gather_forward(dla, images, dl_s, dl_r, j)
        gather_forward(pla, images, pl_s, pl_r, j)
    proj_part = scatter_middle(pacc, rp, gpx, gpz, gpr, gpx_s, gpx_r, gpz_s, gpz_r)
    gproj[...] = scatter_finish(proj_part, gpr, gpz_s, gpz_r)
    gather_finish(dla, images, dl_s, dl_r)
    gather_finish(pla, images, pl_s, pl_r)
    plt[...] = pla[...].T
    left = plt[pl.ds(pl.multiple_of(d * rc, rc), rc), :]
    gcls[...] = mm(left, dla[...])
    gbias[...] = jnp.sum(dla[...].astype(F32), axis=0, keepdims=True)
    gone[...] = bn1[0, 2:4, :] + bn1[1, 2:4, :] + bn1[2, 2:4, :] + bn1[3, 2:4, :]
    gtwo[...] = bn2[0, 1:3, :] + bn2[1, 1:3, :] + bn2[2, 1:3, :] + bn2[3, 1:3, :]
    loss = bn1[0, 4:5, :] + bn1[1, 4:5, :] + bn1[2, 4:5, :] + bn1[3, 4:5, :]
    gloss[...] = loss / total_images

    conv_part = scatter_middle(acc, r1, gcx, gcz, gcr, gcx_s, gcx_r, gcz_s, gcz_r)
    gconv[...] = scatter_finish(conv_part, gcr, gcz_s, gcz_r)

    gather_drain(wfull, r1, cw_s, cw_r)
    gather_drain(pfull, rp, pw_s, pw_r)
    gather_drain(cfull, rc, kw_s, kw_r)
    gather_drain(dla, images, dl_s, dl_r)
    gather_drain(pla, images, pl_s, pl_r)
    stats_drain(st0, s0_s, s0_r)
    stats_drain(st1, s1_s, s1_r)
    scatter_drain(gps, gpz, gpx_s, gpx_r, gpz_s, gpz_r)
    scatter_drain(gcs, gcz, gcx_s, gcx_r, gcz_s, gcz_r)

    def drain(m, carry):
        for i in range(3):
            src = part(xv, m, c)
            remote(src, src, fx_s.at[i, m], fx_r.at[c, m], sibdev).wait_send()
            src = part(af, m, c)
            remote(src, src, af_s.at[i, m], af_r.at[c, m], sibdev).wait_send()
            src = lgt.at[m, c]
            remote(src, src, lg_s.at[i, m], lg_r.at[c, m], sibdev).wait_send()
        for i in range(2):
            remote(sr.at[m, i], sr.at[m, i], sr_s.at[i, m], sr_r.at[i, m], sibdev).wait_send()
        remote(es.at[m], er.at[m], er_s.at[m], er_r.at[m], oppdev).wait_send()
        stats_drain(st2.at[m], s2_s.at[m], s2_r.at[m])
        stats_drain(st3.at[m], s3_s.at[m], s3_r.at[m])
        stats_drain(st4.at[m], s4_s.at[m], s4_r.at[m])
        return carry

    lax.fori_loop(0, MICRO, drain, 0)


def fused_gradients(
    features, shortcut, valid_masks, labels, w_conv, w_proj, w_cls, cls_bias, norm_one, norm_two
):
    nd, nc = lax.axis_size("dp"), lax.axis_size("chan")
    nz = nd // 2
    pixels, c1l = features.shape
    c2l = shortcut.shape[1]
    images = valid_masks.shape[0]
    imb, pm = images // MICRO, pixels // MICRO
    r1, rp, rc = w_conv.shape[0], w_proj.shape[0], w_cls.shape[0]
    classes = w_cls.shape[1]
    c1 = c1l * nc
    nq = c2l // 128
    dims = (nd, nc, pm, imb, c1l, c2l, r1, rp, rc, classes, images * nd)
    vmem = pltpu.VMEM
    dma = pltpu.SemaphoreType.DMA
    m4 = MICRO
    scratch = [
        vmem((r1, c1l), F32), vmem((rp, c2l), F32), vmem((rc, classes), F32),
        vmem((9 * c1, c1l), BF), vmem((c1, c2l), BF), vmem((c2l, classes), BF),
        vmem((pixels, c1), BF), vmem((pixels, c2l), BF),
        vmem((m4, pm, c1), BF), vmem((m4, c1, pm), BF),
        vmem((9, PAD + pm + PAD, c1l), F32), vmem((m4, pm, c1l), F32), vmem((m4, pm, 128), F32),
        vmem((4, pm, 128), F32), vmem((m4, 1, 128), F32), vmem((m4, imb, 128), F32),
        vmem((pixels, c1), BF), vmem((m4, c1, pm), BF),
        vmem((m4, pm, c2l), F32), vmem((m4, pm, c2l), F32),
        vmem((m4, 8, c1l), F32), vmem((m4, 8, c2l), F32),
        vmem((m4, 2, imb, c2l), F32), vmem((m4, imb, c2l), F32),
        vmem((m4, nc, imb, classes), F32), vmem((m4, imb, classes), F32), vmem((m4, imb, c2l), F32),
        vmem((pm, c2l), BF), vmem((m4, nc, pm, c1l), F32), vmem((m4, nc, pm, c1l), BF),
        vmem((m4, 2, pm, c1l), BF), vmem((m4, pm, c1l), BF), vmem((m4, pm, c1l), BF),
        vmem((m4, pm, c1l), F32), vmem((PAD + pm + PAD, c1l), F32),
        vmem((9 * c1, c1l), F32), vmem((c1, c2l), F32),
        vmem((nd, 8, c1l), F32), vmem((nd, 8, c1l), F32),
        vmem((m4, nd, 2 * nq, 128), F32), vmem((m4, nd, 2 * nq, 128), F32),
        vmem((m4, nd, 8, c1l), F32),
        vmem((nz, r1, c1l), BF), vmem((nz, r1, c1l), BF),
        vmem((nz, r1, c1l), BF), vmem((nz, r1, c1l), BF),
        vmem((nz, rp, c2l), BF), vmem((nz, rp, c2l), BF),
        vmem((nz, rp, c2l), BF), vmem((nz, rp, c2l), BF),
        vmem((nd * images, classes), BF), vmem((nd * images, c2l), BF), vmem((c2l, nd * images), BF),
        dma((5,)),
        dma((2 * nz,)), dma((nd,)), dma((2 * nz,)), dma((nd,)), dma((2 * nz,)), dma((nd,)),
        dma((3, m4)), dma((nc, m4)), dma((3, m4)), dma((nc, m4)),
        dma((nd,)), dma((nd,)), dma((nd,)), dma((nd,)),
        dma((m4, nd)), dma((m4, nd)), dma((m4, nd)), dma((m4, nd)), dma((m4, nd)), dma((m4, nd)),
        dma((3, m4)), dma((nc, m4)), dma((2, m4)), dma((2, m4)), dma((m4,)), dma((m4,)),
        dma((2 * nz,)), dma((nd,)), dma((2 * nz,)), dma((nd,)),
        dma((nz,)), dma((nz,)), dma((nz,)), dma((nz,)),
        dma((nz,)), dma((nz,)), dma((nz,)), dma((nz,)),
    ]
    whole = pl.BlockSpec(memory_space=pltpu.VMEM)
    hbm = pl.BlockSpec(memory_space=pl.ANY)
    scalar = pl.BlockSpec(memory_space=pltpu.SMEM)
    shape = jax.ShapeDtypeStruct
    return pl.pallas_call(
        functools.partial(fused_kernel, dims),
        out_shape=(
            shape((r1, c1l), F32), shape((rp, c2l), F32), shape((rc, classes), F32),
            shape((1, classes), F32), shape((2, c1l), F32), shape((2, c2l), F32),
            shape((1, 128), F32),
        ),
        in_specs=[hbm, hbm, whole, scalar, hbm, hbm, hbm, whole, whole, whole],
        out_specs=(whole,) * 7,
        scratch_shapes=scratch,
        compiler_params=pltpu.CompilerParams(
            collective_id=0, has_side_effects=True, vmem_limit_bytes=58 * 1024 * 1024
        ),
    )(
        features, shortcut, valid_masks, labels, w_conv, w_proj, w_cls,
        cls_bias.reshape(1, classes), norm_one, norm_two,
    )


def adam_kernel(*refs):
    for i, (rate, decay) in enumerate(ADAM_RATES):
        weight, moment, second, grad = (ref[...] for ref in refs[4 * i : 4 * i + 4])
        outs = refs[4 * len(ADAM_RATES) + 1 + 3 * i :]
        new_weight, new_moment, new_second = adam_step(weight, moment, second, grad, rate, decay)
        outs[0][...] = new_weight
        outs[1][...] = new_moment
        outs[2][...] = new_second
        if i < 3:
            refs[7 * len(ADAM_RATES) + 1 + i][...] = new_weight.astype(BF)
    refs[-1][...] = refs[4 * len(ADAM_RATES)][...]


ADAM_RATES = (
    (rate_matrix, weight_decay),
    (rate_matrix, weight_decay),
    (rate_matrix, weight_decay),
    (rate_small, 0.0),
    (rate_small, 0.0),
    (rate_small, 0.0),
)


def fused_device(
    features, shortcut, valid_masks, labels, w_conv, w_proj, w_cls, cls_bias, norm_one, norm_two,
    conv_moment, conv_second, proj_moment, proj_second, cls_moment, cls_second,
    bias_moment, bias_second, one_moment, one_second, two_moment, two_second,
):
    grads = fused_gradients(
        features, shortcut, valid_masks, labels, w_conv, w_proj, w_cls, cls_bias, norm_one, norm_two
    )
    states = (
        (w_conv, conv_moment, conv_second),
        (w_proj, proj_moment, proj_second),
        (w_cls, cls_moment, cls_second),
        (cls_bias.reshape(1, -1), bias_moment.reshape(1, -1), bias_second.reshape(1, -1)),
        (norm_one, one_moment, one_second),
        (norm_two, two_moment, two_second),
    )
    operands, outs = [], []
    for state, grad in zip(states, grads[:6]):
        operands += list(state) + [grad]
        outs += [jax.ShapeDtypeStruct(grad.shape, F32)] * 3
    outs += [jax.ShapeDtypeStruct(grads[i].shape, BF) for i in range(3)]
    outs.append(jax.ShapeDtypeStruct(grads[6].shape, F32))
    whole = pl.BlockSpec(memory_space=pltpu.VMEM)
    done = list(
        pl.pallas_call(
            adam_kernel,
            out_shape=tuple(outs),
            in_specs=[whole] * (len(operands) + 1),
            out_specs=(whole,) * len(outs),
            compiler_params=pltpu.CompilerParams(vmem_limit_bytes=40 * 1024 * 1024),
        )(*operands, grads[6])
    )
    for i in (9, 10, 11):
        done[i] = done[i].reshape(-1)
    return tuple(done[:21]) + (done[21][0, 0],)


def run_device(*args):
    features, shortcut, valid_masks = args[:3]
    w_cls = args[6]
    fits = (
        lax.axis_size("chan") == 4
        and lax.axis_size("dp") % 2 == 0
        and features.shape[1] == 128
        and shortcut.shape[1] % 128 == 0
        and w_cls.shape[0] % 16 == 0
        and valid_masks.shape[0] % (4 * MICRO) == 0
    )
    return (fused_device if fits else per_device)(*args)


def solution(mesh):
    placed = (
        P("dp", "chan"),
        P("dp", "chan"),
        P("dp", None),
        P("dp"),
        P("dp", "chan"),
        P("dp", "chan"),
        P(("chan", "dp"), None),
        P(),
        P(None, "chan"),
        P(None, "chan"),
        P("dp", "chan"),
        P("dp", "chan"),
        P("dp", "chan"),
        P("dp", "chan"),
        P(("chan", "dp"), None),
        P(("chan", "dp"), None),
        P(),
        P(),
        P(None, "chan"),
        P(None, "chan"),
        P(None, "chan"),
        P(None, "chan"),
    )
    return jax.shard_map(
        run_device,
        mesh=mesh,
        in_specs=placed,
        out_specs=(
            P("dp", "chan"),
            P("dp", "chan"),
            P("dp", "chan"),
            P("dp", "chan"),
            P("dp", "chan"),
            P("dp", "chan"),
            P(("chan", "dp"), None),
            P(("chan", "dp"), None),
            P(("chan", "dp"), None),
            P(),
            P(),
            P(),
            P(None, "chan"),
            P(None, "chan"),
            P(None, "chan"),
            P(None, "chan"),
            P(None, "chan"),
            P(None, "chan"),
            P("dp", "chan"),
            P("dp", "chan"),
            P(("chan", "dp"), None),
            P(),
        ),
        check_vma=False,
    )
```

```python
import functools

import jax
import jax.numpy as jnp
from jax import lax
from jax.experimental import pallas as pl
from jax.experimental.pallas import tpu as pltpu
from jax.sharding import PartitionSpec as P

SIDE = 10
MICRO = 4
STEP = 3


norm_eps = 1e-05
adam_eps = 1e-08
beta_decay = 0.5
rate_matrix = 0.02
rate_small = 0.5
weight_decay = 0.01


def tap_columns(flat, images):
    width = flat.shape[1]
    grid = flat.reshape(images, SIDE, SIDE, width)
    padded = jnp.pad(grid, ((0, 0), (1, 1), (1, 1), (0, 0)))
    pieces = [
        padded[:, down : down + SIDE, across : across + SIDE, :]
        for down in range(3)
        for across in range(3)
    ]
    return jnp.concatenate(pieces, axis=3).reshape(images * SIDE * SIDE, 9 * width)


def silu_slope(value):
    sigma = jax.nn.sigmoid(value)
    return sigma * (1.0 + value * (1.0 - sigma))


def norm_forward(hidden, weights, params):
    sums, squares, count = lax.psum(
        (
            jnp.sum(hidden * weights, axis=1),
            jnp.sum(hidden * hidden * weights, axis=1),
            jnp.sum(weights, axis=1),
        ),
        "dp",
    )
    center = sums / count
    scale = lax.rsqrt(squares / count - center * center + norm_eps)
    normed = (hidden - center[:, None]) * scale[:, None]
    return (params[0] * normed + params[1], normed, scale[:, None], count[:, None])


def norm_backward(upstream, normed, scale, count, weights, params):
    total, along = lax.psum((jnp.sum(upstream, axis=1), jnp.sum(upstream * normed, axis=1)), "dp")
    grad = (
        weights
        * params[0]
        * scale
        * (upstream - (total[:, None] + normed * along[:, None]) / count)
    )
    return (grad, jnp.stack([jnp.sum(along, axis=0), jnp.sum(total, axis=0)]))


def contract_rows(left, right):
    return lax.dot_general(
        left, right, (((0,), (0,)), ((), ())), preferred_element_type=jnp.float32
    )


def contract_cols(left, right):
    return lax.dot_general(
        left, right, (((1,), (1,)), ((), ())), preferred_element_type=jnp.float32
    )


def adam_step(weight, moment, second, grad, rate, decay):
    moment = beta_decay * moment + (1.0 - beta_decay) * grad
    second = beta_decay * second + (1.0 - beta_decay) * grad * grad
    correct = 1.0 - beta_decay**STEP
    weight = weight - rate * (
        moment / correct / (jnp.sqrt(second / correct) + adam_eps) + decay * weight
    )
    return (weight, moment, second)


def per_device(
    features,
    shortcut,
    valid_masks,
    labels,
    w_conv,
    w_proj,
    w_cls,
    cls_bias,
    norm_one,
    norm_two,
    conv_moment,
    conv_second,
    proj_moment,
    proj_second,
    cls_moment,
    cls_second,
    bias_moment,
    bias_second,
    one_moment,
    one_second,
    two_moment,
    two_second,
):
    images = valid_masks.shape[0]
    area = SIDE * SIDE
    pixels = images * area
    total_images = images * lax.axis_size("dp")
    classes = w_cls.shape[1]
    conv_full, proj_full, cls_full = (
        lax.all_gather(w_conv.astype(jnp.bfloat16), "dp", axis=0, tiled=True),
        lax.all_gather(w_proj.astype(jnp.bfloat16), "dp", axis=0, tiled=True),
        lax.all_gather(w_cls.astype(jnp.bfloat16), "dp", axis=0, tiled=True),
    )

    def split(flat):
        return flat.reshape((MICRO, -1) + flat.shape[1:])

    def join(parts):
        return parts.reshape((-1,) + parts.shape[2:])

    image_mask = valid_masks.astype(jnp.float32)
    pixel_counts = jnp.sum(image_mask, axis=1)
    weights = split(image_mask.reshape(pixels, 1))
    masked = features * join(weights).astype(jnp.bfloat16)
    gathered = lax.all_gather(masked, "chan", axis=1, tiled=True)
    columns = tap_columns(gathered, images)
    hidden = jnp.dot(columns, conv_full, preferred_element_type=jnp.float32)
    shifted, normed_one, scale_one, count = norm_forward(split(hidden), weights, norm_one)
    active = join((jax.nn.silu(shifted) * weights).astype(jnp.bfloat16))
    active_full = lax.all_gather(active, "chan", axis=1, tiled=True)
    second = jnp.dot(active_full, proj_full, preferred_element_type=jnp.float32)
    shifted_two, normed_two, scale_two, _ = norm_forward(split(second), weights, norm_two)
    summed = shifted_two + split(shortcut.astype(jnp.float32))
    output = jax.nn.silu(summed) * weights
    channels = shortcut.shape[1]
    pooled = (
        jnp.sum(output.reshape(images, area, channels), axis=1) / pixel_counts[:, None]
    ).astype(jnp.bfloat16)
    partial_value = jnp.dot(pooled, cls_full, preferred_element_type=jnp.float32)
    logits = lax.psum(partial_value, "chan") + cls_bias
    top = jnp.max(logits, axis=1, keepdims=True)
    expo = jnp.exp(logits - top)
    expo_sum = jnp.sum(expo, axis=1, keepdims=True)
    onehot = (labels[:, None] == jnp.arange(classes)[None, :]).astype(jnp.float32)
    picked = jnp.sum(logits * onehot, axis=1)
    loss_sum = jnp.sum(top[:, 0] + jnp.log(expo_sum[:, 0]) - picked)
    dlogits = ((expo / expo_sum - onehot) / total_images).astype(jnp.bfloat16)
    grad_bias = jnp.sum(dlogits.astype(jnp.float32), axis=0)
    local_cls = contract_rows(pooled, dlogits)
    grad_pool = contract_cols(dlogits, cls_full)
    spread_back = jnp.broadcast_to(
        (grad_pool / pixel_counts[:, None])[:, None, :], (images, area, channels)
    ).reshape(MICRO, -1, channels)
    upstream_two = spread_back * weights * silu_slope(summed)
    grad_second, grad_two = norm_backward(
        upstream_two, normed_two, scale_two, count, weights, norm_two
    )
    grad_second = join(grad_second.astype(jnp.bfloat16))
    local_proj = contract_rows(active_full, grad_second)
    partial_act = contract_cols(grad_second, proj_full)
    grad_active = lax.psum_scatter(
        partial_act.astype(jnp.bfloat16), "chan", scatter_dimension=1, tiled=True
    ).astype(jnp.float32)
    upstream_one = split(grad_active) * weights * silu_slope(shifted)
    grad_hidden, grad_one = norm_backward(
        upstream_one, normed_one, scale_one, count, weights, norm_one
    )
    local_conv = contract_rows(columns, join(grad_hidden.astype(jnp.bfloat16)))
    sum_conv, sum_proj, sum_cls = (
        lax.psum_scatter(
            local_conv.astype(jnp.bfloat16), "dp", scatter_dimension=0, tiled=True
        ).astype(jnp.float32),
        lax.psum_scatter(
            local_proj.astype(jnp.bfloat16), "dp", scatter_dimension=0, tiled=True
        ).astype(jnp.float32),
        lax.psum_scatter(
            local_cls.astype(jnp.bfloat16), "dp", scatter_dimension=0, tiled=True
        ).astype(jnp.float32),
    )
    loss_total, bias_total = lax.psum((loss_sum, grad_bias), "dp")
    train_loss = loss_total / total_images
    conv_w, conv_m, conv_v = adam_step(
        w_conv, conv_moment, conv_second, sum_conv, rate_matrix, weight_decay
    )
    proj_w, proj_m, proj_v = adam_step(
        w_proj, proj_moment, proj_second, sum_proj, rate_matrix, weight_decay
    )
    cls_w, cls_m, cls_v = adam_step(
        w_cls, cls_moment, cls_second, sum_cls, rate_matrix, weight_decay
    )
    bias_w, bias_m, bias_v = adam_step(
        cls_bias, bias_moment, bias_second, bias_total, rate_small, 0.0
    )
    one_w, one_m, one_v = adam_step(norm_one, one_moment, one_second, grad_one, rate_small, 0.0)
    two_w, two_m, two_v = adam_step(norm_two, two_moment, two_second, grad_two, rate_small, 0.0)
    return (
        conv_w,
        conv_m,
        conv_v,
        proj_w,
        proj_m,
        proj_v,
        cls_w,
        cls_m,
        cls_v,
        bias_w,
        bias_m,
        bias_v,
        one_w,
        one_m,
        one_v,
        two_w,
        two_m,
        two_v,
        conv_w.astype(jnp.bfloat16),
        proj_w.astype(jnp.bfloat16),
        cls_w.astype(jnp.bfloat16),
        train_loss,
    )


MESH = pl.DeviceIdType.MESH
AREA = SIDE * SIDE
PAD = 16
BF = jnp.bfloat16
F32 = jnp.float32


def flip(value, bits):
    bit = 1
    while bit <= bits:
        if bits & bit:
            value = value + bit - 2 * bit * (lax.div(value, bit) % 2)
        bit *= 2
    return value


def nt_dot(left, right):
    return lax.dot_general(left, right, (((1,), (1,)), ((), ())), preferred_element_type=F32)


def mm(left, right):
    return jnp.dot(left, right, preferred_element_type=F32)


def sigmoid(value):
    return 1.0 / (1.0 + jnp.exp(-value))


def row_iota(shape):
    return lax.broadcasted_iota(jnp.int32, shape, 0)


def lane_iota(shape):
    return lax.broadcasted_iota(jnp.int32, shape, 1)


def fused_kernel(dims, *refs):
    nd, nc, pm, imb, c1l, c2l, r1, rp, rc, classes, total_images = dims
    (
        feat, short, masks, labels, wconv, wproj, wcls, cbias, n1, n2, gout,
        wf, pf, cf, wfull, pfull, cfull, xv, sv, xm, xt, yb, hid, mk, edge, cntm, cnti,
        af, at, sec, slp, bn1, bn2, tsum, pool, lgt, dlm, dpd, dsb, da, dab, sr, es, er,
        du, dhp, acc, pacc, st1, st2, st3, st4,
        gcs, gcx, gcz, gcr, gps, gpx, gpz, gpr, dla, plt,
        ld_s, cw_s, cw_r, pw_s, pw_r, kw_s, kw_r, dl_s, dl_r, fx_s, fx_r, af_s, af_r, st_s, st_r,
        lg_s, lg_r, sr_s, sr_r, er_s, er_r, gc_s, gc_r, gp_s, gp_r,
    ) = refs
    nz = nd // 2
    c1 = c1l * nc
    nq = c2l // 128
    d = lax.axis_index("dp")
    c = lax.axis_index("chan")
    z, x = lax.div(d, 2), d % 2
    y, k = lax.div(c, 2), c % 2
    sib = y * 2 + 1 - k
    opp = (1 - y) * 2 + k
    dia = (1 - y) * 2 + 1 - k
    xdev = (z * 2 + 1 - x, c)
    sibdev = (d, sib)
    oppdev = (d, opp)

    def zdev(j):
        return (flip(z, j) * 2 + x, c)

    def remote(src, dst, ssem, rsem, dev):
        return pltpu.make_async_remote_copy(
            src_ref=src, dst_ref=dst, send_sem=ssem, recv_sem=rsem,
            device_id=dev, device_id_type=MESH,
        )

    def unit(buf, u, rows):
        return buf.at[pl.ds(pl.multiple_of(u * rows, rows), rows)]

    def span(buf, units, rows):
        return buf.at[pl.ds(0, units * rows)]

    def gather_near(buf, rows, ss, rr, js):
        mine = unit(buf, d, rows)
        for j in js:
            if j == 0:
                remote(mine, mine, ss.at[0], rr.at[d], xdev).start()
            elif j < nz:
                remote(mine, mine, ss.at[1], rr.at[d], zdev(j)).start()

    def gather_start(buf, rows, ss, rr):
        gather_near(buf, rows, ss, rr, range(nz))

    def gather_forward(buf, rows, ss, rr, j):
        if j < nz:
            u = flip(z, j) * 2 + x
            got = unit(buf, u, rows)
            copy = remote(got, got, ss.at[0], rr.at[u], xdev)
            copy.wait_recv()
            copy.start()

    def gather_finish(buf, rows, ss, rr):
        for j in range(nz):
            u = flip(z, j) * 2 + 1 - x
            got = unit(buf, u, rows)
            remote(got, got, ss.at[0], rr.at[u], xdev).wait_recv()

    def gather_drain(buf, rows, ss, rr):
        for i, units in ((0, nz), (1, nz - 1)):
            if units:
                sent = span(buf, units, rows)
                remote(sent, sent, ss.at[i], rr.at[d], xdev).wait_send()

    def stats_send(buf, ss, rr):
        for p in range(1, nd):
            remote(buf.at[0], buf.at[p], ss, rr, (flip(d, p), c)).start()

    def stats_wait(buf, ss, rr):
        got = buf.at[pl.ds(1, nd - 1)]
        remote(got, got, ss, rr, xdev).wait_recv()

    def stats_sum(buf):
        total = buf[d]
        for u in range(1, nd):
            total = total + buf[flip(d, u)]
        return total

    def stats_drain(buf, ss, rr):
        got = buf.at[pl.ds(1, nd - 1)]
        remote(got, got, ss, rr, xdev).wait_send()

    def rows(m):
        return pl.ds(pl.multiple_of(m * pm, pm), pm)

    def lanes(chunk):
        return pl.ds(pl.multiple_of(chunk * c1l, c1l), c1l)

    def part(buf, m, chunk):
        return buf.at[rows(m), lanes(chunk)]

    def local(src, dst, i):
        return pltpu.make_async_copy(src, dst, ld_s.at[i])

    loads = [
        local(wconv, wf, 0),
        local(wproj, pf, 1),
        local(wcls, cf, 2),
        local(feat, xv.at[:, lanes(c)], 3),
        local(short, sv, 4),
    ]
    for load in loads:
        load.start()

    barrier = pltpu.get_barrier_semaphore()
    powers = [j for j in (1, 2) if j < nz]
    others = [sibdev, oppdev, xdev] + [zdev(j) for j in powers]
    for dev in others:
        pl.semaphore_signal(barrier, inc=1, device_id=dev, device_id_type=MESH)
    loads[0].wait()
    wfull[pl.ds(pl.multiple_of(d * r1, r1), r1), :] = wf[...].astype(BF)
    pl.semaphore_wait(barrier, len(others))

    gather_near(wfull, r1, cw_s, cw_r, [0] + powers)
    for m in range(MICRO):
        src = feat.at[pl.ds(m * pm, pm)]
        remote(src, part(xv, m, c), fx_s, fx_r.at[c, m], oppdev).start()
        remote(src, part(xv, m, c), fx_s, fx_r.at[c, m], sibdev).start()

    loads[1].wait()
    pfull[pl.ds(pl.multiple_of(d * rp, rp), rp), :] = pf[...].astype(BF)
    loads[2].wait()
    cfull[pl.ds(pl.multiple_of(d * rc, rc), rc), :] = cf[...].astype(BF)

    pixel = row_iota((pm, 128))
    image = jnp.zeros((pm, 128), jnp.int32)
    for i in range(1, imb):
        image = image + (pixel >= AREA * i).astype(jnp.int32)
    pixel = pixel - AREA * image
    line = jnp.zeros((pm, 128), jnp.int32)
    for i in range(1, SIDE):
        line = line + (pixel >= SIDE * i).astype(jnp.int32)
    across = pixel - SIDE * line
    edge[0] = (line > 0).astype(F32)
    edge[1] = (line < SIDE - 1).astype(F32)
    edge[2] = (across > 0).astype(F32)
    edge[3] = (across < SIDE - 1).astype(F32)
    mask_bf = masks[...].astype(F32).astype(BF)
    images = imb * MICRO
    chosen = (pixel[:, :AREA] == lane_iota((pm, AREA))).astype(F32)
    ones = jnp.ones((AREA, 128), BF)
    image_count = jnp.sum(masks[...].astype(F32), axis=1, keepdims=True)
    for m in range(MICRO):
        away = row_iota((pm, images)) - AREA * (lane_iota((pm, images)) - imb * m)
        owner = jnp.where((away >= 0) & (away < AREA), 1.0, 0.0).astype(BF)
        spread = mm((mm(owner, mask_bf) * chosen).astype(BF), ones)
        mk[m] = spread
        cntm[m] = jnp.sum(spread, axis=0, keepdims=True)
        cnti[m] = jnp.broadcast_to(image_count[m * imb : (m + 1) * imb], (imb, 128))
        st1[m, 0, 2:3, :] = cntm[m]

    yb[:, 0:PAD, :] = jnp.zeros((9, PAD, c1l), F32)
    yb[:, PAD + pm :, :] = jnp.zeros((9, PAD, c1l), F32)
    dhp[0:PAD, :] = jnp.zeros((PAD, c1l), F32)
    dhp[PAD + pm :, :] = jnp.zeros((PAD, c1l), F32)

    for m in range(MICRO):
        got = part(xv, m, opp)
        copy = remote(got, got, fx_s, fx_r.at[opp, m], sibdev)
        copy.wait_recv()
        copy.start()
        if m >= 1:
            gather_forward(wfull, r1, cw_s, cw_r, m)
        if m == 1:
            gather_near(wfull, r1, cw_s, cw_r, [3])
    loads[3].wait()

    def take_features(m, carry):
        for chunk in (sib, dia):
            got = part(xv, m, chunk)
            remote(got, got, fx_s, fx_r.at[chunk, m], sibdev).wait_recv()
        flat_mask = mk[m].astype(BF)
        for q in range(nc):
            piece = xv[rows(m), q * c1l : (q + 1) * c1l] * flat_mask
            xm[m, :, q * c1l : (q + 1) * c1l] = piece
            xt[m, q * c1l : (q + 1) * c1l, :] = piece.T
        return carry

    lax.fori_loop(0, MICRO, take_features, 0)
    gather_finish(wfull, r1, cw_s, cw_r)
    gather_start(pfull, rp, pw_s, pw_r)

    def tap(t):
        return wfull[t * c1 : (t + 1) * c1, :]

    def edges(ky, kx):
        found = None
        if ky == 0:
            found = edge[0]
        if ky == 2:
            found = edge[1]
        if kx == 0:
            found = edge[2] if found is None else found * edge[2]
        if kx == 2:
            found = edge[3] if found is None else found * edge[3]
        return found

    def conv(m, carry):
        inputs = xm[m]
        for t in range(0, 9, 2):
            if t < 8:
                pair = mm(inputs, jnp.concatenate([tap(t), tap(t + 1)], axis=1))
                yb[t, PAD : PAD + pm, :] = pair[:, :c1l]
                yb[t + 1, PAD : PAD + pm, :] = pair[:, c1l:]
            else:
                yb[t, PAD : PAD + pm, :] = mm(inputs, tap(t))
        hidden = None
        for kx in range(3):
            column = None
            for ky in range(3):
                off = PAD + (ky - 1) * SIDE + kx - 1
                value = yb[3 * ky + kx, off : off + pm, :]
                if ky != 1:
                    value = value * edge[0 if ky == 0 else 1]
                column = value if column is None else column + value
            if kx != 1:
                column = column * edge[2 if kx == 0 else 3]
            hidden = column if hidden is None else hidden + column
        hid[m] = hidden
        valid = hidden * mk[m]
        st1[m, 0, 0:1, :] = jnp.sum(valid, axis=0, keepdims=True)
        st1[m, 0, 1:2, :] = jnp.sum(valid * hidden, axis=0, keepdims=True)
        stats_send(st1.at[m], st_s.at[0, m], st_r.at[0, m])
        return carry

    lax.fori_loop(0, MICRO, conv, 0)
    gather_start(cfull, rc, kw_s, kw_r)
    for j in range(1, nz):
        gather_forward(pfull, rp, pw_s, pw_r, j)
    acc[...] = jnp.zeros_like(acc)
    pacc[...] = jnp.zeros_like(pacc)

    def activate(m, carry):
        stats_wait(st1.at[m], st_s.at[0, m], st_r.at[0, m])
        totals = stats_sum(st1.at[m])
        n = totals[2:3]
        cntm[m] = n
        center = totals[0:1] / n
        bn1[m, 0:1, :] = center
        bn1[m, 1:2, :] = lax.rsqrt(totals[1:2] / n - center * center + norm_eps)
        normed = (hid[m] - bn1[m, 0:1, :]) * bn1[m, 1:2, :]
        shifted = n1[0:1, :] * normed + n1[1:2, :]
        active = (shifted * sigmoid(shifted) * mk[m]).astype(BF)
        mine = part(af, m, c)
        mine[...] = active
        remote(mine, mine, af_s, af_r.at[c, m], oppdev).start()
        remote(mine, mine, af_s, af_r.at[c, m], sibdev).start()
        return carry

    lax.fori_loop(0, MICRO, activate, 0)
    gather_forward(cfull, rc, kw_s, kw_r, 1)
    gather_finish(pfull, rp, pw_s, pw_r)
    loads[4].wait()

    def turn(m, chunk):
        at[m, lanes_sub(chunk), :] = part(af, m, chunk)[...].T

    def lanes_sub(chunk):
        return pl.ds(pl.multiple_of(chunk * c1l, c1l), c1l)

    def stage_a(m):
        got = part(af, m, opp)
        copy = remote(got, got, af_s, af_r.at[opp, m], sibdev)
        copy.wait_recv()
        copy.start()
        turn(m, c)
        turn(m, opp)
        got = part(af, m, sib)
        remote(got, got, af_s, af_r.at[sib, m], sibdev).wait_recv()
        turn(m, sib)
        got = part(af, m, dia)
        remote(got, got, af_s, af_r.at[dia, m], sibdev).wait_recv()
        turn(m, dia)
        second = mm(af[rows(m), :], pfull[...])
        sec[m] = second
        mask = mk[m]
        for q in range(nq):
            piece = second[:, q * 128 : (q + 1) * 128]
            valid = piece * mask
            st2[m, 0, q : q + 1, :] = jnp.sum(valid, axis=0, keepdims=True)
            st2[m, 0, nq + q : nq + q + 1, :] = jnp.sum(valid * piece, axis=0, keepdims=True)
        stats_send(st2.at[m], st_s.at[1, m], st_r.at[1, m])

    low_half = row_iota((2, 8, 128)) * 0 + lax.broadcasted_iota(jnp.int32, (2, 8, 128), 1)
    tiles = AREA // 4
    half = tiles // 2

    def image_sums(value):
        value = value.reshape(imb // 2, tiles, 8, 128)
        middle = value[:, half]
        first = jnp.sum(value[:, :half], axis=1) + jnp.where(low_half < 4, middle, 0.0)
        last = jnp.sum(value[:, half + 1 :], axis=1) + jnp.where(low_half < 4, 0.0, middle)
        first = jnp.sum(first, axis=1)
        last = jnp.sum(last, axis=1)
        found = []
        for i in range(imb // 2):
            found += [first[i : i + 1], last[i : i + 1]]
        return jnp.concatenate(found, axis=0)

    def image_spread(value):
        pieces = []
        for i in range(imb // 2):
            first = jnp.broadcast_to(value[2 * i : 2 * i + 1], (8, 128))
            last = jnp.broadcast_to(value[2 * i + 1 : 2 * i + 2], (8, 128))
            middle = jnp.where(low_half[0] < 4, first, last)
            pieces.append(jnp.broadcast_to(first[None], (half, 8, 128)))
            pieces.append(middle[None])
            pieces.append(jnp.broadcast_to(last[None], (half, 8, 128)))
        return jnp.concatenate(pieces, axis=0).reshape(pm, 128)

    def stage_b(m):
        stats_wait(st2.at[m], st_s.at[1, m], st_r.at[1, m])
        total = stats_sum(st2.at[m])
        n = cntm[m]
        mask = mk[m]
        for q in range(nq):
            at_q = slice(q * 128, (q + 1) * 128)
            center = total[q : q + 1] / n
            spread = total[nq + q : nq + q + 1] / n - center * center
            scale = lax.rsqrt(spread + norm_eps)
            bn2[m, 0:1, at_q] = scale
            normed = (sec[m, :, at_q] - center) * scale
            sec[m, :, at_q] = normed
            summed = n2[0:1, at_q] * normed + n2[1:2, at_q]
            summed = summed + sv[rows(m), at_q].astype(F32)
            sigma = sigmoid(summed)
            slope = sigma * (1.0 + summed * (1.0 - sigma)) * mask
            slp[m, :, at_q] = slope
            pool[m, :, at_q] = (image_sums(summed * sigma * mask) / cnti[m]).astype(BF).astype(F32)
            tsum[m, 0, :, at_q] = image_sums(slope)
            tsum[m, 1, :, at_q] = image_sums(slope * normed)
        lgt[m, c] = mm(pool[m].astype(BF), cfull[...])
        for dev in (oppdev, (d, dia), sibdev):
            remote(lgt.at[m, c], lgt.at[m, c], lg_s, lg_r.at[m], dev).start()

    def stage_c(m):
        got = lgt.at[m, pl.ds(0, nc - 1)]
        remote(got, got, lg_s, lg_r.at[m], sibdev).wait_recv()
        logits = lgt[m, 0]
        for q in range(1, nc):
            logits = logits + lgt[m, q]
        logits = logits + cbias[...]
        top = jnp.max(logits, axis=1, keepdims=True)
        expo = jnp.exp(logits - top)
        expo_sum = jnp.sum(expo, axis=1, keepdims=True)
        image_row = row_iota((imb, classes))
        target = jnp.zeros((imb, classes), jnp.int32)
        for i in range(imb):
            target = jnp.where(image_row == i, labels[m * imb + i], target)
        onehot = (target == lane_iota((imb, classes))).astype(F32)
        picked = jnp.sum(logits * onehot, axis=1, keepdims=True)
        loss = jnp.sum(top + jnp.log(expo_sum) - picked, axis=0, keepdims=True)
        st4[m, 0, 2:3, :] = jnp.broadcast_to(loss, (1, 128))
        dlogits = ((expo / expo_sum - onehot) / total_images).astype(BF)
        dlm[m] = dlogits.astype(F32)
        spread = nt_dot(dlogits, cfull[...])
        for q in range(nq):
            at_q = slice(q * 128, (q + 1) * 128)
            value = spread[:, at_q] / cnti[m]
            dpd[m, :, at_q] = value
            st3[m, 0, q : q + 1, :] = jnp.sum(value * tsum[m, 0, :, at_q], axis=0, keepdims=True)
            st3[m, 0, nq + q : nq + q + 1, :] = jnp.sum(
                value * tsum[m, 1, :, at_q], axis=0, keepdims=True
            )
        stats_send(st3.at[m], st_s.at[2, m], st_r.at[2, m])

    def stage_d(m):
        stats_wait(st3.at[m], st_s.at[2, m], st_r.at[2, m])
        total = stats_sum(st3.at[m])
        n = cntm[m]
        mask = mk[m]
        for q in range(nq):
            at_q = slice(q * 128, (q + 1) * 128)
            gain = n2[0:1, at_q] * bn2[m, 0:1, at_q]
            base = gain * total[q : q + 1] / n
            ramp = gain * total[nq + q : nq + q + 1] / n
            value = image_spread(gain * dpd[m, :, at_q]) * slp[m, :, at_q]
            value = value - mask * (base + ramp * sec[m, :, at_q])
            dsb[:, at_q] = value.astype(BF)
        for q in range(nq):
            at_q = slice(q * 128, (q + 1) * 128)
            bn2[m, 1:2, at_q] = total[nq + q : nq + q + 1]
            bn2[m, 2:3, at_q] = total[q : q + 1]
        back = nt_dot(dsb[...], pfull[...])
        for q in range(nc):
            piece = back[:, q * c1l : (q + 1) * c1l]
            da[m, q % 2, q // 2] = piece
            dab[m, q % 2, q // 2] = piece.astype(BF)
        remote(dab.at[m, 1 - k], sr.at[m], sr_s, sr_r.at[m], sibdev).start()
        pacc[...] += mm(at[m], dsb[...])

    def stage_e(m):
        remote(sr.at[m], sr.at[m], sr_s, sr_r.at[m], sibdev).wait_recv()
        es[m] = (da[m, k, 1 - y] + sr[m, 1 - y].astype(F32)).astype(BF)
        remote(es.at[m], er.at[m], er_s, er_r.at[m], oppdev).start()

    def stage_f(m):
        remote(es.at[m], er.at[m], er_s, er_r.at[m], oppdev).wait_recv()
        upstream = da[m, k, y] + sr[m, y].astype(F32) + er[m].astype(F32)
        normed = (hid[m] - bn1[m, 0:1, :]) * bn1[m, 1:2, :]
        shifted = n1[0:1, :] * normed + n1[1:2, :]
        sigma = sigmoid(shifted)
        upstream = upstream * mk[m] * (sigma * (1.0 + shifted * (1.0 - sigma)))
        du[m] = upstream
        st4[m, 0, 0:1, :] = jnp.sum(upstream, axis=0, keepdims=True)
        st4[m, 0, 1:2, :] = jnp.sum(upstream * normed, axis=0, keepdims=True)
        stats_send(st4.at[m], st_s.at[3, m], st_r.at[3, m])

    def stage_g(m):
        stats_wait(st4.at[m], st_s.at[3, m], st_r.at[3, m])
        total = stats_sum(st4.at[m])
        n = cntm[m]
        bn1[m, 2:3, :] = total[1:2]
        bn1[m, 3:4, :] = total[0:1]
        bn1[m, 4:5, :] = total[2:3]
        normed = (hid[m] - bn1[m, 0:1, :]) * bn1[m, 1:2, :]
        gain = n1[0:1, :] * bn1[m, 1:2, :]
        value = mk[m] * gain * (du[m] - (total[0:1] + normed * total[1:2]) / n)
        dhp[PAD : PAD + pm, :] = value.astype(BF).astype(F32)

        def shifted(t):
            ky, kx = t // 3, t % 3
            off = PAD - (ky - 1) * SIDE - (kx - 1)
            piece = dhp[off : off + pm, :]
            found = edges(2 - ky, 2 - kx)
            return (piece if found is None else piece * found).astype(BF)

        left = xt[m]
        for t in range(0, 9, 2):
            if t < 8:
                pair = mm(left, jnp.concatenate([shifted(t), shifted(t + 1)], axis=1))
                acc[t * c1 : (t + 1) * c1, :] += pair[:, :c1l]
                acc[(t + 1) * c1 : (t + 2) * c1, :] += pair[:, c1l:]
            else:
                acc[t * c1 : (t + 1) * c1, :] += mm(left, shifted(t))

    def scatter_start(total, height, sbuf, xbuf, ss, rr):
        for j in range(nz):
            u = flip(z, j) * 2 + 1 - x
            sbuf[j] = total[pl.ds(pl.multiple_of(u * height, height), height), :].astype(BF)
            remote(sbuf.at[j], xbuf.at[j], ss.at[0], rr.at[j], xdev).start()

    def scatter_middle(total, height, xbuf, zbuf, rbuf, ss, rr):
        for j in list(range(1, nz)) + [0]:
            remote(xbuf.at[j], xbuf.at[j], ss.at[0], rr.at[j], xdev).wait_recv()
            u = flip(z, j) * 2 + x
            found = total[pl.ds(pl.multiple_of(u * height, height), height), :]
            found = found + xbuf[j].astype(F32)
            if j == 0:
                return found
            zbuf[j] = found.astype(BF)
            remote(zbuf.at[j], rbuf.at[j], ss.at[1], rr.at[nz], zdev(j)).start()

    def scatter_finish(found, rbuf, ss, rr):
        if nz > 1:
            got = rbuf.at[pl.ds(1, nz - 1)]
            remote(got, got, ss.at[1], rr.at[nz], xdev).wait_recv()
        for j in range(1, nz):
            found = found + rbuf[j].astype(F32)
        return found

    def scatter_drain(sbuf, zbuf, ss, rr):
        remote(sbuf, sbuf, ss.at[0], rr.at[0], xdev).wait_send()
        if nz > 1:
            sent = zbuf.at[pl.ds(1, nz - 1)]
            remote(sent, sent, ss.at[1], rr.at[0], xdev).wait_send()

    def cls_rows(u):
        return pl.ds(pl.multiple_of(u * images, images), images)

    wide = dla.shape[1] - c2l

    def share_cls():
        mine = jnp.concatenate([dlm[q] for q in range(MICRO)], axis=0).astype(BF)
        dla[cls_rows(d), 0:classes] = mine
        if wide > classes:
            dla[cls_rows(d), classes:wide] = jnp.zeros((images, wide - classes), BF)
        mine = jnp.concatenate([pool[q] for q in range(MICRO)], axis=0).astype(BF)
        dla[cls_rows(d), wide:] = mine
        gather_start(dla, images, dl_s, dl_r)

    def start_proj():
        scatter_start(pacc, rp, gps, gpx, gp_s, gp_r)

    def middle_proj():
        part_sum = scatter_middle(pacc, rp, gpx, gpz, gpr, gp_s, gp_r)
        for q in range(nq):
            gout[r1 + q * rp : r1 + (q + 1) * rp, :] = part_sum[:, q * 128 : (q + 1) * 128]

    def finish_cls():
        gather_finish(cfull, rc, kw_s, kw_r)

    offsets = dict(a=0, b=2, c=4, d=6, e=7, f=9, g=11)
    stages = dict(a=stage_a, b=stage_b, c=stage_c, d=stage_d, e=stage_e, f=stage_f, g=stage_g)
    hooks = {
        (0, "a"): lambda: gather_forward(cfull, rc, kw_s, kw_r, 2),
        (1, "a"): lambda: gather_forward(cfull, rc, kw_s, kw_r, 3),
        (2, "a"): finish_cls,
        (7, "c"): share_cls,
        (9, "d"): start_proj,
        (9, "g"): lambda: gather_forward(dla, images, dl_s, dl_r, 1),
        (11, "f"): lambda: gather_forward(dla, images, dl_s, dl_r, 2),
        (12, "f"): middle_proj,
        (13, "f"): lambda: gather_forward(dla, images, dl_s, dl_r, 3),
    }

    def step(s, carry):
        for name in "acbegfd":
            i = offsets[name]

            @pl.when((s >= i) & (s < i + MICRO))
            def run(name=name, i=i):
                stages[name](s - i)

            for (when, after), hook in hooks.items():
                if after == name:

                    @pl.when(s == when)
                    def extra(hook=hook):
                        hook()

        return carry

    lax.fori_loop(0, MICRO + offsets["g"], step, 0)

    scatter_start(acc, r1, gcs, gcx, gc_s, gc_r)

    gather_finish(dla, images, dl_s, dl_r)
    plt[...] = dla[:, wide:].T
    left = plt[pl.ds(pl.multiple_of(d * rc, rc), rc), :]
    row = r1 + nq * rp
    share = mm(left, dla[:, 0:wide])
    for q in range(wide // 128):
        gout[row + q * rc : row + (q + 1) * rc, :] = share[:, q * 128 : (q + 1) * 128]
    row = row + wide // 128 * rc
    share = jnp.sum(dla[:, 0:wide].astype(F32), axis=0, keepdims=True)
    for q in range(wide // 128):
        gout[row + q : row + q + 1, :] = share[:, q * 128 : (q + 1) * 128]
    row = row + wide // 128
    share = bn2[0, 1:3, :] + bn2[1, 1:3, :] + bn2[2, 1:3, :] + bn2[3, 1:3, :]
    for q in range(nq):
        gout[row + 2 * q : row + 2 * q + 2, :] = share[:, q * 128 : (q + 1) * 128]
    row = row + 2 * nq
    gout[row : row + 2, :] = bn1[0, 2:4, :] + bn1[1, 2:4, :] + bn1[2, 2:4, :] + bn1[3, 2:4, :]
    loss = bn1[0, 4:5, :] + bn1[1, 4:5, :] + bn1[2, 4:5, :] + bn1[3, 4:5, :]
    gout[row + 2 : row + 3, :] = loss / total_images
    if nz > 1:
        got = gpr.at[pl.ds(1, nz - 1)]
        remote(got, got, gp_s.at[1], gp_r.at[nz], xdev).wait_recv()
    for q in range(nq):
        share = gout[r1 + q * rp : r1 + (q + 1) * rp, :]
        for j in range(1, nz):
            share = share + gpr[j, :, q * 128 : (q + 1) * 128].astype(F32)
        gout[r1 + q * rp : r1 + (q + 1) * rp, :] = share

    conv_part = scatter_middle(acc, r1, gcx, gcz, gcr, gc_s, gc_r)
    gout[0:r1, :] = scatter_finish(conv_part, gcr, gc_s, gc_r)

    gather_drain(wfull, r1, cw_s, cw_r)
    gather_drain(pfull, rp, pw_s, pw_r)
    gather_drain(cfull, rc, kw_s, kw_r)
    gather_drain(dla, images, dl_s, dl_r)
    scatter_drain(gps, gpz, gp_s, gp_r)
    scatter_drain(gcs, gcz, gc_s, gc_r)
    sent = xv.at[:, pl.ds(0, 3 * c1l)]
    remote(sent, sent, fx_s, fx_r.at[0, 0], sibdev).wait_send()
    sent = af.at[:, pl.ds(0, 3 * c1l)]
    remote(sent, sent, af_s, af_r.at[0, 0], sibdev).wait_send()
    sent = lgt.at[pl.ds(0, nc - 1)]
    remote(sent, sent, lg_s, lg_r.at[0], sibdev).wait_send()
    remote(sr, sr, sr_s, sr_r.at[0], sibdev).wait_send()
    remote(es, es, er_s, er_r.at[0], oppdev).wait_send()

    def drain(m, carry):
        for i, buf in enumerate((st1, st2, st3, st4)):
            stats_drain(buf.at[m], st_s.at[i, m], st_r.at[i, m])
        return carry

    lax.fori_loop(0, MICRO, drain, 0)


def fused_gradients(
    features, shortcut, valid_masks, labels, w_conv, w_proj, w_cls, cls_bias, norm_one, norm_two
):
    nd, nc = lax.axis_size("dp"), lax.axis_size("chan")
    nz = nd // 2
    pixels, c1l = features.shape
    c2l = shortcut.shape[1]
    images = valid_masks.shape[0]
    imb, pm = images // MICRO, pixels // MICRO
    r1, rp, rc = w_conv.shape[0], w_proj.shape[0], w_cls.shape[0]
    classes = w_cls.shape[1]
    c1 = c1l * nc
    nq = c2l // 128
    wide = -(-classes // 128) * 128
    grad_rows = r1 + nq * rp + wide // 128 * (rc + 1) + 2 * nq + 3
    grad_rows = -(-grad_rows // 8) * 8
    dims = (nd, nc, pm, imb, c1l, c2l, r1, rp, rc, classes, images * nd)
    vmem = pltpu.VMEM
    dma = pltpu.SemaphoreType.DMA
    m4 = MICRO
    scratch = [
        vmem((r1, c1l), F32), vmem((rp, c2l), F32), vmem((rc, classes), F32),
        vmem((9 * c1, c1l), BF), vmem((c1, c2l), BF), vmem((c2l, classes), BF),
        vmem((pixels, c1), BF), vmem((pixels, c2l), BF),
        vmem((m4, pm, c1), BF), vmem((m4, c1, pm), BF),
        vmem((9, PAD + pm + PAD, c1l), F32), vmem((m4, pm, c1l), F32), vmem((m4, pm, 128), F32),
        vmem((4, pm, 128), F32), vmem((m4, 1, 128), F32), vmem((m4, imb, 128), F32),
        vmem((pixels, c1), BF), vmem((m4, c1, pm), BF),
        vmem((m4, pm, c2l), F32), vmem((m4, pm, c2l), F32),
        vmem((m4, 8, c1l), F32), vmem((m4, 8, c2l), F32),
        vmem((m4, 2, imb, c2l), F32), vmem((m4, imb, c2l), F32),
        vmem((m4, nc, imb, classes), F32), vmem((m4, imb, classes), F32), vmem((m4, imb, c2l), F32),
        vmem((pm, c2l), BF), vmem((m4, 2, 2, pm, c1l), F32), vmem((m4, 2, 2, pm, c1l), BF),
        vmem((m4, 2, pm, c1l), BF), vmem((m4, pm, c1l), BF), vmem((m4, pm, c1l), BF),
        vmem((m4, pm, c1l), F32), vmem((PAD + pm + PAD, c1l), F32),
        vmem((9 * c1, c1l), F32), vmem((c1, c2l), F32),
        vmem((m4, nd, 8, c1l), F32),
        vmem((m4, nd, 2 * nq, 128), F32), vmem((m4, nd, 2 * nq, 128), F32),
        vmem((m4, nd, 8, c1l), F32),
        vmem((nz, r1, c1l), BF), vmem((nz, r1, c1l), BF),
        vmem((nz, r1, c1l), BF), vmem((nz, r1, c1l), BF),
        vmem((nz, rp, c2l), BF), vmem((nz, rp, c2l), BF),
        vmem((nz, rp, c2l), BF), vmem((nz, rp, c2l), BF),
        vmem((nd * images, wide + c2l), BF), vmem((c2l, nd * images), BF),
        dma((5,)),
        dma((2,)), dma((nd,)), dma((2,)), dma((nd,)), dma((2,)), dma((nd,)), dma((2,)), dma((nd,)),
        dma, dma((nc, m4)), dma, dma((nc, m4)), dma((4, m4)), dma((4, m4)),
        dma, dma((m4,)), dma, dma((m4,)), dma, dma((m4,)),
        dma((2,)), dma((nz + 1,)), dma((2,)), dma((nz + 1,)),
    ]
    whole = pl.BlockSpec(memory_space=pltpu.VMEM)
    hbm = pl.BlockSpec(memory_space=pl.ANY)
    scalar = pl.BlockSpec(memory_space=pltpu.SMEM)
    shape = jax.ShapeDtypeStruct
    return pl.pallas_call(
        functools.partial(fused_kernel, dims),
        out_shape=shape((grad_rows, 128), F32),
        in_specs=[hbm, hbm, whole, scalar, hbm, hbm, hbm, whole, whole, whole],
        out_specs=whole,
        scratch_shapes=scratch,
        compiler_params=pltpu.CompilerParams(
            collective_id=0, has_side_effects=True, vmem_limit_bytes=58 * 1024 * 1024
        ),
    )(
        features, shortcut, valid_masks, labels, w_conv, w_proj, w_cls,
        cls_bias.reshape(1, classes), norm_one, norm_two,
    )


def adam_kernel(grads, *refs):
    states, outs = refs[:18], refs[18:]
    row = 0
    for i, (rate, decay) in enumerate(ADAM_RATES):
        weight, moment, second = states[3 * i : 3 * i + 3]
        height, width = weight.shape
        for start in range(0, width, 128):
            size = min(128, width - start)
            at_q = slice(start, start + size)
            found = adam_step(
                weight[:, at_q], moment[:, at_q], second[:, at_q],
                grads[row : row + height, 0:size], rate, decay,
            )
            row += height
            for out, value in zip(outs[3 * i : 3 * i + 3], found):
                out[:, at_q] = value
            if i < 3:
                outs[18 + i][:, at_q] = found[0].astype(BF)
    outs[21][...] = grads[row : row + 1, :]


ADAM_RATES = (
    (rate_matrix, weight_decay),
    (rate_matrix, weight_decay),
    (rate_matrix, weight_decay),
    (rate_small, 0.0),
    (rate_small, 0.0),
    (rate_small, 0.0),
)


def fused_device(
    features, shortcut, valid_masks, labels, w_conv, w_proj, w_cls, cls_bias, norm_one, norm_two,
    conv_moment, conv_second, proj_moment, proj_second, cls_moment, cls_second,
    bias_moment, bias_second, one_moment, one_second, two_moment, two_second,
):
    grads = fused_gradients(
        features, shortcut, valid_masks, labels, w_conv, w_proj, w_cls, cls_bias, norm_one, norm_two
    )
    states = (
        (w_conv, conv_moment, conv_second),
        (w_proj, proj_moment, proj_second),
        (w_cls, cls_moment, cls_second),
        (cls_bias.reshape(1, -1), bias_moment.reshape(1, -1), bias_second.reshape(1, -1)),
        (norm_two, two_moment, two_second),
        (norm_one, one_moment, one_second),
    )
    operands, outs = [], []
    for state in states:
        operands += list(state)
        outs += [jax.ShapeDtypeStruct(state[0].shape, F32)] * 3
    outs += [jax.ShapeDtypeStruct(state[0].shape, BF) for state in states[:3]]
    outs.append(jax.ShapeDtypeStruct((1, 128), F32))
    whole = pl.BlockSpec(memory_space=pltpu.VMEM)
    done = list(
        pl.pallas_call(
            adam_kernel,
            out_shape=tuple(outs),
            in_specs=[whole] * (len(operands) + 1),
            out_specs=(whole,) * len(outs),
            compiler_params=pltpu.CompilerParams(vmem_limit_bytes=40 * 1024 * 1024),
        )(grads, *operands)
    )
    biases = [done[i].reshape(-1) for i in (9, 10, 11)]
    return tuple(done[:9] + biases + done[15:18] + done[12:15] + done[18:21]) + (done[21][0, 0],)


def run_device(*args):
    features, shortcut, valid_masks = args[:3]
    w_cls = args[6]
    fits = (
        lax.axis_size("chan") == 4
        and lax.axis_size("dp") in (2, 4, 8)
        and features.shape[1] == 128
        and shortcut.shape[1] % 128 == 0
        and w_cls.shape[0] % 16 == 0
        and valid_masks.shape[0] % (4 * MICRO) == 0
    )
    return (fused_device if fits else per_device)(*args)


def solution(mesh):
    placed = (
        P("dp", "chan"),
        P("dp", "chan"),
        P("dp", None),
        P("dp"),
        P("dp", "chan"),
        P("dp", "chan"),
        P(("chan", "dp"), None),
        P(),
        P(None, "chan"),
        P(None, "chan"),
        P("dp", "chan"),
        P("dp", "chan"),
        P("dp", "chan"),
        P("dp", "chan"),
        P(("chan", "dp"), None),
        P(("chan", "dp"), None),
        P(),
        P(),
        P(None, "chan"),
        P(None, "chan"),
        P(None, "chan"),
        P(None, "chan"),
    )
    return jax.shard_map(
        run_device,
        mesh=mesh,
        in_specs=placed,
        out_specs=(
            P("dp", "chan"),
            P("dp", "chan"),
            P("dp", "chan"),
            P("dp", "chan"),
            P("dp", "chan"),
            P("dp", "chan"),
            P(("chan", "dp"), None),
            P(("chan", "dp"), None),
            P(("chan", "dp"), None),
            P(),
            P(),
            P(),
            P(None, "chan"),
            P(None, "chan"),
            P(None, "chan"),
            P(None, "chan"),
            P(None, "chan"),
            P(None, "chan"),
            P("dp", "chan"),
            P("dp", "chan"),
            P(("chan", "dp"), None),
            P(),
        ),
        check_vma=False,
    )
```

```python
import functools

import jax
import jax.numpy as jnp
from jax import lax
from jax.experimental import pallas as pl
from jax.experimental.pallas import tpu as pltpu
from jax.sharding import PartitionSpec as P

SIDE = 10
MICRO = 4
STEP = 3


norm_eps = 1e-05
adam_eps = 1e-08
beta_decay = 0.5
rate_matrix = 0.02
rate_small = 0.5
weight_decay = 0.01


def tap_columns(flat, images):
    width = flat.shape[1]
    grid = flat.reshape(images, SIDE, SIDE, width)
    padded = jnp.pad(grid, ((0, 0), (1, 1), (1, 1), (0, 0)))
    pieces = [
        padded[:, down : down + SIDE, across : across + SIDE, :]
        for down in range(3)
        for across in range(3)
    ]
    return jnp.concatenate(pieces, axis=3).reshape(images * SIDE * SIDE, 9 * width)


def silu_slope(value):
    sigma = jax.nn.sigmoid(value)
    return sigma * (1.0 + value * (1.0 - sigma))


def norm_forward(hidden, weights, params):
    sums, squares, count = lax.psum(
        (
            jnp.sum(hidden * weights, axis=1),
            jnp.sum(hidden * hidden * weights, axis=1),
            jnp.sum(weights, axis=1),
        ),
        "dp",
    )
    center = sums / count
    scale = lax.rsqrt(squares / count - center * center + norm_eps)
    normed = (hidden - center[:, None]) * scale[:, None]
    return (params[0] * normed + params[1], normed, scale[:, None], count[:, None])


def norm_backward(upstream, normed, scale, count, weights, params):
    total, along = lax.psum((jnp.sum(upstream, axis=1), jnp.sum(upstream * normed, axis=1)), "dp")
    grad = (
        weights
        * params[0]
        * scale
        * (upstream - (total[:, None] + normed * along[:, None]) / count)
    )
    return (grad, jnp.stack([jnp.sum(along, axis=0), jnp.sum(total, axis=0)]))


def contract_rows(left, right):
    return lax.dot_general(
        left, right, (((0,), (0,)), ((), ())), preferred_element_type=jnp.float32
    )


def contract_cols(left, right):
    return lax.dot_general(
        left, right, (((1,), (1,)), ((), ())), preferred_element_type=jnp.float32
    )


def adam_step(weight, moment, second, grad, rate, decay):
    moment = beta_decay * moment + (1.0 - beta_decay) * grad
    second = beta_decay * second + (1.0 - beta_decay) * grad * grad
    correct = 1.0 - beta_decay**STEP
    weight = weight - rate * (
        moment / correct / (jnp.sqrt(second / correct) + adam_eps) + decay * weight
    )
    return (weight, moment, second)


def per_device(
    features,
    shortcut,
    valid_masks,
    labels,
    w_conv,
    w_proj,
    w_cls,
    cls_bias,
    norm_one,
    norm_two,
    conv_moment,
    conv_second,
    proj_moment,
    proj_second,
    cls_moment,
    cls_second,
    bias_moment,
    bias_second,
    one_moment,
    one_second,
    two_moment,
    two_second,
):
    images = valid_masks.shape[0]
    area = SIDE * SIDE
    pixels = images * area
    total_images = images * lax.axis_size("dp")
    classes = w_cls.shape[1]
    conv_full, proj_full, cls_full = (
        lax.all_gather(w_conv.astype(jnp.bfloat16), "dp", axis=0, tiled=True),
        lax.all_gather(w_proj.astype(jnp.bfloat16), "dp", axis=0, tiled=True),
        lax.all_gather(w_cls.astype(jnp.bfloat16), "dp", axis=0, tiled=True),
    )

    def split(flat):
        return flat.reshape((MICRO, -1) + flat.shape[1:])

    def join(parts):
        return parts.reshape((-1,) + parts.shape[2:])

    image_mask = valid_masks.astype(jnp.float32)
    pixel_counts = jnp.sum(image_mask, axis=1)
    weights = split(image_mask.reshape(pixels, 1))
    masked = features * join(weights).astype(jnp.bfloat16)
    gathered = lax.all_gather(masked, "chan", axis=1, tiled=True)
    columns = tap_columns(gathered, images)
    hidden = jnp.dot(columns, conv_full, preferred_element_type=jnp.float32)
    shifted, normed_one, scale_one, count = norm_forward(split(hidden), weights, norm_one)
    active = join((jax.nn.silu(shifted) * weights).astype(jnp.bfloat16))
    active_full = lax.all_gather(active, "chan", axis=1, tiled=True)
    second = jnp.dot(active_full, proj_full, preferred_element_type=jnp.float32)
    shifted_two, normed_two, scale_two, _ = norm_forward(split(second), weights, norm_two)
    summed = shifted_two + split(shortcut.astype(jnp.float32))
    output = jax.nn.silu(summed) * weights
    channels = shortcut.shape[1]
    pooled = (
        jnp.sum(output.reshape(images, area, channels), axis=1) / pixel_counts[:, None]
    ).astype(jnp.bfloat16)
    partial_value = jnp.dot(pooled, cls_full, preferred_element_type=jnp.float32)
    logits = lax.psum(partial_value, "chan") + cls_bias
    top = jnp.max(logits, axis=1, keepdims=True)
    expo = jnp.exp(logits - top)
    expo_sum = jnp.sum(expo, axis=1, keepdims=True)
    onehot = (labels[:, None] == jnp.arange(classes)[None, :]).astype(jnp.float32)
    picked = jnp.sum(logits * onehot, axis=1)
    loss_sum = jnp.sum(top[:, 0] + jnp.log(expo_sum[:, 0]) - picked)
    dlogits = ((expo / expo_sum - onehot) / total_images).astype(jnp.bfloat16)
    grad_bias = jnp.sum(dlogits.astype(jnp.float32), axis=0)
    local_cls = contract_rows(pooled, dlogits)
    grad_pool = contract_cols(dlogits, cls_full)
    spread_back = jnp.broadcast_to(
        (grad_pool / pixel_counts[:, None])[:, None, :], (images, area, channels)
    ).reshape(MICRO, -1, channels)
    upstream_two = spread_back * weights * silu_slope(summed)
    grad_second, grad_two = norm_backward(
        upstream_two, normed_two, scale_two, count, weights, norm_two
    )
    grad_second = join(grad_second.astype(jnp.bfloat16))
    local_proj = contract_rows(active_full, grad_second)
    partial_act = contract_cols(grad_second, proj_full)
    grad_active = lax.psum_scatter(
        partial_act.astype(jnp.bfloat16), "chan", scatter_dimension=1, tiled=True
    ).astype(jnp.float32)
    upstream_one = split(grad_active) * weights * silu_slope(shifted)
    grad_hidden, grad_one = norm_backward(
        upstream_one, normed_one, scale_one, count, weights, norm_one
    )
    local_conv = contract_rows(columns, join(grad_hidden.astype(jnp.bfloat16)))
    sum_conv, sum_proj, sum_cls = (
        lax.psum_scatter(
            local_conv.astype(jnp.bfloat16), "dp", scatter_dimension=0, tiled=True
        ).astype(jnp.float32),
        lax.psum_scatter(
            local_proj.astype(jnp.bfloat16), "dp", scatter_dimension=0, tiled=True
        ).astype(jnp.float32),
        lax.psum_scatter(
            local_cls.astype(jnp.bfloat16), "dp", scatter_dimension=0, tiled=True
        ).astype(jnp.float32),
    )
    loss_total, bias_total = lax.psum((loss_sum, grad_bias), "dp")
    train_loss = loss_total / total_images
    conv_w, conv_m, conv_v = adam_step(
        w_conv, conv_moment, conv_second, sum_conv, rate_matrix, weight_decay
    )
    proj_w, proj_m, proj_v = adam_step(
        w_proj, proj_moment, proj_second, sum_proj, rate_matrix, weight_decay
    )
    cls_w, cls_m, cls_v = adam_step(
        w_cls, cls_moment, cls_second, sum_cls, rate_matrix, weight_decay
    )
    bias_w, bias_m, bias_v = adam_step(
        cls_bias, bias_moment, bias_second, bias_total, rate_small, 0.0
    )
    one_w, one_m, one_v = adam_step(norm_one, one_moment, one_second, grad_one, rate_small, 0.0)
    two_w, two_m, two_v = adam_step(norm_two, two_moment, two_second, grad_two, rate_small, 0.0)
    return (
        conv_w,
        conv_m,
        conv_v,
        proj_w,
        proj_m,
        proj_v,
        cls_w,
        cls_m,
        cls_v,
        bias_w,
        bias_m,
        bias_v,
        one_w,
        one_m,
        one_v,
        two_w,
        two_m,
        two_v,
        conv_w.astype(jnp.bfloat16),
        proj_w.astype(jnp.bfloat16),
        cls_w.astype(jnp.bfloat16),
        train_loss,
    )


MESH = pl.DeviceIdType.MESH
AREA = SIDE * SIDE
PAD = 16
BF = jnp.bfloat16
F32 = jnp.float32


def flip(value, bits):
    bit = 1
    while bit <= bits:
        if bits & bit:
            value = value + bit - 2 * bit * (lax.div(value, bit) % 2)
        bit *= 2
    return value


def nt_dot(left, right):
    return lax.dot_general(left, right, (((1,), (1,)), ((), ())), preferred_element_type=F32)


def mm(left, right):
    return jnp.dot(left, right, preferred_element_type=F32)


def sigmoid(value):
    return 1.0 / (1.0 + jnp.exp(-value))


def row_iota(shape):
    return lax.broadcasted_iota(jnp.int32, shape, 0)


def lane_iota(shape):
    return lax.broadcasted_iota(jnp.int32, shape, 1)


def fused_kernel(dims, *refs):
    nd, nc, pm, imb, c1l, c2l, r1, rp, rc, classes, total_images = dims
    (
        feat, short, masks, labels, wconv, wproj, wcls, cbias, n1, n2, gout,
        wf, pf, cf, wfull, pfull, cfull, xv, sv, xm, xt, yb, hid, mk, edge, cntm, cnti,
        af, at, sec, slp, bn1, bn2, tsum, pool, lgt, dlm, dpd, dsb, da, dab, sr, es, er,
        du, dhp, acc, pacc, st1, st2, st3, st4,
        gcs, gcx, gcz, gcr, gps, gpx, gpz, gpr, dla, plt,
        ld_s, cw_s, cw_r, pw_s, pw_r, kw_s, kw_r, dl_s, dl_r, fx_s, fx_r, af_s, af_r, st_s, st_r,
        lg_s, lg_r, sr_s, sr_r, er_s, er_r, gc_s, gc_r, gp_s, gp_r,
    ) = refs
    nz = nd // 2
    c1 = c1l * nc
    nq = c2l // 128
    d = lax.axis_index("dp")
    c = lax.axis_index("chan")
    z, x = lax.div(d, 2), d % 2
    y, k = lax.div(c, 2), c % 2
    sib = y * 2 + 1 - k
    opp = (1 - y) * 2 + k
    dia = (1 - y) * 2 + 1 - k
    xdev = (z * 2 + 1 - x, c)
    sibdev = (d, sib)
    oppdev = (d, opp)

    def zdev(j):
        return (flip(z, j) * 2 + x, c)

    def remote(src, dst, ssem, rsem, dev):
        return pltpu.make_async_remote_copy(
            src_ref=src, dst_ref=dst, send_sem=ssem, recv_sem=rsem,
            device_id=dev, device_id_type=MESH,
        )

    def unit(buf, u, rows):
        return buf.at[pl.ds(pl.multiple_of(u * rows, rows), rows)]

    leftdev = ((z + nz - 1) % nz * 2 + x, c)
    rightdev = ((z + 1) % nz * 2 + x, c)
    has_left = lax.div(z + nz - 1, nz)
    has_right = 1 - lax.div(z + 1, nz)

    def gather_pieces(buf, rr, u):
        pieces = rr.shape[1]
        size = buf.shape[0] // (nd * pieces)
        for h in range(pieces):
            first = pl.multiple_of(u * (size * pieces) + h * size, size)
            yield buf.at[pl.ds(first, size)], rr.at[u, h]

    def gather_across(buf, ss, rr):
        for mine, arrived in gather_pieces(buf, rr, d):
            remote(mine, mine, ss.at[0], arrived, xdev).start()

    def gather_along(buf, ss, rr):
        for mine, arrived in gather_pieces(buf, rr, d):
            @pl.when(has_left > 0)
            def go_left():
                remote(mine, mine, ss.at[1], arrived, leftdev).start()

            @pl.when(has_right > 0)
            def go_right():
                remote(mine, mine, ss.at[2], arrived, rightdev).start()

    def gather_step(buf, ss, rr, j):
        if j >= nz:
            return

        def pass_on(got, arrived, onward, i, dev):
            copy = remote(got, got, ss.at[0], arrived, xdev)
            copy.wait_recv()
            copy.start()

            @pl.when(onward > 0)
            def go_on():
                remote(got, got, ss.at[i], arrived, dev).start()

        from_left = gather_pieces(buf, rr, (z + nz - j) % nz * 2 + x)
        from_right = gather_pieces(buf, rr, (z + j) % nz * 2 + x)
        for one, two in zip(from_left, from_right):
            @pl.when(z >= j)
            def left():
                pass_on(*one, has_right, 2, rightdev)

            @pl.when(z + j < nz)
            def right():
                pass_on(*two, has_left, 1, leftdev)

    def gather_finish(buf, ss, rr):
        for q in range(nz):
            for got, arrived in gather_pieces(buf, rr, q * 2 + 1 - x):
                remote(got, got, ss.at[0], arrived, xdev).wait_recv()

    def gather_drain(buf, ss, rr):
        def sent(i, units):
            some = buf.at[pl.ds(0, buf.shape[0] // nd * units)]
            remote(some, some, ss.at[i], rr.at[d, 0], xdev).wait_send()

        sent(0, nz)
        for q in range(nz):
            @pl.when(z == q)
            def mine(q=q):
                if q > 0:
                    sent(1, nz - q)
                if q < nz - 1:
                    sent(2, q + 1)

    def stats_send(buf, ss, rr):
        for p in range(1, nd):
            remote(buf.at[0], buf.at[p], ss, rr, (flip(d, p), c)).start()

    def stats_wait(buf, ss, rr):
        got = buf.at[pl.ds(1, nd - 1)]
        remote(got, got, ss, rr, xdev).wait_recv()

    def stats_sum(buf):
        total = buf[d]
        for u in range(1, nd):
            total = total + buf[flip(d, u)]
        return total

    def stats_drain(buf, ss, rr):
        got = buf.at[pl.ds(1, nd - 1)]
        remote(got, got, ss, rr, xdev).wait_send()

    def rows(m):
        return pl.ds(pl.multiple_of(m * pm, pm), pm)

    def lanes(chunk):
        return pl.ds(pl.multiple_of(chunk * c1l, c1l), c1l)

    def part(buf, m, chunk):
        return buf.at[rows(m), lanes(chunk)]

    def local(src, dst, i):
        return pltpu.make_async_copy(src, dst, ld_s.at[i])

    loads = [
        local(wconv, wf, 0),
        local(wproj, pf, 1),
        local(wcls, cf, 2),
        local(feat, xv.at[:, lanes(c)], 3),
        local(short, sv, 4),
    ]
    for load in loads:
        load.start()

    barrier = pltpu.get_barrier_semaphore()
    for dev in (sibdev, oppdev, xdev):
        pl.semaphore_signal(barrier, inc=1, device_id=dev, device_id_type=MESH)

    @pl.when(has_left > 0)
    def greet_left():
        pl.semaphore_signal(barrier, inc=1, device_id=leftdev, device_id_type=MESH)

    @pl.when(has_right > 0)
    def greet_right():
        pl.semaphore_signal(barrier, inc=1, device_id=rightdev, device_id_type=MESH)

    loads[0].wait()
    wfull[pl.ds(pl.multiple_of(d * r1, r1), r1), :] = wf[...].astype(BF)
    pl.semaphore_wait(barrier, 3 + has_left + has_right)

    gather_across(wfull, cw_s, cw_r)
    gather_along(wfull, cw_s, cw_r)
    for m in range(MICRO):
        src = feat.at[pl.ds(m * pm, pm)]
        remote(src, part(xv, m, c), fx_s, fx_r.at[c, m], oppdev).start()
        remote(src, part(xv, m, c), fx_s, fx_r.at[c, m], sibdev).start()

    loads[1].wait()
    pfull[pl.ds(pl.multiple_of(d * rp, rp), rp), :] = pf[...].astype(BF)
    gather_across(pfull, pw_s, pw_r)
    loads[2].wait()
    cfull[pl.ds(pl.multiple_of(d * rc, rc), rc), :] = cf[...].astype(BF)

    pixel = row_iota((pm, 128))
    image = jnp.zeros((pm, 128), jnp.int32)
    for i in range(1, imb):
        image = image + (pixel >= AREA * i).astype(jnp.int32)
    pixel = pixel - AREA * image
    line = jnp.zeros((pm, 128), jnp.int32)
    for i in range(1, SIDE):
        line = line + (pixel >= SIDE * i).astype(jnp.int32)
    across = pixel - SIDE * line
    edge[0] = (line > 0).astype(F32)
    edge[1] = (line < SIDE - 1).astype(F32)
    edge[2] = (across > 0).astype(F32)
    edge[3] = (across < SIDE - 1).astype(F32)
    mask_bf = masks[...].astype(F32).astype(BF)
    images = imb * MICRO
    chosen = (pixel[:, :AREA] == lane_iota((pm, AREA))).astype(F32)
    ones = jnp.ones((AREA, 128), BF)
    image_count = jnp.sum(masks[...].astype(F32), axis=1, keepdims=True)
    for m in range(MICRO):
        away = row_iota((pm, images)) - AREA * (lane_iota((pm, images)) - imb * m)
        owner = jnp.where((away >= 0) & (away < AREA), 1.0, 0.0).astype(BF)
        spread = mm((mm(owner, mask_bf) * chosen).astype(BF), ones)
        mk[m] = spread
        cntm[m] = jnp.sum(spread, axis=0, keepdims=True)
        cnti[m] = jnp.broadcast_to(image_count[m * imb : (m + 1) * imb], (imb, 128))
        st1[m, 0, 2:3, :] = cntm[m]

    yb[:, 0:PAD, :] = jnp.zeros((9, PAD, c1l), F32)
    yb[:, PAD + pm :, :] = jnp.zeros((9, PAD, c1l), F32)
    dhp[0:PAD, :] = jnp.zeros((PAD, c1l), F32)
    dhp[PAD + pm :, :] = jnp.zeros((PAD, c1l), F32)

    def pass_features(m):
        got = part(xv, m, opp)
        copy = remote(got, got, fx_s, fx_r.at[opp, m], sibdev)
        copy.wait_recv()
        copy.start()

    def take_features(m, carry):
        for chunk in (sib, dia):
            got = part(xv, m, chunk)
            remote(got, got, fx_s, fx_r.at[chunk, m], sibdev).wait_recv()
        flat_mask = mk[m].astype(BF)
        for q in range(nc):
            piece = xv[rows(m), q * c1l : (q + 1) * c1l] * flat_mask
            xm[m, :, q * c1l : (q + 1) * c1l] = piece
            xt[m, q * c1l : (q + 1) * c1l, :] = piece.T
        return carry

    gather_step(wfull, cw_s, cw_r, 1)
    pass_features(0)
    gather_step(wfull, cw_s, cw_r, 2)
    gather_along(pfull, pw_s, pw_r)
    gather_along(cfull, kw_s, kw_r)
    pass_features(1)
    pass_features(2)
    loads[3].wait()
    gather_step(wfull, cw_s, cw_r, 3)
    gather_across(cfull, kw_s, kw_r)
    pass_features(3)
    lax.fori_loop(0, MICRO, take_features, 0)
    gather_finish(wfull, cw_s, cw_r)

    def tap(t):
        return wfull[t * c1 : (t + 1) * c1, :]

    def edges(ky, kx):
        found = None
        if ky == 0:
            found = edge[0]
        if ky == 2:
            found = edge[1]
        if kx == 0:
            found = edge[2] if found is None else found * edge[2]
        if kx == 2:
            found = edge[3] if found is None else found * edge[3]
        return found

    def conv(m, carry):
        inputs = xm[m]
        for t in range(0, 9, 2):
            if t < 8:
                pair = mm(inputs, jnp.concatenate([tap(t), tap(t + 1)], axis=1))
                yb[t, PAD : PAD + pm, :] = pair[:, :c1l]
                yb[t + 1, PAD : PAD + pm, :] = pair[:, c1l:]
            else:
                yb[t, PAD : PAD + pm, :] = mm(inputs, tap(t))
        hidden = None
        for kx in range(3):
            column = None
            for ky in range(3):
                off = PAD + (ky - 1) * SIDE + kx - 1
                value = yb[3 * ky + kx, off : off + pm, :]
                if ky != 1:
                    value = value * edge[0 if ky == 0 else 1]
                column = value if column is None else column + value
            if kx != 1:
                column = column * edge[2 if kx == 0 else 3]
            hidden = column if hidden is None else hidden + column
        hid[m] = hidden
        valid = hidden * mk[m]
        st1[m, 0, 0:1, :] = jnp.sum(valid, axis=0, keepdims=True)
        st1[m, 0, 1:2, :] = jnp.sum(valid * hidden, axis=0, keepdims=True)
        stats_send(st1.at[m], st_s.at[0, m], st_r.at[0, m])

        @pl.when(m == 0)
        def move_proj():
            gather_step(pfull, pw_s, pw_r, 1)

        @pl.when(m == 2)
        def move_cls():
            gather_step(cfull, kw_s, kw_r, 1)

        return carry

    lax.fori_loop(0, MICRO, conv, 0)
    acc[...] = jnp.zeros_like(acc)
    pacc[...] = jnp.zeros_like(pacc)

    def activate(m, carry):
        stats_wait(st1.at[m], st_s.at[0, m], st_r.at[0, m])
        totals = stats_sum(st1.at[m])
        n = totals[2:3]
        cntm[m] = n
        center = totals[0:1] / n
        bn1[m, 0:1, :] = center
        bn1[m, 1:2, :] = lax.rsqrt(totals[1:2] / n - center * center + norm_eps)
        normed = (hid[m] - bn1[m, 0:1, :]) * bn1[m, 1:2, :]
        shifted = n1[0:1, :] * normed + n1[1:2, :]
        active = (shifted * sigmoid(shifted) * mk[m]).astype(BF)
        mine = part(af, m, c)
        mine[...] = active
        remote(mine, mine, af_s, af_r.at[c, m], oppdev).start()
        remote(mine, mine, af_s, af_r.at[c, m], sibdev).start()
        return carry

    activate(0, 0)
    gather_step(pfull, pw_s, pw_r, 2)
    lax.fori_loop(1, MICRO, activate, 0)
    gather_step(cfull, kw_s, kw_r, 2)
    gather_step(pfull, pw_s, pw_r, 3)
    gather_finish(pfull, pw_s, pw_r)
    loads[4].wait()

    def turn(m, chunk):
        at[m, lanes_sub(chunk), :] = part(af, m, chunk)[...].T

    def lanes_sub(chunk):
        return pl.ds(pl.multiple_of(chunk * c1l, c1l), c1l)

    def stage_a(m):
        got = part(af, m, opp)
        copy = remote(got, got, af_s, af_r.at[opp, m], sibdev)
        copy.wait_recv()
        copy.start()
        turn(m, c)
        turn(m, opp)
        got = part(af, m, sib)
        remote(got, got, af_s, af_r.at[sib, m], sibdev).wait_recv()
        turn(m, sib)
        got = part(af, m, dia)
        remote(got, got, af_s, af_r.at[dia, m], sibdev).wait_recv()
        turn(m, dia)
        second = mm(af[rows(m), :], pfull[...])
        sec[m] = second
        mask = mk[m]
        for q in range(nq):
            piece = second[:, q * 128 : (q + 1) * 128]
            valid = piece * mask
            st2[m, 0, q : q + 1, :] = jnp.sum(valid, axis=0, keepdims=True)
            st2[m, 0, nq + q : nq + q + 1, :] = jnp.sum(valid * piece, axis=0, keepdims=True)
        stats_send(st2.at[m], st_s.at[1, m], st_r.at[1, m])

    low_half = row_iota((2, 8, 128)) * 0 + lax.broadcasted_iota(jnp.int32, (2, 8, 128), 1)
    tiles = AREA // 4
    half = tiles // 2

    def image_sums(value):
        value = value.reshape(imb // 2, tiles, 8, 128)
        middle = value[:, half]
        first = jnp.sum(value[:, :half], axis=1) + jnp.where(low_half < 4, middle, 0.0)
        last = jnp.sum(value[:, half + 1 :], axis=1) + jnp.where(low_half < 4, 0.0, middle)
        first = jnp.sum(first, axis=1)
        last = jnp.sum(last, axis=1)
        found = []
        for i in range(imb // 2):
            found += [first[i : i + 1], last[i : i + 1]]
        return jnp.concatenate(found, axis=0)

    def image_spread(value):
        pieces = []
        for i in range(imb // 2):
            first = jnp.broadcast_to(value[2 * i : 2 * i + 1], (8, 128))
            last = jnp.broadcast_to(value[2 * i + 1 : 2 * i + 2], (8, 128))
            middle = jnp.where(low_half[0] < 4, first, last)
            pieces.append(jnp.broadcast_to(first[None], (half, 8, 128)))
            pieces.append(middle[None])
            pieces.append(jnp.broadcast_to(last[None], (half, 8, 128)))
        return jnp.concatenate(pieces, axis=0).reshape(pm, 128)

    def stage_b(m):
        stats_wait(st2.at[m], st_s.at[1, m], st_r.at[1, m])
        total = stats_sum(st2.at[m])
        n = cntm[m]
        mask = mk[m]
        for q in range(nq):
            at_q = slice(q * 128, (q + 1) * 128)
            center = total[q : q + 1] / n
            spread = total[nq + q : nq + q + 1] / n - center * center
            scale = lax.rsqrt(spread + norm_eps)
            bn2[m, 0:1, at_q] = scale
            normed = (sec[m, :, at_q] - center) * scale
            sec[m, :, at_q] = normed
            summed = n2[0:1, at_q] * normed + n2[1:2, at_q]
            summed = summed + sv[rows(m), at_q].astype(F32)
            sigma = sigmoid(summed)
            slope = sigma * (1.0 + summed * (1.0 - sigma)) * mask
            slp[m, :, at_q] = slope
            pool[m, :, at_q] = (image_sums(summed * sigma * mask) / cnti[m]).astype(BF).astype(F32)
            tsum[m, 0, :, at_q] = image_sums(slope)
            tsum[m, 1, :, at_q] = image_sums(slope * normed)
        lgt[m, c] = mm(pool[m].astype(BF), cfull[...])
        for dev in (oppdev, (d, dia), sibdev):
            remote(lgt.at[m, c], lgt.at[m, c], lg_s, lg_r.at[m], dev).start()

    def stage_c(m):
        got = lgt.at[m, pl.ds(0, nc - 1)]
        remote(got, got, lg_s, lg_r.at[m], sibdev).wait_recv()
        logits = lgt[m, 0]
        for q in range(1, nc):
            logits = logits + lgt[m, q]
        logits = logits + cbias[...]
        top = jnp.max(logits, axis=1, keepdims=True)
        expo = jnp.exp(logits - top)
        expo_sum = jnp.sum(expo, axis=1, keepdims=True)
        image_row = row_iota((imb, classes))
        target = jnp.zeros((imb, classes), jnp.int32)
        for i in range(imb):
            target = jnp.where(image_row == i, labels[m * imb + i], target)
        onehot = (target == lane_iota((imb, classes))).astype(F32)
        picked = jnp.sum(logits * onehot, axis=1, keepdims=True)
        loss = jnp.sum(top + jnp.log(expo_sum) - picked, axis=0, keepdims=True)
        st4[m, 0, 2:3, :] = jnp.broadcast_to(loss, (1, 128))
        dlogits = ((expo / expo_sum - onehot) / total_images).astype(BF)
        dlm[m] = dlogits.astype(F32)
        spread = nt_dot(dlogits, cfull[...])
        for q in range(nq):
            at_q = slice(q * 128, (q + 1) * 128)
            value = spread[:, at_q] / cnti[m]
            dpd[m, :, at_q] = value
            st3[m, 0, q : q + 1, :] = jnp.sum(value * tsum[m, 0, :, at_q], axis=0, keepdims=True)
            st3[m, 0, nq + q : nq + q + 1, :] = jnp.sum(
                value * tsum[m, 1, :, at_q], axis=0, keepdims=True
            )
        stats_send(st3.at[m], st_s.at[2, m], st_r.at[2, m])

    def stage_d(m):
        stats_wait(st3.at[m], st_s.at[2, m], st_r.at[2, m])
        total = stats_sum(st3.at[m])
        n = cntm[m]
        mask = mk[m]
        for q in range(nq):
            at_q = slice(q * 128, (q + 1) * 128)
            gain = n2[0:1, at_q] * bn2[m, 0:1, at_q]
            base = gain * total[q : q + 1] / n
            ramp = gain * total[nq + q : nq + q + 1] / n
            value = image_spread(gain * dpd[m, :, at_q]) * slp[m, :, at_q]
            value = value - mask * (base + ramp * sec[m, :, at_q])
            dsb[:, at_q] = value.astype(BF)
        for q in range(nq):
            at_q = slice(q * 128, (q + 1) * 128)
            bn2[m, 1:2, at_q] = total[nq + q : nq + q + 1]
            bn2[m, 2:3, at_q] = total[q : q + 1]
        back = nt_dot(dsb[...], pfull[...])
        for q in range(nc):
            piece = back[:, q * c1l : (q + 1) * c1l]
            da[m, q % 2, q // 2] = piece
            dab[m, q % 2, q // 2] = piece.astype(BF)
        remote(dab.at[m, 1 - k], sr.at[m], sr_s, sr_r.at[m], sibdev).start()
        pacc[...] += mm(at[m], dsb[...])

    def stage_e(m):
        remote(sr.at[m], sr.at[m], sr_s, sr_r.at[m], sibdev).wait_recv()
        es[m] = (da[m, k, 1 - y] + sr[m, 1 - y].astype(F32)).astype(BF)
        remote(es.at[m], er.at[m], er_s, er_r.at[m], oppdev).start()

    def stage_f(m):
        remote(es.at[m], er.at[m], er_s, er_r.at[m], oppdev).wait_recv()
        upstream = da[m, k, y] + sr[m, y].astype(F32) + er[m].astype(F32)
        normed = (hid[m] - bn1[m, 0:1, :]) * bn1[m, 1:2, :]
        shifted = n1[0:1, :] * normed + n1[1:2, :]
        sigma = sigmoid(shifted)
        upstream = upstream * mk[m] * (sigma * (1.0 + shifted * (1.0 - sigma)))
        du[m] = upstream
        st4[m, 0, 0:1, :] = jnp.sum(upstream, axis=0, keepdims=True)
        st4[m, 0, 1:2, :] = jnp.sum(upstream * normed, axis=0, keepdims=True)
        stats_send(st4.at[m], st_s.at[3, m], st_r.at[3, m])

    def stage_g(m):
        stats_wait(st4.at[m], st_s.at[3, m], st_r.at[3, m])
        total = stats_sum(st4.at[m])
        n = cntm[m]
        bn1[m, 2:3, :] = total[1:2]
        bn1[m, 3:4, :] = total[0:1]
        bn1[m, 4:5, :] = total[2:3]
        normed = (hid[m] - bn1[m, 0:1, :]) * bn1[m, 1:2, :]
        gain = n1[0:1, :] * bn1[m, 1:2, :]
        value = mk[m] * gain * (du[m] - (total[0:1] + normed * total[1:2]) / n)
        dhp[PAD : PAD + pm, :] = value.astype(BF).astype(F32)

        def shifted(t):
            ky, kx = t // 3, t % 3
            off = PAD - (ky - 1) * SIDE - (kx - 1)
            piece = dhp[off : off + pm, :]
            found = edges(2 - ky, 2 - kx)
            return (piece if found is None else piece * found).astype(BF)

        left = xt[m]
        for t in range(0, 9, 2):
            if t < 8:
                pair = mm(left, jnp.concatenate([shifted(t), shifted(t + 1)], axis=1))
                acc[t * c1 : (t + 1) * c1, :] += pair[:, :c1l]
                acc[(t + 1) * c1 : (t + 2) * c1, :] += pair[:, c1l:]
            else:
                acc[t * c1 : (t + 1) * c1, :] += mm(left, shifted(t))

    def scatter_start(total, height, sbuf, xbuf, ss, rr, js=range(nz)):
        for j in js:
            u = flip(z, j) * 2 + 1 - x
            sbuf[j] = total[pl.ds(pl.multiple_of(u * height, height), height), :].astype(BF)
            remote(sbuf.at[j], xbuf.at[j], ss.at[0], rr.at[j], xdev).start()

    def scatter_middle(total, height, xbuf, zbuf, rbuf, ss, rr):
        for j in list(range(1, nz)) + [0]:
            remote(xbuf.at[j], xbuf.at[j], ss.at[0], rr.at[j], xdev).wait_recv()
            u = flip(z, j) * 2 + x
            found = total[pl.ds(pl.multiple_of(u * height, height), height), :]
            found = found + xbuf[j].astype(F32)
            if j == 0:
                return found
            zbuf[j] = found.astype(BF)
            remote(zbuf.at[j], rbuf.at[j], ss.at[1], rr.at[nz], zdev(j)).start()

    def scatter_finish(found, rbuf, ss, rr):
        if nz > 1:
            got = rbuf.at[pl.ds(1, nz - 1)]
            remote(got, got, ss.at[1], rr.at[nz], xdev).wait_recv()
        for j in range(1, nz):
            found = found + rbuf[j].astype(F32)
        return found

    def scatter_drain(sbuf, zbuf, ss, rr):
        remote(sbuf, sbuf, ss.at[0], rr.at[0], xdev).wait_send()
        if nz > 1:
            sent = zbuf.at[pl.ds(1, nz - 1)]
            remote(sent, sent, ss.at[1], rr.at[0], xdev).wait_send()

    def cls_rows(u):
        return pl.ds(pl.multiple_of(u * images, images), images)

    wide = dla.shape[1] - c2l

    def share_cls():
        mine = jnp.concatenate([dlm[q] for q in range(MICRO)], axis=0).astype(BF)
        dla[cls_rows(d), 0:classes] = mine
        if wide > classes:
            dla[cls_rows(d), classes:wide] = jnp.zeros((images, wide - classes), BF)
        mine = jnp.concatenate([pool[q] for q in range(MICRO)], axis=0).astype(BF)
        dla[cls_rows(d), wide:] = mine
        gather_across(dla, dl_s, dl_r)
        gather_along(dla, dl_s, dl_r)

    def start_proj(j):
        if j < nz:
            scatter_start(pacc, rp, gps, gpx, gp_s, gp_r, [j])

    def middle_proj():
        part_sum = scatter_middle(pacc, rp, gpx, gpz, gpr, gp_s, gp_r)
        for q in range(nq):
            gout[r1 + q * rp : r1 + (q + 1) * rp, :] = part_sum[:, q * 128 : (q + 1) * 128]

    def finish_cls():
        gather_finish(cfull, kw_s, kw_r)

    offsets = dict(a=0, b=2, c=4, d=6, e=7, f=9, g=11)
    stages = dict(a=stage_a, b=stage_b, c=stage_c, d=stage_d, e=stage_e, f=stage_f, g=stage_g)
    hooks = {
        (0, "a"): lambda: gather_step(cfull, kw_s, kw_r, 3),
        (2, "a"): finish_cls,
        (7, "c"): share_cls,
        (9, "d"): lambda: start_proj(1),
        (10, "f"): lambda: start_proj(2),
        (11, "e"): lambda: start_proj(3),
        (12, "d"): lambda: start_proj(0),
        (9, "g"): lambda: gather_step(dla, dl_s, dl_r, 1),
        (11, "f"): lambda: gather_step(dla, dl_s, dl_r, 2),
        (14, "f"): middle_proj,
        (13, "f"): lambda: gather_step(dla, dl_s, dl_r, 3),
    }

    def step(s, carry):
        for name in "acbegfd":
            i = offsets[name]

            @pl.when((s >= i) & (s < i + MICRO))
            def run(name=name, i=i):
                stages[name](s - i)

            for (when, after), hook in hooks.items():
                if after == name:

                    @pl.when(s == when)
                    def extra(hook=hook):
                        hook()

        return carry

    lax.fori_loop(0, MICRO + offsets["g"], step, 0)

    scatter_start(acc, r1, gcs, gcx, gc_s, gc_r)

    gather_finish(dla, dl_s, dl_r)
    plt[...] = dla[:, wide:].T
    left = plt[pl.ds(pl.multiple_of(d * rc, rc), rc), :]
    row = r1 + nq * rp
    share = mm(left, dla[:, 0:wide])
    for q in range(wide // 128):
        gout[row + q * rc : row + (q + 1) * rc, :] = share[:, q * 128 : (q + 1) * 128]
    row = row + wide // 128 * rc
    share = jnp.sum(dla[:, 0:wide].astype(F32), axis=0, keepdims=True)
    for q in range(wide // 128):
        gout[row + q : row + q + 1, :] = share[:, q * 128 : (q + 1) * 128]
    row = row + wide // 128
    share = bn2[0, 1:3, :] + bn2[1, 1:3, :] + bn2[2, 1:3, :] + bn2[3, 1:3, :]
    for q in range(nq):
        gout[row + 2 * q : row + 2 * q + 2, :] = share[:, q * 128 : (q + 1) * 128]
    row = row + 2 * nq
    gout[row : row + 2, :] = bn1[0, 2:4, :] + bn1[1, 2:4, :] + bn1[2, 2:4, :] + bn1[3, 2:4, :]
    loss = bn1[0, 4:5, :] + bn1[1, 4:5, :] + bn1[2, 4:5, :] + bn1[3, 4:5, :]
    gout[row + 2 : row + 3, :] = loss / total_images
    if nz > 1:
        got = gpr.at[pl.ds(1, nz - 1)]
        remote(got, got, gp_s.at[1], gp_r.at[nz], xdev).wait_recv()
    for q in range(nq):
        share = gout[r1 + q * rp : r1 + (q + 1) * rp, :]
        for j in range(1, nz):
            share = share + gpr[j, :, q * 128 : (q + 1) * 128].astype(F32)
        gout[r1 + q * rp : r1 + (q + 1) * rp, :] = share

    conv_part = scatter_middle(acc, r1, gcx, gcz, gcr, gc_s, gc_r)
    gout[0:r1, :] = scatter_finish(conv_part, gcr, gc_s, gc_r)

    gather_drain(wfull, cw_s, cw_r)
    gather_drain(pfull, pw_s, pw_r)
    gather_drain(cfull, kw_s, kw_r)
    gather_drain(dla, dl_s, dl_r)
    scatter_drain(gps, gpz, gp_s, gp_r)
    scatter_drain(gcs, gcz, gc_s, gc_r)
    sent = xv.at[:, pl.ds(0, 3 * c1l)]
    remote(sent, sent, fx_s, fx_r.at[0, 0], sibdev).wait_send()
    sent = af.at[:, pl.ds(0, 3 * c1l)]
    remote(sent, sent, af_s, af_r.at[0, 0], sibdev).wait_send()
    sent = lgt.at[pl.ds(0, nc - 1)]
    remote(sent, sent, lg_s, lg_r.at[0], sibdev).wait_send()
    remote(sr, sr, sr_s, sr_r.at[0], sibdev).wait_send()
    remote(es, es, er_s, er_r.at[0], oppdev).wait_send()

    def drain(m, carry):
        for i, buf in enumerate((st1, st2, st3, st4)):
            stats_drain(buf.at[m], st_s.at[i, m], st_r.at[i, m])
        return carry

    lax.fori_loop(0, MICRO, drain, 0)


def fused_gradients(
    features, shortcut, valid_masks, labels, w_conv, w_proj, w_cls, cls_bias, norm_one, norm_two
):
    nd, nc = lax.axis_size("dp"), lax.axis_size("chan")
    nz = nd // 2
    pixels, c1l = features.shape
    c2l = shortcut.shape[1]
    images = valid_masks.shape[0]
    imb, pm = images // MICRO, pixels // MICRO
    r1, rp, rc = w_conv.shape[0], w_proj.shape[0], w_cls.shape[0]
    classes = w_cls.shape[1]
    c1 = c1l * nc
    nq = c2l // 128
    wide = -(-classes // 128) * 128
    grad_rows = r1 + nq * rp + wide // 128 * (rc + 1) + 2 * nq + 3
    grad_rows = -(-grad_rows // 8) * 8
    dims = (nd, nc, pm, imb, c1l, c2l, r1, rp, rc, classes, images * nd)
    vmem = pltpu.VMEM
    dma = pltpu.SemaphoreType.DMA
    m4 = MICRO
    scratch = [
        vmem((r1, c1l), F32), vmem((rp, c2l), F32), vmem((rc, classes), F32),
        vmem((9 * c1, c1l), BF), vmem((c1, c2l), BF), vmem((c2l, classes), BF),
        vmem((pixels, c1), BF), vmem((pixels, c2l), BF),
        vmem((m4, pm, c1), BF), vmem((m4, c1, pm), BF),
        vmem((9, PAD + pm + PAD, c1l), F32), vmem((m4, pm, c1l), F32), vmem((m4, pm, 128), F32),
        vmem((4, pm, 128), F32), vmem((m4, 1, 128), F32), vmem((m4, imb, 128), F32),
        vmem((pixels, c1), BF), vmem((m4, c1, pm), BF),
        vmem((m4, pm, c2l), F32), vmem((m4, pm, c2l), F32),
        vmem((m4, 8, c1l), F32), vmem((m4, 8, c2l), F32),
        vmem((m4, 2, imb, c2l), F32), vmem((m4, imb, c2l), F32),
        vmem((m4, nc, imb, classes), F32), vmem((m4, imb, classes), F32), vmem((m4, imb, c2l), F32),
        vmem((pm, c2l), BF), vmem((m4, 2, 2, pm, c1l), F32), vmem((m4, 2, 2, pm, c1l), BF),
        vmem((m4, 2, pm, c1l), BF), vmem((m4, pm, c1l), BF), vmem((m4, pm, c1l), BF),
        vmem((m4, pm, c1l), F32), vmem((PAD + pm + PAD, c1l), F32),
        vmem((9 * c1, c1l), F32), vmem((c1, c2l), F32),
        vmem((m4, nd, 8, c1l), F32),
        vmem((m4, nd, 2 * nq, 128), F32), vmem((m4, nd, 2 * nq, 128), F32),
        vmem((m4, nd, 8, c1l), F32),
        vmem((nz, r1, c1l), BF), vmem((nz, r1, c1l), BF),
        vmem((nz, r1, c1l), BF), vmem((nz, r1, c1l), BF),
        vmem((nz, rp, c2l), BF), vmem((nz, rp, c2l), BF),
        vmem((nz, rp, c2l), BF), vmem((nz, rp, c2l), BF),
        vmem((nd * images, wide + c2l), BF), vmem((c2l, nd * images), BF),
        dma((5,)),
        dma((3,)), dma((nd, 3)), dma((3,)), dma((nd, 1)), dma((3,)), dma((nd, 2)),
        dma((3,)), dma((nd, 1)),
        dma, dma((nc, m4)), dma, dma((nc, m4)), dma((4, m4)), dma((4, m4)),
        dma, dma((m4,)), dma, dma((m4,)), dma, dma((m4,)),
        dma((2,)), dma((nz + 1,)), dma((2,)), dma((nz + 1,)),
    ]
    whole = pl.BlockSpec(memory_space=pltpu.VMEM)
    hbm = pl.BlockSpec(memory_space=pl.ANY)
    scalar = pl.BlockSpec(memory_space=pltpu.SMEM)
    shape = jax.ShapeDtypeStruct
    return pl.pallas_call(
        functools.partial(fused_kernel, dims),
        out_shape=shape((grad_rows, 128), F32),
        in_specs=[hbm, hbm, whole, scalar, hbm, hbm, hbm, whole, whole, whole],
        out_specs=whole,
        scratch_shapes=scratch,
        compiler_params=pltpu.CompilerParams(
            collective_id=0, has_side_effects=True, vmem_limit_bytes=58 * 1024 * 1024
        ),
    )(
        features, shortcut, valid_masks, labels, w_conv, w_proj, w_cls,
        cls_bias.reshape(1, classes), norm_one, norm_two,
    )


def adam_kernel(grads, *refs):
    states, outs = refs[:18], refs[18:]
    row = 0
    for i, (rate, decay) in enumerate(ADAM_RATES):
        weight, moment, second = states[3 * i : 3 * i + 3]
        height, width = weight.shape
        for start in range(0, width, 128):
            size = min(128, width - start)
            at_q = slice(start, start + size)
            found = adam_step(
                weight[:, at_q], moment[:, at_q], second[:, at_q],
                grads[row : row + height, 0:size], rate, decay,
            )
            row += height
            for out, value in zip(outs[3 * i : 3 * i + 3], found):
                out[:, at_q] = value
            if i < 3:
                outs[18 + i][:, at_q] = found[0].astype(BF)
    outs[21][...] = grads[row : row + 1, :]


ADAM_RATES = (
    (rate_matrix, weight_decay),
    (rate_matrix, weight_decay),
    (rate_matrix, weight_decay),
    (rate_small, 0.0),
    (rate_small, 0.0),
    (rate_small, 0.0),
)


def fused_device(
    features, shortcut, valid_masks, labels, w_conv, w_proj, w_cls, cls_bias, norm_one, norm_two,
    conv_moment, conv_second, proj_moment, proj_second, cls_moment, cls_second,
    bias_moment, bias_second, one_moment, one_second, two_moment, two_second,
):
    grads = fused_gradients(
        features, shortcut, valid_masks, labels, w_conv, w_proj, w_cls, cls_bias, norm_one, norm_two
    )
    states = (
        (w_conv, conv_moment, conv_second),
        (w_proj, proj_moment, proj_second),
        (w_cls, cls_moment, cls_second),
        (cls_bias.reshape(1, -1), bias_moment.reshape(1, -1), bias_second.reshape(1, -1)),
        (norm_two, two_moment, two_second),
        (norm_one, one_moment, one_second),
    )
    operands, outs = [], []
    for state in states:
        operands += list(state)
        outs += [jax.ShapeDtypeStruct(state[0].shape, F32)] * 3
    outs += [jax.ShapeDtypeStruct(state[0].shape, BF) for state in states[:3]]
    outs.append(jax.ShapeDtypeStruct((1, 128), F32))
    whole = pl.BlockSpec(memory_space=pltpu.VMEM)
    done = list(
        pl.pallas_call(
            adam_kernel,
            out_shape=tuple(outs),
            in_specs=[whole] * (len(operands) + 1),
            out_specs=(whole,) * len(outs),
            compiler_params=pltpu.CompilerParams(vmem_limit_bytes=40 * 1024 * 1024),
        )(grads, *operands)
    )
    biases = [done[i].reshape(-1) for i in (9, 10, 11)]
    return tuple(done[:9] + biases + done[15:18] + done[12:15] + done[18:21]) + (done[21][0, 0],)


def run_device(*args):
    features, shortcut, valid_masks = args[:3]
    w_cls = args[6]
    fits = (
        lax.axis_size("chan") == 4
        and lax.axis_size("dp") in (2, 4, 8)
        and features.shape[1] == 128
        and shortcut.shape[1] % 128 == 0
        and w_cls.shape[0] % 16 == 0
        and valid_masks.shape[0] % (4 * MICRO) == 0
    )
    return (fused_device if fits else per_device)(*args)


def solution(mesh):
    placed = (
        P("dp", "chan"),
        P("dp", "chan"),
        P("dp", None),
        P("dp"),
        P("dp", "chan"),
        P("dp", "chan"),
        P(("chan", "dp"), None),
        P(),
        P(None, "chan"),
        P(None, "chan"),
        P("dp", "chan"),
        P("dp", "chan"),
        P("dp", "chan"),
        P("dp", "chan"),
        P(("chan", "dp"), None),
        P(("chan", "dp"), None),
        P(),
        P(),
        P(None, "chan"),
        P(None, "chan"),
        P(None, "chan"),
        P(None, "chan"),
    )
    return jax.shard_map(
        run_device,
        mesh=mesh,
        in_specs=placed,
        out_specs=(
            P("dp", "chan"),
            P("dp", "chan"),
            P("dp", "chan"),
            P("dp", "chan"),
            P("dp", "chan"),
            P("dp", "chan"),
            P(("chan", "dp"), None),
            P(("chan", "dp"), None),
            P(("chan", "dp"), None),
            P(),
            P(),
            P(),
            P(None, "chan"),
            P(None, "chan"),
            P(None, "chan"),
            P(None, "chan"),
            P(None, "chan"),
            P(None, "chan"),
            P("dp", "chan"),
            P("dp", "chan"),
            P(("chan", "dp"), None),
            P(),
        ),
        check_vma=False,
    )
```

```python
import functools

import jax
import jax.numpy as jnp
from jax import lax
from jax.experimental import pallas as pl
from jax.experimental.pallas import tpu as pltpu
from jax.sharding import PartitionSpec as P

SIDE = 10
MICRO = 4
STEP = 3


norm_eps = 1e-05
adam_eps = 1e-08
beta_decay = 0.5
rate_matrix = 0.02
rate_small = 0.5
weight_decay = 0.01


def tap_columns(flat, images):
    width = flat.shape[1]
    grid = flat.reshape(images, SIDE, SIDE, width)
    padded = jnp.pad(grid, ((0, 0), (1, 1), (1, 1), (0, 0)))
    pieces = [
        padded[:, down : down + SIDE, across : across + SIDE, :]
        for down in range(3)
        for across in range(3)
    ]
    return jnp.concatenate(pieces, axis=3).reshape(images * SIDE * SIDE, 9 * width)


def silu_slope(value):
    sigma = jax.nn.sigmoid(value)
    return sigma * (1.0 + value * (1.0 - sigma))


def norm_forward(hidden, weights, params):
    sums, squares, count = lax.psum(
        (
            jnp.sum(hidden * weights, axis=1),
            jnp.sum(hidden * hidden * weights, axis=1),
            jnp.sum(weights, axis=1),
        ),
        "dp",
    )
    center = sums / count
    scale = lax.rsqrt(squares / count - center * center + norm_eps)
    normed = (hidden - center[:, None]) * scale[:, None]
    return (params[0] * normed + params[1], normed, scale[:, None], count[:, None])


def norm_backward(upstream, normed, scale, count, weights, params):
    total, along = lax.psum((jnp.sum(upstream, axis=1), jnp.sum(upstream * normed, axis=1)), "dp")
    grad = (
        weights
        * params[0]
        * scale
        * (upstream - (total[:, None] + normed * along[:, None]) / count)
    )
    return (grad, jnp.stack([jnp.sum(along, axis=0), jnp.sum(total, axis=0)]))


def contract_rows(left, right):
    return lax.dot_general(
        left, right, (((0,), (0,)), ((), ())), preferred_element_type=jnp.float32
    )


def contract_cols(left, right):
    return lax.dot_general(
        left, right, (((1,), (1,)), ((), ())), preferred_element_type=jnp.float32
    )


def adam_step(weight, moment, second, grad, rate, decay):
    moment = beta_decay * moment + (1.0 - beta_decay) * grad
    second = beta_decay * second + (1.0 - beta_decay) * grad * grad
    correct = 1.0 - beta_decay**STEP
    weight = weight - rate * (
        moment / correct / (jnp.sqrt(second / correct) + adam_eps) + decay * weight
    )
    return (weight, moment, second)


def per_device(
    features,
    shortcut,
    valid_masks,
    labels,
    w_conv,
    w_proj,
    w_cls,
    cls_bias,
    norm_one,
    norm_two,
    conv_moment,
    conv_second,
    proj_moment,
    proj_second,
    cls_moment,
    cls_second,
    bias_moment,
    bias_second,
    one_moment,
    one_second,
    two_moment,
    two_second,
):
    images = valid_masks.shape[0]
    area = SIDE * SIDE
    pixels = images * area
    total_images = images * lax.axis_size("dp")
    classes = w_cls.shape[1]
    conv_full, proj_full, cls_full = (
        lax.all_gather(w_conv.astype(jnp.bfloat16), "dp", axis=0, tiled=True),
        lax.all_gather(w_proj.astype(jnp.bfloat16), "dp", axis=0, tiled=True),
        lax.all_gather(w_cls.astype(jnp.bfloat16), "dp", axis=0, tiled=True),
    )

    def split(flat):
        return flat.reshape((MICRO, -1) + flat.shape[1:])

    def join(parts):
        return parts.reshape((-1,) + parts.shape[2:])

    image_mask = valid_masks.astype(jnp.float32)
    pixel_counts = jnp.sum(image_mask, axis=1)
    weights = split(image_mask.reshape(pixels, 1))
    masked = features * join(weights).astype(jnp.bfloat16)
    gathered = lax.all_gather(masked, "chan", axis=1, tiled=True)
    columns = tap_columns(gathered, images)
    hidden = jnp.dot(columns, conv_full, preferred_element_type=jnp.float32)
    shifted, normed_one, scale_one, count = norm_forward(split(hidden), weights, norm_one)
    active = join((jax.nn.silu(shifted) * weights).astype(jnp.bfloat16))
    active_full = lax.all_gather(active, "chan", axis=1, tiled=True)
    second = jnp.dot(active_full, proj_full, preferred_element_type=jnp.float32)
    shifted_two, normed_two, scale_two, _ = norm_forward(split(second), weights, norm_two)
    summed = shifted_two + split(shortcut.astype(jnp.float32))
    output = jax.nn.silu(summed) * weights
    channels = shortcut.shape[1]
    pooled = (
        jnp.sum(output.reshape(images, area, channels), axis=1) / pixel_counts[:, None]
    ).astype(jnp.bfloat16)
    partial_value = jnp.dot(pooled, cls_full, preferred_element_type=jnp.float32)
    logits = lax.psum(partial_value, "chan") + cls_bias
    top = jnp.max(logits, axis=1, keepdims=True)
    expo = jnp.exp(logits - top)
    expo_sum = jnp.sum(expo, axis=1, keepdims=True)
    onehot = (labels[:, None] == jnp.arange(classes)[None, :]).astype(jnp.float32)
    picked = jnp.sum(logits * onehot, axis=1)
    loss_sum = jnp.sum(top[:, 0] + jnp.log(expo_sum[:, 0]) - picked)
    dlogits = ((expo / expo_sum - onehot) / total_images).astype(jnp.bfloat16)
    grad_bias = jnp.sum(dlogits.astype(jnp.float32), axis=0)
    local_cls = contract_rows(pooled, dlogits)
    grad_pool = contract_cols(dlogits, cls_full)
    spread_back = jnp.broadcast_to(
        (grad_pool / pixel_counts[:, None])[:, None, :], (images, area, channels)
    ).reshape(MICRO, -1, channels)
    upstream_two = spread_back * weights * silu_slope(summed)
    grad_second, grad_two = norm_backward(
        upstream_two, normed_two, scale_two, count, weights, norm_two
    )
    grad_second = join(grad_second.astype(jnp.bfloat16))
    local_proj = contract_rows(active_full, grad_second)
    partial_act = contract_cols(grad_second, proj_full)
    grad_active = lax.psum_scatter(
        partial_act.astype(jnp.bfloat16), "chan", scatter_dimension=1, tiled=True
    ).astype(jnp.float32)
    upstream_one = split(grad_active) * weights * silu_slope(shifted)
    grad_hidden, grad_one = norm_backward(
        upstream_one, normed_one, scale_one, count, weights, norm_one
    )
    local_conv = contract_rows(columns, join(grad_hidden.astype(jnp.bfloat16)))
    sum_conv, sum_proj, sum_cls = (
        lax.psum_scatter(
            local_conv.astype(jnp.bfloat16), "dp", scatter_dimension=0, tiled=True
        ).astype(jnp.float32),
        lax.psum_scatter(
            local_proj.astype(jnp.bfloat16), "dp", scatter_dimension=0, tiled=True
        ).astype(jnp.float32),
        lax.psum_scatter(
            local_cls.astype(jnp.bfloat16), "dp", scatter_dimension=0, tiled=True
        ).astype(jnp.float32),
    )
    loss_total, bias_total = lax.psum((loss_sum, grad_bias), "dp")
    train_loss = loss_total / total_images
    conv_w, conv_m, conv_v = adam_step(
        w_conv, conv_moment, conv_second, sum_conv, rate_matrix, weight_decay
    )
    proj_w, proj_m, proj_v = adam_step(
        w_proj, proj_moment, proj_second, sum_proj, rate_matrix, weight_decay
    )
    cls_w, cls_m, cls_v = adam_step(
        w_cls, cls_moment, cls_second, sum_cls, rate_matrix, weight_decay
    )
    bias_w, bias_m, bias_v = adam_step(
        cls_bias, bias_moment, bias_second, bias_total, rate_small, 0.0
    )
    one_w, one_m, one_v = adam_step(norm_one, one_moment, one_second, grad_one, rate_small, 0.0)
    two_w, two_m, two_v = adam_step(norm_two, two_moment, two_second, grad_two, rate_small, 0.0)
    return (
        conv_w,
        conv_m,
        conv_v,
        proj_w,
        proj_m,
        proj_v,
        cls_w,
        cls_m,
        cls_v,
        bias_w,
        bias_m,
        bias_v,
        one_w,
        one_m,
        one_v,
        two_w,
        two_m,
        two_v,
        conv_w.astype(jnp.bfloat16),
        proj_w.astype(jnp.bfloat16),
        cls_w.astype(jnp.bfloat16),
        train_loss,
    )


MESH = pl.DeviceIdType.MESH
AREA = SIDE * SIDE
PAD = 16
BF = jnp.bfloat16
F32 = jnp.float32


def flip(value, bits):
    bit = 1
    while bit <= bits:
        if bits & bit:
            value = value + bit - 2 * bit * (lax.div(value, bit) % 2)
        bit *= 2
    return value


def nt_dot(left, right):
    return lax.dot_general(left, right, (((1,), (1,)), ((), ())), preferred_element_type=F32)


def mm(left, right):
    return jnp.dot(left, right, preferred_element_type=F32)


def sigmoid(value):
    return 1.0 / (1.0 + jnp.exp(-value))


def row_iota(shape):
    return lax.broadcasted_iota(jnp.int32, shape, 0)


def lane_iota(shape):
    return lax.broadcasted_iota(jnp.int32, shape, 1)


def fused_kernel(dims, *refs):
    nd, nc, pm, imb, c1l, c2l, r1, rp, rc, classes, total_images = dims
    (
        feat, short, masks, labels, wconv, wproj, wcls, cbias, n1, n2, gout,
        wf, pf, cf, wfull, pfull, cfull, xv, sv, xm, xt, yb, hid, mk, edge, cntm, cnti,
        af, at, sec, slp, bn1, bn2, tsum, pool, lgt, dlm, dpd, dsb, da, dab, sr, es, er,
        du, dhp, acc, pacc, st1, st2, st3, st4,
        gcs, gcx, gcz, gcr, gps, gpx, gpz, gpr, dla, plt,
        ld_s, cw_s, cw_r, pw_s, pw_r, kw_s, kw_r, dl_s, dl_r, fx_s, fx_r, af_s, af_r, st_s, st_r,
        lg_s, lg_r, sr_s, sr_r, er_s, er_r, gc_s, gc_r, gp_s, gp_r,
    ) = refs
    nz = nd // 2
    c1 = c1l * nc
    nq = c2l // 128
    d = lax.axis_index("dp")
    c = lax.axis_index("chan")
    z, x = lax.div(d, 2), d % 2
    y, k = lax.div(c, 2), c % 2
    sib = y * 2 + 1 - k
    opp = (1 - y) * 2 + k
    dia = (1 - y) * 2 + 1 - k
    xdev = (z * 2 + 1 - x, c)
    sibdev = (d, sib)
    oppdev = (d, opp)

    def zdev(j):
        return (flip(z, j) * 2 + x, c)

    def remote(src, dst, ssem, rsem, dev):
        return pltpu.make_async_remote_copy(
            src_ref=src, dst_ref=dst, send_sem=ssem, recv_sem=rsem,
            device_id=dev, device_id_type=MESH,
        )

    def unit(buf, u, rows):
        return buf.at[pl.ds(pl.multiple_of(u * rows, rows), rows)]

    leftdev = ((z + nz - 1) % nz * 2 + x, c)
    rightdev = ((z + 1) % nz * 2 + x, c)
    has_left = lax.div(z + nz - 1, nz)
    has_right = 1 - lax.div(z + 1, nz)

    def gather_pieces(buf, rr, u):
        pieces = rr.shape[1]
        size = buf.shape[0] // (nd * pieces)
        for h in range(pieces):
            first = pl.multiple_of(u * (size * pieces) + h * size, size)
            yield buf.at[pl.ds(first, size)], rr.at[u, h]

    def gather_across(buf, ss, rr):
        for mine, arrived in gather_pieces(buf, rr, d):
            remote(mine, mine, ss.at[0], arrived, xdev).start()

    def gather_along(buf, ss, rr):
        for mine, arrived in gather_pieces(buf, rr, d):
            @pl.when(has_left > 0)
            def go_left():
                remote(mine, mine, ss.at[1], arrived, leftdev).start()

            @pl.when(has_right > 0)
            def go_right():
                remote(mine, mine, ss.at[2], arrived, rightdev).start()

    outer = 1 - has_left * has_right

    def gather_far(buf, ss, rr):
        if nz == 4:
            for mine, arrived in gather_pieces(buf, rr, d):
                @pl.when(outer > 0)
                def go_far():
                    remote(mine, mine, ss.at[3], arrived, zdev(3)).start()

    def gather_step(buf, ss, rr, j, relay=True):
        if j >= nz:
            return

        def pass_on(got, arrived, onward, i, dev):
            copy = remote(got, got, ss.at[0], arrived, xdev)
            copy.wait_recv()
            copy.start()

            if relay:
                @pl.when(onward > 0)
                def go_on():
                    remote(got, got, ss.at[i], arrived, dev).start()

        from_left = gather_pieces(buf, rr, (z + nz - j) % nz * 2 + x)
        from_right = gather_pieces(buf, rr, (z + j) % nz * 2 + x)
        for one, two in zip(from_left, from_right):
            @pl.when(z >= j)
            def left():
                pass_on(*one, has_right, 2, rightdev)

            @pl.when(z + j < nz)
            def right():
                pass_on(*two, has_left, 1, leftdev)

    def gather_finish(buf, ss, rr):
        for q in range(nz):
            for got, arrived in gather_pieces(buf, rr, q * 2 + 1 - x):
                remote(got, got, ss.at[0], arrived, xdev).wait_recv()

    def gather_drain(buf, ss, rr, far=False):
        def sent(i, units):
            some = buf.at[pl.ds(0, buf.shape[0] // nd * units)]
            remote(some, some, ss.at[i], rr.at[d, 0], xdev).wait_send()

        sent(0, nz)
        for q in range(nz):
            @pl.when(z == q)
            def mine(q=q):
                if q > 0:
                    sent(1, min(nz - q, 2) if far else nz - q)
                if q < nz - 1:
                    sent(2, min(q + 1, 2) if far else q + 1)
                if far and nz == 4 and q in (0, nz - 1):
                    sent(3, 1)

    def stats_send(buf, ss, rr):
        for p in reversed(range(1, nd)):
            remote(buf.at[0], buf.at[p], ss, rr, (flip(d, p), c)).start()

    def stats_wait(buf, ss, rr):
        got = buf.at[pl.ds(1, nd - 1)]
        remote(got, got, ss, rr, xdev).wait_recv()

    def stats_sum(buf):
        total = buf[d]
        for u in range(1, nd):
            total = total + buf[flip(d, u)]
        return total

    def stats_drain(buf, ss, rr):
        got = buf.at[pl.ds(1, nd - 1)]
        remote(got, got, ss, rr, xdev).wait_send()

    def rows(m):
        return pl.ds(pl.multiple_of(m * pm, pm), pm)

    def lanes(chunk):
        return pl.ds(pl.multiple_of(chunk * c1l, c1l), c1l)

    def part(buf, m, chunk):
        return buf.at[rows(m), lanes(chunk)]

    def local(src, dst, i):
        return pltpu.make_async_copy(src, dst, ld_s.at[i])

    loads = [
        local(wconv, wf, 0),
        local(wproj, pf, 1),
        local(wcls, cf, 2),
        local(feat, xv.at[:, lanes(c)], 3),
        local(short, sv, 4),
    ]
    for load in loads:
        load.start()

    barrier = pltpu.get_barrier_semaphore()
    for dev in (sibdev, oppdev, xdev):
        pl.semaphore_signal(barrier, inc=1, device_id=dev, device_id_type=MESH)

    @pl.when(has_left > 0)
    def greet_left():
        pl.semaphore_signal(barrier, inc=1, device_id=leftdev, device_id_type=MESH)

    @pl.when(has_right > 0)
    def greet_right():
        pl.semaphore_signal(barrier, inc=1, device_id=rightdev, device_id_type=MESH)

    loads[0].wait()
    wfull[pl.ds(pl.multiple_of(d * r1, r1), r1), :] = wf[...].astype(BF)
    pl.semaphore_wait(barrier, 3 + has_left + has_right)

    gather_across(wfull, cw_s, cw_r)
    gather_along(wfull, cw_s, cw_r)
    for m in range(MICRO):
        src = feat.at[pl.ds(m * pm, pm)]
        remote(src, part(xv, m, c), fx_s, fx_r.at[c, m], oppdev).start()
        remote(src, part(xv, m, c), fx_s, fx_r.at[c, m], sibdev).start()

    loads[1].wait()
    pfull[pl.ds(pl.multiple_of(d * rp, rp), rp), :] = pf[...].astype(BF)
    gather_across(pfull, pw_s, pw_r)
    loads[2].wait()
    cfull[pl.ds(pl.multiple_of(d * rc, rc), rc), :] = cf[...].astype(BF)

    pixel = row_iota((pm, 128))
    image = jnp.zeros((pm, 128), jnp.int32)
    for i in range(1, imb):
        image = image + (pixel >= AREA * i).astype(jnp.int32)
    pixel = pixel - AREA * image
    line = jnp.zeros((pm, 128), jnp.int32)
    for i in range(1, SIDE):
        line = line + (pixel >= SIDE * i).astype(jnp.int32)
    across = pixel - SIDE * line
    edge[0] = (line > 0).astype(F32)
    edge[1] = (line < SIDE - 1).astype(F32)
    edge[2] = (across > 0).astype(F32)
    edge[3] = (across < SIDE - 1).astype(F32)
    mask_bf = masks[...].astype(F32).astype(BF)
    images = imb * MICRO
    chosen = (pixel[:, :AREA] == lane_iota((pm, AREA))).astype(F32)
    ones = jnp.ones((AREA, 128), BF)
    image_count = jnp.sum(masks[...].astype(F32), axis=1, keepdims=True)
    for m in range(MICRO):
        away = row_iota((pm, images)) - AREA * (lane_iota((pm, images)) - imb * m)
        owner = jnp.where((away >= 0) & (away < AREA), 1.0, 0.0).astype(BF)
        spread = mm((mm(owner, mask_bf) * chosen).astype(BF), ones)
        mk[m] = spread
        cntm[m] = jnp.sum(spread, axis=0, keepdims=True)
        cnti[m] = jnp.broadcast_to(image_count[m * imb : (m + 1) * imb], (imb, 128))
        st1[m, 0, 2:3, :] = cntm[m]

    yb[:, 0:PAD, :] = jnp.zeros((9, PAD, c1l), F32)
    yb[:, PAD + pm :, :] = jnp.zeros((9, PAD, c1l), F32)
    dhp[0:PAD, :] = jnp.zeros((PAD, c1l), F32)
    dhp[PAD + pm :, :] = jnp.zeros((PAD, c1l), F32)

    def pass_features(m):
        got = part(xv, m, opp)
        copy = remote(got, got, fx_s, fx_r.at[opp, m], sibdev)
        copy.wait_recv()
        copy.start()

    def take_features(m, carry):
        for chunk in (sib, dia):
            got = part(xv, m, chunk)
            remote(got, got, fx_s, fx_r.at[chunk, m], sibdev).wait_recv()
        flat_mask = mk[m].astype(BF)
        for q in range(nc):
            piece = xv[rows(m), q * c1l : (q + 1) * c1l] * flat_mask
            xm[m, :, q * c1l : (q + 1) * c1l] = piece
            xt[m, q * c1l : (q + 1) * c1l, :] = piece.T
        return carry

    gather_step(wfull, cw_s, cw_r, 1)
    pass_features(0)
    gather_step(wfull, cw_s, cw_r, 2)
    gather_along(pfull, pw_s, pw_r)
    gather_far(pfull, pw_s, pw_r)
    gather_along(cfull, kw_s, kw_r)
    pass_features(1)
    pass_features(2)
    loads[3].wait()
    gather_step(wfull, cw_s, cw_r, 3)
    gather_across(cfull, kw_s, kw_r)
    pass_features(3)
    lax.fori_loop(0, MICRO, take_features, 0)
    gather_finish(wfull, cw_s, cw_r)

    def tap(t):
        return wfull[t * c1 : (t + 1) * c1, :]

    def edges(ky, kx):
        found = None
        if ky == 0:
            found = edge[0]
        if ky == 2:
            found = edge[1]
        if kx == 0:
            found = edge[2] if found is None else found * edge[2]
        if kx == 2:
            found = edge[3] if found is None else found * edge[3]
        return found

    def conv(m, carry):
        inputs = xm[m]
        for t in range(0, 9, 2):
            if t < 8:
                pair = mm(inputs, jnp.concatenate([tap(t), tap(t + 1)], axis=1))
                yb[t, PAD : PAD + pm, :] = pair[:, :c1l]
                yb[t + 1, PAD : PAD + pm, :] = pair[:, c1l:]
            else:
                yb[t, PAD : PAD + pm, :] = mm(inputs, tap(t))
        hidden = None
        for kx in range(3):
            column = None
            for ky in range(3):
                off = PAD + (ky - 1) * SIDE + kx - 1
                value = yb[3 * ky + kx, off : off + pm, :]
                if ky != 1:
                    value = value * edge[0 if ky == 0 else 1]
                column = value if column is None else column + value
            if kx != 1:
                column = column * edge[2 if kx == 0 else 3]
            hidden = column if hidden is None else hidden + column
        hid[m] = hidden
        valid = hidden * mk[m]
        st1[m, 0, 0:1, :] = jnp.sum(valid, axis=0, keepdims=True)
        st1[m, 0, 1:2, :] = jnp.sum(valid * hidden, axis=0, keepdims=True)
        stats_send(st1.at[m], st_s.at[0, m], st_r.at[0, m])

        @pl.when(m == 0)
        def move_proj():
            gather_step(pfull, pw_s, pw_r, 1)

        @pl.when(m == 1)
        def move_proj_far():
            gather_step(pfull, pw_s, pw_r, 3)

        @pl.when(m == 2)
        def move_cls():
            gather_far(cfull, kw_s, kw_r)

        @pl.when(m == 3)
        def pass_cls():
            gather_step(cfull, kw_s, kw_r, 1)

        return carry

    lax.fori_loop(0, MICRO, conv, 0)
    acc[...] = jnp.zeros_like(acc)
    pacc[...] = jnp.zeros_like(pacc)

    def activate(m, carry):
        stats_wait(st1.at[m], st_s.at[0, m], st_r.at[0, m])
        totals = stats_sum(st1.at[m])
        n = totals[2:3]
        cntm[m] = n
        center = totals[0:1] / n
        bn1[m, 0:1, :] = center
        bn1[m, 1:2, :] = lax.rsqrt(totals[1:2] / n - center * center + norm_eps)
        normed = (hid[m] - bn1[m, 0:1, :]) * bn1[m, 1:2, :]
        shifted = n1[0:1, :] * normed + n1[1:2, :]
        active = (shifted * sigmoid(shifted) * mk[m]).astype(BF)
        mine = part(af, m, c)
        mine[...] = active
        remote(mine, mine, af_s, af_r.at[c, m], oppdev).start()
        remote(mine, mine, af_s, af_r.at[c, m], sibdev).start()
        return carry

    activate(0, 0)
    gather_step(pfull, pw_s, pw_r, 2, False)
    lax.fori_loop(1, MICRO, activate, 0)
    gather_step(cfull, kw_s, kw_r, 3)
    gather_finish(pfull, pw_s, pw_r)
    loads[4].wait()

    def turn(m, chunk):
        at[m, lanes_sub(chunk), :] = part(af, m, chunk)[...].T

    def lanes_sub(chunk):
        return pl.ds(pl.multiple_of(chunk * c1l, c1l), c1l)

    def stage_a(m):
        got = part(af, m, opp)
        copy = remote(got, got, af_s, af_r.at[opp, m], sibdev)
        copy.wait_recv()
        copy.start()
        turn(m, c)
        turn(m, opp)
        got = part(af, m, sib)
        remote(got, got, af_s, af_r.at[sib, m], sibdev).wait_recv()
        turn(m, sib)
        got = part(af, m, dia)
        remote(got, got, af_s, af_r.at[dia, m], sibdev).wait_recv()
        turn(m, dia)
        second = mm(af[rows(m), :], pfull[...])
        sec[m] = second
        mask = mk[m]
        for q in range(nq):
            piece = second[:, q * 128 : (q + 1) * 128]
            valid = piece * mask
            st2[m, 0, q : q + 1, :] = jnp.sum(valid, axis=0, keepdims=True)
            st2[m, 0, nq + q : nq + q + 1, :] = jnp.sum(valid * piece, axis=0, keepdims=True)
        stats_send(st2.at[m], st_s.at[1, m], st_r.at[1, m])

    low_half = row_iota((2, 8, 128)) * 0 + lax.broadcasted_iota(jnp.int32, (2, 8, 128), 1)
    tiles = AREA // 4
    half = tiles // 2

    def image_sums(value):
        value = value.reshape(imb // 2, tiles, 8, 128)
        middle = value[:, half]
        first = jnp.sum(value[:, :half], axis=1) + jnp.where(low_half < 4, middle, 0.0)
        last = jnp.sum(value[:, half + 1 :], axis=1) + jnp.where(low_half < 4, 0.0, middle)
        first = jnp.sum(first, axis=1)
        last = jnp.sum(last, axis=1)
        found = []
        for i in range(imb // 2):
            found += [first[i : i + 1], last[i : i + 1]]
        return jnp.concatenate(found, axis=0)

    def image_spread(value):
        pieces = []
        for i in range(imb // 2):
            first = jnp.broadcast_to(value[2 * i : 2 * i + 1], (8, 128))
            last = jnp.broadcast_to(value[2 * i + 1 : 2 * i + 2], (8, 128))
            middle = jnp.where(low_half[0] < 4, first, last)
            pieces.append(jnp.broadcast_to(first[None], (half, 8, 128)))
            pieces.append(middle[None])
            pieces.append(jnp.broadcast_to(last[None], (half, 8, 128)))
        return jnp.concatenate(pieces, axis=0).reshape(pm, 128)

    def stage_b(m):
        stats_wait(st2.at[m], st_s.at[1, m], st_r.at[1, m])
        total = stats_sum(st2.at[m])
        n = cntm[m]
        mask = mk[m]
        for q in range(nq):
            at_q = slice(q * 128, (q + 1) * 128)
            center = total[q : q + 1] / n
            spread = total[nq + q : nq + q + 1] / n - center * center
            scale = lax.rsqrt(spread + norm_eps)
            bn2[m, 0:1, at_q] = scale
            normed = (sec[m, :, at_q] - center) * scale
            sec[m, :, at_q] = normed
            summed = n2[0:1, at_q] * normed + n2[1:2, at_q]
            summed = summed + sv[rows(m), at_q].astype(F32)
            sigma = sigmoid(summed)
            slope = sigma * (1.0 + summed * (1.0 - sigma)) * mask
            slp[m, :, at_q] = slope
            pool[m, :, at_q] = (image_sums(summed * sigma * mask) / cnti[m]).astype(BF).astype(F32)
            tsum[m, 0, :, at_q] = image_sums(slope)
            tsum[m, 1, :, at_q] = image_sums(slope * normed)

    def stage_l(m):
        lgt[m, c] = mm(pool[m].astype(BF), cfull[...])
        for dev in (oppdev, (d, dia), sibdev):
            remote(lgt.at[m, c], lgt.at[m, c], lg_s, lg_r.at[m], dev).start()

    def stage_c(m):
        got = lgt.at[m, pl.ds(0, nc - 1)]
        remote(got, got, lg_s, lg_r.at[m], sibdev).wait_recv()
        logits = lgt[m, 0]
        for q in range(1, nc):
            logits = logits + lgt[m, q]
        logits = logits + cbias[...]
        top = jnp.max(logits, axis=1, keepdims=True)
        expo = jnp.exp(logits - top)
        expo_sum = jnp.sum(expo, axis=1, keepdims=True)
        image_row = row_iota((imb, classes))
        target = jnp.zeros((imb, classes), jnp.int32)
        for i in range(imb):
            target = jnp.where(image_row == i, labels[m * imb + i], target)
        onehot = (target == lane_iota((imb, classes))).astype(F32)
        picked = jnp.sum(logits * onehot, axis=1, keepdims=True)
        loss = jnp.sum(top + jnp.log(expo_sum) - picked, axis=0, keepdims=True)
        st4[m, 0, 2:3, :] = jnp.broadcast_to(loss, (1, 128))
        dlogits = ((expo / expo_sum - onehot) / total_images).astype(BF)
        dlm[m] = dlogits.astype(F32)
        spread = nt_dot(dlogits, cfull[...])
        for q in range(nq):
            at_q = slice(q * 128, (q + 1) * 128)
            value = spread[:, at_q] / cnti[m]
            dpd[m, :, at_q] = value
            st3[m, 0, q : q + 1, :] = jnp.sum(value * tsum[m, 0, :, at_q], axis=0, keepdims=True)
            st3[m, 0, nq + q : nq + q + 1, :] = jnp.sum(
                value * tsum[m, 1, :, at_q], axis=0, keepdims=True
            )
        stats_send(st3.at[m], st_s.at[2, m], st_r.at[2, m])

    def stage_d(m):
        stats_wait(st3.at[m], st_s.at[2, m], st_r.at[2, m])
        total = stats_sum(st3.at[m])
        n = cntm[m]
        mask = mk[m]
        for q in range(nq):
            at_q = slice(q * 128, (q + 1) * 128)
            gain = n2[0:1, at_q] * bn2[m, 0:1, at_q]
            base = gain * total[q : q + 1] / n
            ramp = gain * total[nq + q : nq + q + 1] / n
            value = image_spread(gain * dpd[m, :, at_q]) * slp[m, :, at_q]
            value = value - mask * (base + ramp * sec[m, :, at_q])
            dsb[:, at_q] = value.astype(BF)
        for q in range(nq):
            at_q = slice(q * 128, (q + 1) * 128)
            bn2[m, 1:2, at_q] = total[nq + q : nq + q + 1]
            bn2[m, 2:3, at_q] = total[q : q + 1]
        back = nt_dot(dsb[...], pfull[...])
        for q in range(nc):
            piece = back[:, q * c1l : (q + 1) * c1l]
            da[m, q % 2, q // 2] = piece
            dab[m, q % 2, q // 2] = piece.astype(BF)
        remote(dab.at[m, 1 - k], sr.at[m], sr_s, sr_r.at[m], sibdev).start()
        pacc[...] += mm(at[m], dsb[...])

    def stage_e(m):
        remote(sr.at[m], sr.at[m], sr_s, sr_r.at[m], sibdev).wait_recv()
        es[m] = (da[m, k, 1 - y] + sr[m, 1 - y].astype(F32)).astype(BF)
        remote(es.at[m], er.at[m], er_s, er_r.at[m], oppdev).start()

    def stage_f(m):
        remote(es.at[m], er.at[m], er_s, er_r.at[m], oppdev).wait_recv()
        upstream = da[m, k, y] + sr[m, y].astype(F32) + er[m].astype(F32)
        normed = (hid[m] - bn1[m, 0:1, :]) * bn1[m, 1:2, :]
        shifted = n1[0:1, :] * normed + n1[1:2, :]
        sigma = sigmoid(shifted)
        upstream = upstream * mk[m] * (sigma * (1.0 + shifted * (1.0 - sigma)))
        du[m] = upstream
        st4[m, 0, 0:1, :] = jnp.sum(upstream, axis=0, keepdims=True)
        st4[m, 0, 1:2, :] = jnp.sum(upstream * normed, axis=0, keepdims=True)
        stats_send(st4.at[m], st_s.at[3, m], st_r.at[3, m])

    def stage_g(m):
        stats_wait(st4.at[m], st_s.at[3, m], st_r.at[3, m])
        total = stats_sum(st4.at[m])
        n = cntm[m]
        bn1[m, 2:3, :] = total[1:2]
        bn1[m, 3:4, :] = total[0:1]
        bn1[m, 4:5, :] = total[2:3]
        normed = (hid[m] - bn1[m, 0:1, :]) * bn1[m, 1:2, :]
        gain = n1[0:1, :] * bn1[m, 1:2, :]
        value = mk[m] * gain * (du[m] - (total[0:1] + normed * total[1:2]) / n)
        dhp[PAD : PAD + pm, :] = value.astype(BF).astype(F32)

        def shifted(t):
            ky, kx = t // 3, t % 3
            off = PAD - (ky - 1) * SIDE - (kx - 1)
            piece = dhp[off : off + pm, :]
            found = edges(2 - ky, 2 - kx)
            return (piece if found is None else piece * found).astype(BF)

        left = xt[m]
        for t in range(0, 9, 2):
            if t < 8:
                pair = mm(left, jnp.concatenate([shifted(t), shifted(t + 1)], axis=1))
                acc[t * c1 : (t + 1) * c1, :] += pair[:, :c1l]
                acc[(t + 1) * c1 : (t + 2) * c1, :] += pair[:, c1l:]
            else:
                acc[t * c1 : (t + 1) * c1, :] += mm(left, shifted(t))

    orders = [2, 3, 1, 0] if nz == 4 else list(range(nz))

    def scatter_pieces(rr):
        return (rr.shape[0] - 4) // nz

    def scatter_start(total, sbuf, xbuf, ss, rr, js=orders):
        height = sbuf.shape[1]
        size = height // scatter_pieces(rr)
        for j in js:
            u = flip(z, j) * 2 + 1 - x
            for h in range(height // size):
                at_h = pl.ds(h * size, size)
                first = pl.multiple_of(u * height + h * size, size)
                sbuf[j, at_h] = total[pl.ds(first, size), :].astype(BF)
                remote(
                    sbuf.at[j, at_h], xbuf.at[j, at_h], ss.at[0],
                    rr.at[4 + j * (height // size) + h], xdev,
                ).start()

    def scatter_middle(total, xbuf, zbuf, rbuf, ss, rr, js, keep):
        height = xbuf.shape[1]
        pieces = scatter_pieces(rr)
        size = height // pieces
        for j in js:
            u = flip(z, j) * 2 + x
            for h in range(pieces):
                at_h = pl.ds(h * size, size)
                got = xbuf.at[j, at_h]
                remote(got, got, ss.at[0], rr.at[4 + j * pieces + h], xdev).wait_recv()
                first = pl.multiple_of(u * height + h * size, size)
                found = total[pl.ds(first, size), :] + got[...].astype(F32)
                if j == 0:
                    keep(h * size, found)
                    continue
                mine = zbuf.at[j, at_h]
                if j == 2:
                    mine[...] = found.astype(BF)

                    @pl.when(outer > 0)
                    def out_in():
                        to = rbuf.at[2, at_h]
                        remote(mine, to, ss.at[1], rr.at[2], zdev(1)).start()

                    @pl.when(outer == 0)
                    def in_in():
                        to = rbuf.at[0, at_h]
                        remote(mine, to, ss.at[1], rr.at[0], zdev(3)).start()

                    continue
                slot = 2 if j == 3 else 0

                @pl.when(outer > 0)
                def plain():
                    mine[...] = found.astype(BF)

                @pl.when(outer == 0)
                def added():
                    if h == 0:
                        relay = rbuf.at[slot]
                        remote(relay, relay, ss.at[1], rr.at[slot], xdev).wait_recv()
                    mine[...] = (found + rbuf[slot, at_h].astype(F32)).astype(BF)

                remote(mine, rbuf.at[j, at_h], ss.at[1], rr.at[j], zdev(j)).start()

    def scatter_wait(rbuf, ss, rr):
        if nz == 4:
            for j in (3, 1):
                remote(rbuf.at[j], rbuf.at[j], ss.at[1], rr.at[j], xdev).wait_recv()

    def scatter_drain(sbuf, zbuf, ss, rr):
        remote(sbuf, sbuf, ss.at[0], rr.at[0], xdev).wait_send()
        if nz > 1:
            sent = zbuf.at[pl.ds(1, nz - 1)]
            remote(sent, sent, ss.at[1], rr.at[0], xdev).wait_send()

    def cls_rows(u):
        return pl.ds(pl.multiple_of(u * images, images), images)

    wide = dla.shape[1] - c2l

    def share_cls():
        mine = jnp.concatenate([dlm[q] for q in range(MICRO)], axis=0).astype(BF)
        dla[cls_rows(d), 0:classes] = mine
        if wide > classes:
            dla[cls_rows(d), classes:wide] = jnp.zeros((images, wide - classes), BF)
        mine = jnp.concatenate([pool[q] for q in range(MICRO)], axis=0).astype(BF)
        dla[cls_rows(d), wide:] = mine
        gather_across(dla, dl_s, dl_r)
        gather_along(dla, dl_s, dl_r)

    def start_proj(j):
        if j < nz:
            scatter_start(pacc, gps, gpx, gp_s, gp_r, [j])

    def middle_proj(js):
        def keep(first, value):
            for q in range(nq):
                row = r1 + q * rp + first
                gout[row : row + value.shape[0], :] = value[:, q * 128 : (q + 1) * 128]

        scatter_middle(pacc, gpx, gpz, gpr, gp_s, gp_r, js, keep)

    def finish_cls():
        gather_finish(cfull, kw_s, kw_r)

    offsets = dict(a=0, b=2, l=3, c=5, d=8, e=9, f=12, g=14)
    stages = dict(
        a=stage_a, b=stage_b, l=stage_l, c=stage_c, d=stage_d, e=stage_e, f=stage_f, g=stage_g
    )
    hooks = {
        (0, "a"): lambda: gather_step(cfull, kw_s, kw_r, 2, False),
        (3, "a"): finish_cls,
        (8, "c"): share_cls,
        (10, "d"): lambda: gather_step(dla, dl_s, dl_r, 1),
        (11, "d"): lambda: start_proj(2),
        (12, "e"): lambda: gather_step(dla, dl_s, dl_r, 2),
        (12, "f"): lambda: start_proj(3),
        (13, "f"): lambda: start_proj(1),
        (14, "g"): lambda: gather_step(dla, dl_s, dl_r, 3),
        (14, "f"): lambda: start_proj(0),
        (16, "g"): lambda: middle_proj(orders[:1]),
    }

    def step(s, carry):
        for name in "alcbedgf":
            i = offsets[name]

            @pl.when((s >= i) & (s < i + MICRO))
            def run(name=name, i=i):
                stages[name](s - i)

            for (when, after), hook in hooks.items():
                if after == name:

                    @pl.when(s == when)
                    def extra(hook=hook):
                        hook()

        return carry

    lax.fori_loop(0, MICRO + offsets["g"], step, 0)

    scatter_start(acc, gcs, gcx, gc_s, gc_r)
    middle_proj(orders[1:])

    gather_finish(dla, dl_s, dl_r)
    plt[...] = dla[:, wide:].T
    left = plt[pl.ds(pl.multiple_of(d * rc, rc), rc), :]
    row = r1 + nq * rp
    share = mm(left, dla[:, 0:wide])
    for q in range(wide // 128):
        gout[row + q * rc : row + (q + 1) * rc, :] = share[:, q * 128 : (q + 1) * 128]
    row = row + wide // 128 * rc
    share = jnp.sum(dla[:, 0:wide].astype(F32), axis=0, keepdims=True)
    for q in range(wide // 128):
        gout[row + q : row + q + 1, :] = share[:, q * 128 : (q + 1) * 128]
    row = row + wide // 128
    share = bn2[0, 1:3, :] + bn2[1, 1:3, :] + bn2[2, 1:3, :] + bn2[3, 1:3, :]
    for q in range(nq):
        gout[row + 2 * q : row + 2 * q + 2, :] = share[:, q * 128 : (q + 1) * 128]
    row = row + 2 * nq
    gout[row : row + 2, :] = bn1[0, 2:4, :] + bn1[1, 2:4, :] + bn1[2, 2:4, :] + bn1[3, 2:4, :]
    loss = bn1[0, 4:5, :] + bn1[1, 4:5, :] + bn1[2, 4:5, :] + bn1[3, 4:5, :]
    gout[row + 2 : row + 3, :] = loss / total_images
    scatter_wait(gpr, gp_s, gp_r)
    if nz == 4:
        for q in range(nq):
            at_q = slice(q * 128, (q + 1) * 128)
            share = gpr[1, :, at_q].astype(F32) + gpr[3, :, at_q].astype(F32)
            gout[r1 + q * rp : r1 + (q + 1) * rp, :] += share

    def keep_conv(first, value):
        gout[first : first + value.shape[0], :] = value

    scatter_middle(acc, gcx, gcz, gcr, gc_s, gc_r, orders, keep_conv)
    scatter_wait(gcr, gc_s, gc_r)
    if nz == 4:
        gout[0:r1, :] += gcr[1].astype(F32) + gcr[3].astype(F32)

    gather_drain(wfull, cw_s, cw_r)
    gather_drain(pfull, pw_s, pw_r, True)
    gather_drain(cfull, kw_s, kw_r, True)
    gather_drain(dla, dl_s, dl_r)
    scatter_drain(gps, gpz, gp_s, gp_r)
    scatter_drain(gcs, gcz, gc_s, gc_r)
    sent = xv.at[:, pl.ds(0, 3 * c1l)]
    remote(sent, sent, fx_s, fx_r.at[0, 0], sibdev).wait_send()
    sent = af.at[:, pl.ds(0, 3 * c1l)]
    remote(sent, sent, af_s, af_r.at[0, 0], sibdev).wait_send()
    sent = lgt.at[pl.ds(0, nc - 1)]
    remote(sent, sent, lg_s, lg_r.at[0], sibdev).wait_send()
    remote(sr, sr, sr_s, sr_r.at[0], sibdev).wait_send()
    remote(es, es, er_s, er_r.at[0], oppdev).wait_send()

    def drain(m, carry):
        for i, buf in enumerate((st1, st2, st3, st4)):
            stats_drain(buf.at[m], st_s.at[i, m], st_r.at[i, m])
        return carry

    lax.fori_loop(0, MICRO, drain, 0)


def fused_gradients(
    features, shortcut, valid_masks, labels, w_conv, w_proj, w_cls, cls_bias, norm_one, norm_two
):
    nd, nc = lax.axis_size("dp"), lax.axis_size("chan")
    nz = nd // 2
    pixels, c1l = features.shape
    c2l = shortcut.shape[1]
    images = valid_masks.shape[0]
    imb, pm = images // MICRO, pixels // MICRO
    r1, rp, rc = w_conv.shape[0], w_proj.shape[0], w_cls.shape[0]
    classes = w_cls.shape[1]
    c1 = c1l * nc
    nq = c2l // 128
    wide = -(-classes // 128) * 128
    grad_rows = r1 + nq * rp + wide // 128 * (rc + 1) + 2 * nq + 3
    grad_rows = -(-grad_rows // 8) * 8
    dims = (nd, nc, pm, imb, c1l, c2l, r1, rp, rc, classes, images * nd)
    vmem = pltpu.VMEM
    dma = pltpu.SemaphoreType.DMA
    m4 = MICRO
    scratch = [
        vmem((r1, c1l), F32), vmem((rp, c2l), F32), vmem((rc, classes), F32),
        vmem((9 * c1, c1l), BF), vmem((c1, c2l), BF), vmem((c2l, classes), BF),
        vmem((pixels, c1), BF), vmem((pixels, c2l), BF),
        vmem((m4, pm, c1), BF), vmem((m4, c1, pm), BF),
        vmem((9, PAD + pm + PAD, c1l), F32), vmem((m4, pm, c1l), F32), vmem((m4, pm, 128), F32),
        vmem((4, pm, 128), F32), vmem((m4, 1, 128), F32), vmem((m4, imb, 128), F32),
        vmem((pixels, c1), BF), vmem((m4, c1, pm), BF),
        vmem((m4, pm, c2l), F32), vmem((m4, pm, c2l), F32),
        vmem((m4, 8, c1l), F32), vmem((m4, 8, c2l), F32),
        vmem((m4, 2, imb, c2l), F32), vmem((m4, imb, c2l), F32),
        vmem((m4, nc, imb, classes), F32), vmem((m4, imb, classes), F32), vmem((m4, imb, c2l), F32),
        vmem((pm, c2l), BF), vmem((m4, 2, 2, pm, c1l), F32), vmem((m4, 2, 2, pm, c1l), BF),
        vmem((m4, 2, pm, c1l), BF), vmem((m4, pm, c1l), BF), vmem((m4, pm, c1l), BF),
        vmem((m4, pm, c1l), F32), vmem((PAD + pm + PAD, c1l), F32),
        vmem((9 * c1, c1l), F32), vmem((c1, c2l), F32),
        vmem((m4, nd, 8, c1l), F32),
        vmem((m4, nd, 2 * nq, 128), F32), vmem((m4, nd, 2 * nq, 128), F32),
        vmem((m4, nd, 8, c1l), F32),
        vmem((nz, r1, c1l), BF), vmem((nz, r1, c1l), BF),
        vmem((nz, r1, c1l), BF), vmem((nz, r1, c1l), BF),
        vmem((nz, rp, c2l), BF), vmem((nz, rp, c2l), BF),
        vmem((nz, rp, c2l), BF), vmem((nz, rp, c2l), BF),
        vmem((nd * images, wide + c2l), BF), vmem((c2l, nd * images), BF),
        dma((5,)),
        dma((4,)), dma((nd, 3)), dma((4,)), dma((nd, 1)), dma((4,)), dma((nd, 2)),
        dma((4,)), dma((nd, 1)),
        dma, dma((nc, m4)), dma, dma((nc, m4)), dma((4, m4)), dma((4, m4)),
        dma, dma((m4,)), dma, dma((m4,)), dma, dma((m4,)),
        dma((2,)), dma((4 + 2 * nz,)), dma((2,)), dma((4 + nz,)),
    ]
    whole = pl.BlockSpec(memory_space=pltpu.VMEM)
    hbm = pl.BlockSpec(memory_space=pl.ANY)
    scalar = pl.BlockSpec(memory_space=pltpu.SMEM)
    shape = jax.ShapeDtypeStruct
    return pl.pallas_call(
        functools.partial(fused_kernel, dims),
        out_shape=shape((grad_rows, 128), F32),
        in_specs=[hbm, hbm, whole, scalar, hbm, hbm, hbm, whole, whole, whole],
        out_specs=whole,
        scratch_shapes=scratch,
        compiler_params=pltpu.CompilerParams(
            collective_id=0, has_side_effects=True, vmem_limit_bytes=58 * 1024 * 1024
        ),
    )(
        features, shortcut, valid_masks, labels, w_conv, w_proj, w_cls,
        cls_bias.reshape(1, classes), norm_one, norm_two,
    )


def adam_kernel(grads, *refs):
    states, outs = refs[:18], refs[18:]
    row = 0
    for i, (rate, decay) in enumerate(ADAM_RATES):
        weight, moment, second = states[3 * i : 3 * i + 3]
        height, width = weight.shape
        for start in range(0, width, 128):
            size = min(128, width - start)
            at_q = slice(start, start + size)
            found = adam_step(
                weight[:, at_q], moment[:, at_q], second[:, at_q],
                grads[row : row + height, 0:size], rate, decay,
            )
            row += height
            for out, value in zip(outs[3 * i : 3 * i + 3], found):
                out[:, at_q] = value
            if i < 3:
                outs[18 + i][:, at_q] = found[0].astype(BF)
    outs[21][...] = grads[row : row + 1, :]


ADAM_RATES = (
    (rate_matrix, weight_decay),
    (rate_matrix, weight_decay),
    (rate_matrix, weight_decay),
    (rate_small, 0.0),
    (rate_small, 0.0),
    (rate_small, 0.0),
)


def fused_device(
    features, shortcut, valid_masks, labels, w_conv, w_proj, w_cls, cls_bias, norm_one, norm_two,
    conv_moment, conv_second, proj_moment, proj_second, cls_moment, cls_second,
    bias_moment, bias_second, one_moment, one_second, two_moment, two_second,
):
    grads = fused_gradients(
        features, shortcut, valid_masks, labels, w_conv, w_proj, w_cls, cls_bias, norm_one, norm_two
    )
    states = (
        (w_conv, conv_moment, conv_second),
        (w_proj, proj_moment, proj_second),
        (w_cls, cls_moment, cls_second),
        (cls_bias.reshape(1, -1), bias_moment.reshape(1, -1), bias_second.reshape(1, -1)),
        (norm_two, two_moment, two_second),
        (norm_one, one_moment, one_second),
    )
    operands, outs = [], []
    for state in states:
        operands += list(state)
        outs += [jax.ShapeDtypeStruct(state[0].shape, F32)] * 3
    outs += [jax.ShapeDtypeStruct(state[0].shape, BF) for state in states[:3]]
    outs.append(jax.ShapeDtypeStruct((1, 128), F32))
    whole = pl.BlockSpec(memory_space=pltpu.VMEM)
    done = list(
        pl.pallas_call(
            adam_kernel,
            out_shape=tuple(outs),
            in_specs=[whole] * (len(operands) + 1),
            out_specs=(whole,) * len(outs),
            compiler_params=pltpu.CompilerParams(vmem_limit_bytes=40 * 1024 * 1024),
        )(grads, *operands)
    )
    biases = [done[i].reshape(-1) for i in (9, 10, 11)]
    return tuple(done[:9] + biases + done[15:18] + done[12:15] + done[18:21]) + (done[21][0, 0],)


def run_device(*args):
    features, shortcut, valid_masks = args[:3]
    w_cls = args[6]
    fits = (
        lax.axis_size("chan") == 4
        and lax.axis_size("dp") in (2, 8)
        and features.shape[1] == 128
        and shortcut.shape[1] % 128 == 0
        and w_cls.shape[0] % 16 == 0
        and valid_masks.shape[0] % (4 * MICRO) == 0
    )
    return (fused_device if fits else per_device)(*args)


def solution(mesh):
    placed = (
        P("dp", "chan"),
        P("dp", "chan"),
        P("dp", None),
        P("dp"),
        P("dp", "chan"),
        P("dp", "chan"),
        P(("chan", "dp"), None),
        P(),
        P(None, "chan"),
        P(None, "chan"),
        P("dp", "chan"),
        P("dp", "chan"),
        P("dp", "chan"),
        P("dp", "chan"),
        P(("chan", "dp"), None),
        P(("chan", "dp"), None),
        P(),
        P(),
        P(None, "chan"),
        P(None, "chan"),
        P(None, "chan"),
        P(None, "chan"),
    )
    return jax.shard_map(
        run_device,
        mesh=mesh,
        in_specs=placed,
        out_specs=(
            P("dp", "chan"),
            P("dp", "chan"),
            P("dp", "chan"),
            P("dp", "chan"),
            P("dp", "chan"),
            P("dp", "chan"),
            P(("chan", "dp"), None),
            P(("chan", "dp"), None),
            P(("chan", "dp"), None),
            P(),
            P(),
            P(),
            P(None, "chan"),
            P(None, "chan"),
            P(None, "chan"),
            P(None, "chan"),
            P(None, "chan"),
            P(None, "chan"),
            P("dp", "chan"),
            P("dp", "chan"),
            P(("chan", "dp"), None),
            P(),
        ),
        check_vma=False,
    )
```

```python
import functools

import jax
import jax.numpy as jnp
from jax import lax
from jax.experimental import pallas as pl
from jax.experimental.pallas import tpu as pltpu
from jax.sharding import PartitionSpec as P

SIDE = 10
MICRO = 4
STEP = 3


norm_eps = 1e-05
adam_eps = 1e-08
beta_decay = 0.5
rate_matrix = 0.02
rate_small = 0.5
weight_decay = 0.01


def tap_columns(flat, images):
    width = flat.shape[1]
    grid = flat.reshape(images, SIDE, SIDE, width)
    padded = jnp.pad(grid, ((0, 0), (1, 1), (1, 1), (0, 0)))
    pieces = [
        padded[:, down : down + SIDE, across : across + SIDE, :]
        for down in range(3)
        for across in range(3)
    ]
    return jnp.concatenate(pieces, axis=3).reshape(images * SIDE * SIDE, 9 * width)


def silu_slope(value):
    sigma = jax.nn.sigmoid(value)
    return sigma * (1.0 + value * (1.0 - sigma))


def norm_forward(hidden, weights, params):
    sums, squares, count = lax.psum(
        (
            jnp.sum(hidden * weights, axis=1),
            jnp.sum(hidden * hidden * weights, axis=1),
            jnp.sum(weights, axis=1),
        ),
        "dp",
    )
    center = sums / count
    scale = lax.rsqrt(squares / count - center * center + norm_eps)
    normed = (hidden - center[:, None]) * scale[:, None]
    return (params[0] * normed + params[1], normed, scale[:, None], count[:, None])


def norm_backward(upstream, normed, scale, count, weights, params):
    total, along = lax.psum((jnp.sum(upstream, axis=1), jnp.sum(upstream * normed, axis=1)), "dp")
    grad = (
        weights
        * params[0]
        * scale
        * (upstream - (total[:, None] + normed * along[:, None]) / count)
    )
    return (grad, jnp.stack([jnp.sum(along, axis=0), jnp.sum(total, axis=0)]))


def contract_rows(left, right):
    return lax.dot_general(
        left, right, (((0,), (0,)), ((), ())), preferred_element_type=jnp.float32
    )


def contract_cols(left, right):
    return lax.dot_general(
        left, right, (((1,), (1,)), ((), ())), preferred_element_type=jnp.float32
    )


def adam_step(weight, moment, second, grad, rate, decay):
    moment = beta_decay * moment + (1.0 - beta_decay) * grad
    second = beta_decay * second + (1.0 - beta_decay) * grad * grad
    correct = 1.0 - beta_decay**STEP
    weight = weight - rate * (
        moment / correct / (jnp.sqrt(second / correct) + adam_eps) + decay * weight
    )
    return (weight, moment, second)


def per_device(
    features,
    shortcut,
    valid_masks,
    labels,
    w_conv,
    w_proj,
    w_cls,
    cls_bias,
    norm_one,
    norm_two,
    conv_moment,
    conv_second,
    proj_moment,
    proj_second,
    cls_moment,
    cls_second,
    bias_moment,
    bias_second,
    one_moment,
    one_second,
    two_moment,
    two_second,
):
    images = valid_masks.shape[0]
    area = SIDE * SIDE
    pixels = images * area
    total_images = images * lax.axis_size("dp")
    classes = w_cls.shape[1]
    conv_full, proj_full, cls_full = (
        lax.all_gather(w_conv.astype(jnp.bfloat16), "dp", axis=0, tiled=True),
        lax.all_gather(w_proj.astype(jnp.bfloat16), "dp", axis=0, tiled=True),
        lax.all_gather(w_cls.astype(jnp.bfloat16), "dp", axis=0, tiled=True),
    )

    def split(flat):
        return flat.reshape((MICRO, -1) + flat.shape[1:])

    def join(parts):
        return parts.reshape((-1,) + parts.shape[2:])

    image_mask = valid_masks.astype(jnp.float32)
    pixel_counts = jnp.sum(image_mask, axis=1)
    weights = split(image_mask.reshape(pixels, 1))
    masked = features * join(weights).astype(jnp.bfloat16)
    gathered = lax.all_gather(masked, "chan", axis=1, tiled=True)
    columns = tap_columns(gathered, images)
    hidden = jnp.dot(columns, conv_full, preferred_element_type=jnp.float32)
    shifted, normed_one, scale_one, count = norm_forward(split(hidden), weights, norm_one)
    active = join((jax.nn.silu(shifted) * weights).astype(jnp.bfloat16))
    active_full = lax.all_gather(active, "chan", axis=1, tiled=True)
    second = jnp.dot(active_full, proj_full, preferred_element_type=jnp.float32)
    shifted_two, normed_two, scale_two, _ = norm_forward(split(second), weights, norm_two)
    summed = shifted_two + split(shortcut.astype(jnp.float32))
    output = jax.nn.silu(summed) * weights
    channels = shortcut.shape[1]
    pooled = (
        jnp.sum(output.reshape(images, area, channels), axis=1) / pixel_counts[:, None]
    ).astype(jnp.bfloat16)
    partial_value = jnp.dot(pooled, cls_full, preferred_element_type=jnp.float32)
    logits = lax.psum(partial_value, "chan") + cls_bias
    top = jnp.max(logits, axis=1, keepdims=True)
    expo = jnp.exp(logits - top)
    expo_sum = jnp.sum(expo, axis=1, keepdims=True)
    onehot = (labels[:, None] == jnp.arange(classes)[None, :]).astype(jnp.float32)
    picked = jnp.sum(logits * onehot, axis=1)
    loss_sum = jnp.sum(top[:, 0] + jnp.log(expo_sum[:, 0]) - picked)
    dlogits = ((expo / expo_sum - onehot) / total_images).astype(jnp.bfloat16)
    grad_bias = jnp.sum(dlogits.astype(jnp.float32), axis=0)
    local_cls = contract_rows(pooled, dlogits)
    grad_pool = contract_cols(dlogits, cls_full)
    spread_back = jnp.broadcast_to(
        (grad_pool / pixel_counts[:, None])[:, None, :], (images, area, channels)
    ).reshape(MICRO, -1, channels)
    upstream_two = spread_back * weights * silu_slope(summed)
    grad_second, grad_two = norm_backward(
        upstream_two, normed_two, scale_two, count, weights, norm_two
    )
    grad_second = join(grad_second.astype(jnp.bfloat16))
    local_proj = contract_rows(active_full, grad_second)
    partial_act = contract_cols(grad_second, proj_full)
    grad_active = lax.psum_scatter(
        partial_act.astype(jnp.bfloat16), "chan", scatter_dimension=1, tiled=True
    ).astype(jnp.float32)
    upstream_one = split(grad_active) * weights * silu_slope(shifted)
    grad_hidden, grad_one = norm_backward(
        upstream_one, normed_one, scale_one, count, weights, norm_one
    )
    local_conv = contract_rows(columns, join(grad_hidden.astype(jnp.bfloat16)))
    sum_conv, sum_proj, sum_cls = (
        lax.psum_scatter(
            local_conv.astype(jnp.bfloat16), "dp", scatter_dimension=0, tiled=True
        ).astype(jnp.float32),
        lax.psum_scatter(
            local_proj.astype(jnp.bfloat16), "dp", scatter_dimension=0, tiled=True
        ).astype(jnp.float32),
        lax.psum_scatter(
            local_cls.astype(jnp.bfloat16), "dp", scatter_dimension=0, tiled=True
        ).astype(jnp.float32),
    )
    loss_total, bias_total = lax.psum((loss_sum, grad_bias), "dp")
    train_loss = loss_total / total_images
    conv_w, conv_m, conv_v = adam_step(
        w_conv, conv_moment, conv_second, sum_conv, rate_matrix, weight_decay
    )
    proj_w, proj_m, proj_v = adam_step(
        w_proj, proj_moment, proj_second, sum_proj, rate_matrix, weight_decay
    )
    cls_w, cls_m, cls_v = adam_step(
        w_cls, cls_moment, cls_second, sum_cls, rate_matrix, weight_decay
    )
    bias_w, bias_m, bias_v = adam_step(
        cls_bias, bias_moment, bias_second, bias_total, rate_small, 0.0
    )
    one_w, one_m, one_v = adam_step(norm_one, one_moment, one_second, grad_one, rate_small, 0.0)
    two_w, two_m, two_v = adam_step(norm_two, two_moment, two_second, grad_two, rate_small, 0.0)
    return (
        conv_w,
        conv_m,
        conv_v,
        proj_w,
        proj_m,
        proj_v,
        cls_w,
        cls_m,
        cls_v,
        bias_w,
        bias_m,
        bias_v,
        one_w,
        one_m,
        one_v,
        two_w,
        two_m,
        two_v,
        conv_w.astype(jnp.bfloat16),
        proj_w.astype(jnp.bfloat16),
        cls_w.astype(jnp.bfloat16),
        train_loss,
    )


MESH = pl.DeviceIdType.MESH
AREA = SIDE * SIDE
PAD = 16
BF = jnp.bfloat16
F32 = jnp.float32


def flip(value, bits):
    bit = 1
    while bit <= bits:
        if bits & bit:
            value = value + bit - 2 * bit * (lax.div(value, bit) % 2)
        bit *= 2
    return value


def nt_dot(left, right):
    return lax.dot_general(left, right, (((1,), (1,)), ((), ())), preferred_element_type=F32)


def mm(left, right):
    return jnp.dot(left, right, preferred_element_type=F32)


def sigmoid(value):
    return 1.0 / (1.0 + jnp.exp(-value))


def row_iota(shape):
    return lax.broadcasted_iota(jnp.int32, shape, 0)


def lane_iota(shape):
    return lax.broadcasted_iota(jnp.int32, shape, 1)


def fused_kernel(dims, *refs):
    nd, nc, pm, imb, c1l, c2l, r1, rp, rc, classes, total_images = dims
    (
        feat, short, masks, labels, wconv, wproj, wcls, cbias, n1, n2, gout,
        wf, pf, cf, wfull, pfull, cfull, xv, sv, xm, xt, yb, hid, mk, edge, cntm, cnti,
        af, at, sec, slp, bn1, bn2, tsum, pool, lgt, dlm, dpd, dsb, da, dab, sr, es, er,
        du, dhp, acc, pacc, st1, st2, st3, st4,
        gcs, gcx, gcz, gcr, gps, gpx, gpz, gpr, dla, plt,
        ld_s, cw_s, cw_r, pw_s, pw_r, kw_s, kw_r, dl_s, dl_r, fx_s, fx_r, af_s, af_r, st_s, st_r,
        lg_s, lg_r, sr_s, sr_r, er_s, er_r, gc_s, gc_r, gp_s, gp_r,
    ) = refs
    nz = nd // 2
    c1 = c1l * nc
    nq = c2l // 128
    d = lax.axis_index("dp")
    c = lax.axis_index("chan")
    z, x = lax.div(d, 2), d % 2
    y, k = lax.div(c, 2), c % 2
    sib = y * 2 + 1 - k
    opp = (1 - y) * 2 + k
    dia = (1 - y) * 2 + 1 - k
    xdev = (z * 2 + 1 - x, c)
    sibdev = (d, sib)
    oppdev = (d, opp)

    def zdev(j):
        return (flip(z, j) * 2 + x, c)

    def remote(src, dst, ssem, rsem, dev):
        return pltpu.make_async_remote_copy(
            src_ref=src, dst_ref=dst, send_sem=ssem, recv_sem=rsem,
            device_id=dev, device_id_type=MESH,
        )

    def unit(buf, u, rows):
        return buf.at[pl.ds(pl.multiple_of(u * rows, rows), rows)]

    leftdev = ((z + nz - 1) % nz * 2 + x, c)
    rightdev = ((z + 1) % nz * 2 + x, c)
    has_left = lax.div(z + nz - 1, nz)
    has_right = 1 - lax.div(z + 1, nz)

    def gather_pieces(buf, rr, u):
        pieces = rr.shape[1]
        size = buf.shape[0] // (nd * pieces)
        for h in range(pieces):
            first = pl.multiple_of(u * (size * pieces) + h * size, size)
            yield buf.at[pl.ds(first, size)], rr.at[u, h]

    def gather_across(buf, ss, rr):
        for mine, arrived in gather_pieces(buf, rr, d):
            remote(mine, mine, ss.at[0], arrived, xdev).start()

    def gather_along(buf, ss, rr):
        for mine, arrived in gather_pieces(buf, rr, d):
            @pl.when(has_left > 0)
            def go_left():
                remote(mine, mine, ss.at[1], arrived, leftdev).start()

            @pl.when(has_right > 0)
            def go_right():
                remote(mine, mine, ss.at[2], arrived, rightdev).start()

    outer = 1 - has_left * has_right

    def gather_far(buf, ss, rr):
        if nz == 4:
            for mine, arrived in gather_pieces(buf, rr, d):
                @pl.when(outer > 0)
                def go_far():
                    remote(mine, mine, ss.at[3], arrived, zdev(3)).start()

    def gather_step(buf, ss, rr, j, relay=True):
        if j >= nz:
            return

        def pass_on(got, arrived, onward, i, dev):
            copy = remote(got, got, ss.at[0], arrived, xdev)
            copy.wait_recv()
            copy.start()

            if relay:
                @pl.when(onward > 0)
                def go_on():
                    remote(got, got, ss.at[i], arrived, dev).start()

        from_left = gather_pieces(buf, rr, (z + nz - j) % nz * 2 + x)
        from_right = gather_pieces(buf, rr, (z + j) % nz * 2 + x)
        for one, two in zip(from_left, from_right):
            @pl.when(z >= j)
            def left():
                pass_on(*one, has_right, 2, rightdev)

            @pl.when(z + j < nz)
            def right():
                pass_on(*two, has_left, 1, leftdev)

    def gather_finish(buf, ss, rr):
        for q in range(nz):
            for got, arrived in gather_pieces(buf, rr, q * 2 + 1 - x):
                remote(got, got, ss.at[0], arrived, xdev).wait_recv()

    def gather_drain(buf, ss, rr, far=False):
        def sent(i, units):
            some = buf.at[pl.ds(0, buf.shape[0] // nd * units)]
            remote(some, some, ss.at[i], rr.at[d, 0], xdev).wait_send()

        sent(0, nz)
        for q in range(nz):
            @pl.when(z == q)
            def mine(q=q):
                if q > 0:
                    sent(1, min(nz - q, 2) if far else nz - q)
                if q < nz - 1:
                    sent(2, min(q + 1, 2) if far else q + 1)
                if far and nz == 4 and q in (0, nz - 1):
                    sent(3, 1)

    def stats_send(buf, ss, rr):
        for p in reversed(range(1, nd)):
            remote(buf.at[0], buf.at[p], ss, rr, (flip(d, p), c)).start()

    def stats_wait(buf, ss, rr):
        got = buf.at[pl.ds(1, nd - 1)]
        remote(got, got, ss, rr, xdev).wait_recv()

    def stats_sum(buf):
        total = buf[d]
        for u in range(1, nd):
            total = total + buf[flip(d, u)]
        return total

    def stats_drain(buf, ss, rr):
        got = buf.at[pl.ds(1, nd - 1)]
        remote(got, got, ss, rr, xdev).wait_send()

    def rows(m):
        return pl.ds(pl.multiple_of(m * pm, pm), pm)

    def lanes(chunk):
        return pl.ds(pl.multiple_of(chunk * c1l, c1l), c1l)

    def part(buf, m, chunk):
        return buf.at[rows(m), lanes(chunk)]

    def local(src, dst, i):
        return pltpu.make_async_copy(src, dst, ld_s.at[i])

    loads = [
        local(wconv, wf, 0),
        local(wproj, pf, 1),
        local(wcls, cf, 2),
        local(feat, xv.at[:, lanes(c)], 3),
        local(short, sv, 4),
    ]
    for load in loads:
        load.start()

    barrier = pltpu.get_barrier_semaphore()
    for dev in (sibdev, oppdev, xdev):
        pl.semaphore_signal(barrier, inc=1, device_id=dev, device_id_type=MESH)

    @pl.when(has_left > 0)
    def greet_left():
        pl.semaphore_signal(barrier, inc=1, device_id=leftdev, device_id_type=MESH)

    @pl.when(has_right > 0)
    def greet_right():
        pl.semaphore_signal(barrier, inc=1, device_id=rightdev, device_id_type=MESH)

    loads[0].wait()
    wfull[pl.ds(pl.multiple_of(d * r1, r1), r1), :] = wf[...].astype(BF)
    pl.semaphore_wait(barrier, 3 + has_left + has_right)

    gather_across(wfull, cw_s, cw_r)
    gather_along(wfull, cw_s, cw_r)
    for m in range(MICRO):
        src = feat.at[pl.ds(m * pm, pm)]
        remote(src, part(xv, m, c), fx_s, fx_r.at[c, m], oppdev).start()
        remote(src, part(xv, m, c), fx_s, fx_r.at[c, m], sibdev).start()

    loads[1].wait()
    pfull[pl.ds(pl.multiple_of(d * rp, rp), rp), :] = pf[...].astype(BF)
    gather_across(pfull, pw_s, pw_r)
    loads[2].wait()
    cfull[pl.ds(pl.multiple_of(d * rc, rc), rc), :] = cf[...].astype(BF)

    pixel = row_iota((pm, 128))
    image = jnp.zeros((pm, 128), jnp.int32)
    for i in range(1, imb):
        image = image + (pixel >= AREA * i).astype(jnp.int32)
    pixel = pixel - AREA * image
    line = jnp.zeros((pm, 128), jnp.int32)
    for i in range(1, SIDE):
        line = line + (pixel >= SIDE * i).astype(jnp.int32)
    across = pixel - SIDE * line
    edge[0] = (line > 0).astype(F32)
    edge[1] = (line < SIDE - 1).astype(F32)
    edge[2] = (across > 0).astype(F32)
    edge[3] = (across < SIDE - 1).astype(F32)
    mask_bf = masks[...].astype(F32).astype(BF)
    images = imb * MICRO
    chosen = (pixel[:, :AREA] == lane_iota((pm, AREA))).astype(F32)
    ones = jnp.ones((AREA, 128), BF)
    image_count = jnp.sum(masks[...].astype(F32), axis=1, keepdims=True)
    for m in range(MICRO):
        away = row_iota((pm, images)) - AREA * (lane_iota((pm, images)) - imb * m)
        owner = jnp.where((away >= 0) & (away < AREA), 1.0, 0.0).astype(BF)
        spread = mm((mm(owner, mask_bf) * chosen).astype(BF), ones)
        mk[m] = spread
        cntm[m] = jnp.sum(spread, axis=0, keepdims=True)
        cnti[m] = jnp.broadcast_to(image_count[m * imb : (m + 1) * imb], (imb, 128))
        st1[m, 0, 2:3, :] = cntm[m]

    yb[:, 0:PAD, :] = jnp.zeros((9, PAD, c1l), F32)
    yb[:, PAD + pm :, :] = jnp.zeros((9, PAD, c1l), F32)
    dhp[0:PAD, :] = jnp.zeros((PAD, c1l), F32)
    dhp[PAD + pm :, :] = jnp.zeros((PAD, c1l), F32)

    def pass_features(m):
        got = part(xv, m, opp)
        copy = remote(got, got, fx_s, fx_r.at[opp, m], sibdev)
        copy.wait_recv()
        copy.start()

    def take_features(m, carry):
        for chunk in (sib, dia):
            got = part(xv, m, chunk)
            remote(got, got, fx_s, fx_r.at[chunk, m], sibdev).wait_recv()
        flat_mask = mk[m].astype(BF)
        for q in range(nc):
            piece = xv[rows(m), q * c1l : (q + 1) * c1l] * flat_mask
            xm[m, :, q * c1l : (q + 1) * c1l] = piece
            xt[m, q * c1l : (q + 1) * c1l, :] = piece.T
        return carry

    gather_step(wfull, cw_s, cw_r, 1)
    pass_features(0)
    gather_step(wfull, cw_s, cw_r, 2)
    gather_along(pfull, pw_s, pw_r)
    gather_far(pfull, pw_s, pw_r)
    pass_features(1)
    pass_features(2)
    loads[3].wait()
    gather_step(wfull, cw_s, cw_r, 3)
    gather_step(pfull, pw_s, pw_r, 1)
    pass_features(3)
    lax.fori_loop(0, MICRO, take_features, 0)
    gather_finish(wfull, cw_s, cw_r)

    def tap(t):
        return wfull[t * c1 : (t + 1) * c1, :]

    def edges(ky, kx):
        found = None
        if ky == 0:
            found = edge[0]
        if ky == 2:
            found = edge[1]
        if kx == 0:
            found = edge[2] if found is None else found * edge[2]
        if kx == 2:
            found = edge[3] if found is None else found * edge[3]
        return found

    def conv(m, carry):
        inputs = xm[m]
        for t in range(0, 9, 2):
            if t < 8:
                pair = mm(inputs, jnp.concatenate([tap(t), tap(t + 1)], axis=1))
                yb[t, PAD : PAD + pm, :] = pair[:, :c1l]
                yb[t + 1, PAD : PAD + pm, :] = pair[:, c1l:]
            else:
                yb[t, PAD : PAD + pm, :] = mm(inputs, tap(t))
        hidden = None
        for kx in range(3):
            column = None
            for ky in range(3):
                off = PAD + (ky - 1) * SIDE + kx - 1
                value = yb[3 * ky + kx, off : off + pm, :]
                if ky != 1:
                    value = value * edge[0 if ky == 0 else 1]
                column = value if column is None else column + value
            if kx != 1:
                column = column * edge[2 if kx == 0 else 3]
            hidden = column if hidden is None else hidden + column
        hid[m] = hidden
        valid = hidden * mk[m]
        st1[m, 0, 0:1, :] = jnp.sum(valid, axis=0, keepdims=True)
        st1[m, 0, 1:2, :] = jnp.sum(valid * hidden, axis=0, keepdims=True)
        stats_send(st1.at[m], st_s.at[0, m], st_r.at[0, m])

        @pl.when(m == 3)
        def bulk_3():
            gather_step(pfull, pw_s, pw_r, 3)
            gather_step(pfull, pw_s, pw_r, 2, False)

        return carry

    lax.fori_loop(0, MICRO, conv, 0)
    gather_along(cfull, kw_s, kw_r)
    gather_across(cfull, kw_s, kw_r)
    gather_far(cfull, kw_s, kw_r)
    acc[...] = jnp.zeros_like(acc)
    pacc[...] = jnp.zeros_like(pacc)

    def activate(m, carry):
        stats_wait(st1.at[m], st_s.at[0, m], st_r.at[0, m])
        totals = stats_sum(st1.at[m])
        n = totals[2:3]
        cntm[m] = n
        center = totals[0:1] / n
        bn1[m, 0:1, :] = center
        bn1[m, 1:2, :] = lax.rsqrt(totals[1:2] / n - center * center + norm_eps)
        normed = (hid[m] - bn1[m, 0:1, :]) * bn1[m, 1:2, :]
        shifted = n1[0:1, :] * normed + n1[1:2, :]
        active = (shifted * sigmoid(shifted) * mk[m]).astype(BF)
        mine = part(af, m, c)
        mine[...] = active
        remote(mine, mine, af_s, af_r.at[c, m], oppdev).start()
        remote(mine, mine, af_s, af_r.at[c, m], sibdev).start()
        return carry

    activate(0, 0)
    lax.fori_loop(1, MICRO, activate, 0)
    gather_step(cfull, kw_s, kw_r, 1)
    gather_step(cfull, kw_s, kw_r, 3)
    gather_finish(pfull, pw_s, pw_r)
    loads[4].wait()

    def turn(m, chunk):
        at[m, lanes_sub(chunk), :] = part(af, m, chunk)[...].T

    def lanes_sub(chunk):
        return pl.ds(pl.multiple_of(chunk * c1l, c1l), c1l)

    def stage_a(m):
        got = part(af, m, opp)
        copy = remote(got, got, af_s, af_r.at[opp, m], sibdev)
        copy.wait_recv()
        copy.start()
        turn(m, c)
        turn(m, opp)
        got = part(af, m, sib)
        remote(got, got, af_s, af_r.at[sib, m], sibdev).wait_recv()
        turn(m, sib)
        got = part(af, m, dia)
        remote(got, got, af_s, af_r.at[dia, m], sibdev).wait_recv()
        turn(m, dia)
        second = mm(af[rows(m), :], pfull[...])
        sec[m] = second
        mask = mk[m]
        for q in range(nq):
            piece = second[:, q * 128 : (q + 1) * 128]
            valid = piece * mask
            st2[m, 0, q : q + 1, :] = jnp.sum(valid, axis=0, keepdims=True)
            st2[m, 0, nq + q : nq + q + 1, :] = jnp.sum(valid * piece, axis=0, keepdims=True)
        stats_send(st2.at[m], st_s.at[1, m], st_r.at[1, m])

    low_half = row_iota((2, 8, 128)) * 0 + lax.broadcasted_iota(jnp.int32, (2, 8, 128), 1)
    tiles = AREA // 4
    half = tiles // 2

    def image_sums(value):
        value = value.reshape(imb // 2, tiles, 8, 128)
        middle = value[:, half]
        first = jnp.sum(value[:, :half], axis=1) + jnp.where(low_half < 4, middle, 0.0)
        last = jnp.sum(value[:, half + 1 :], axis=1) + jnp.where(low_half < 4, 0.0, middle)
        first = jnp.sum(first, axis=1)
        last = jnp.sum(last, axis=1)
        found = []
        for i in range(imb // 2):
            found += [first[i : i + 1], last[i : i + 1]]
        return jnp.concatenate(found, axis=0)

    def image_spread(value):
        pieces = []
        for i in range(imb // 2):
            first = jnp.broadcast_to(value[2 * i : 2 * i + 1], (8, 128))
            last = jnp.broadcast_to(value[2 * i + 1 : 2 * i + 2], (8, 128))
            middle = jnp.where(low_half[0] < 4, first, last)
            pieces.append(jnp.broadcast_to(first[None], (half, 8, 128)))
            pieces.append(middle[None])
            pieces.append(jnp.broadcast_to(last[None], (half, 8, 128)))
        return jnp.concatenate(pieces, axis=0).reshape(pm, 128)

    def stage_b(m):
        stats_wait(st2.at[m], st_s.at[1, m], st_r.at[1, m])
        total = stats_sum(st2.at[m])
        n = cntm[m]
        mask = mk[m]
        for q in range(nq):
            at_q = slice(q * 128, (q + 1) * 128)
            center = total[q : q + 1] / n
            spread = total[nq + q : nq + q + 1] / n - center * center
            scale = lax.rsqrt(spread + norm_eps)
            bn2[m, 0:1, at_q] = scale
            normed = (sec[m, :, at_q] - center) * scale
            sec[m, :, at_q] = normed
            summed = n2[0:1, at_q] * normed + n2[1:2, at_q]
            summed = summed + sv[rows(m), at_q].astype(F32)
            sigma = sigmoid(summed)
            slope = sigma * (1.0 + summed * (1.0 - sigma)) * mask
            slp[m, :, at_q] = slope
            pool[m, :, at_q] = (image_sums(summed * sigma * mask) / cnti[m]).astype(BF).astype(F32)
            tsum[m, 0, :, at_q] = image_sums(slope)
            tsum[m, 1, :, at_q] = image_sums(slope * normed)

    def stage_l(m):
        lgt[m, c] = mm(pool[m].astype(BF), cfull[...])
        for dev in (oppdev, (d, dia), sibdev):
            remote(lgt.at[m, c], lgt.at[m, c], lg_s, lg_r.at[m], dev).start()

    def stage_c(m):
        got = lgt.at[m, pl.ds(0, nc - 1)]
        remote(got, got, lg_s, lg_r.at[m], sibdev).wait_recv()
        logits = lgt[m, 0]
        for q in range(1, nc):
            logits = logits + lgt[m, q]
        logits = logits + cbias[...]
        top = jnp.max(logits, axis=1, keepdims=True)
        expo = jnp.exp(logits - top)
        expo_sum = jnp.sum(expo, axis=1, keepdims=True)
        image_row = row_iota((imb, classes))
        target = jnp.zeros((imb, classes), jnp.int32)
        for i in range(imb):
            target = jnp.where(image_row == i, labels[m * imb + i], target)
        onehot = (target == lane_iota((imb, classes))).astype(F32)
        picked = jnp.sum(logits * onehot, axis=1, keepdims=True)
        loss = jnp.sum(top + jnp.log(expo_sum) - picked, axis=0, keepdims=True)
        st4[m, 0, 2:3, :] = jnp.broadcast_to(loss, (1, 128))
        dlogits = ((expo / expo_sum - onehot) / total_images).astype(BF)
        dlm[m] = dlogits.astype(F32)
        spread = nt_dot(dlogits, cfull[...])
        for q in range(nq):
            at_q = slice(q * 128, (q + 1) * 128)
            value = spread[:, at_q] / cnti[m]
            dpd[m, :, at_q] = value
            st3[m, 0, q : q + 1, :] = jnp.sum(value * tsum[m, 0, :, at_q], axis=0, keepdims=True)
            st3[m, 0, nq + q : nq + q + 1, :] = jnp.sum(
                value * tsum[m, 1, :, at_q], axis=0, keepdims=True
            )
        stats_send(st3.at[m], st_s.at[2, m], st_r.at[2, m])

    def stage_d(m):
        stats_wait(st3.at[m], st_s.at[2, m], st_r.at[2, m])
        total = stats_sum(st3.at[m])
        n = cntm[m]
        mask = mk[m]
        for q in range(nq):
            at_q = slice(q * 128, (q + 1) * 128)
            gain = n2[0:1, at_q] * bn2[m, 0:1, at_q]
            base = gain * total[q : q + 1] / n
            ramp = gain * total[nq + q : nq + q + 1] / n
            value = image_spread(gain * dpd[m, :, at_q]) * slp[m, :, at_q]
            value = value - mask * (base + ramp * sec[m, :, at_q])
            dsb[:, at_q] = value.astype(BF)
        for q in range(nq):
            at_q = slice(q * 128, (q + 1) * 128)
            bn2[m, 1:2, at_q] = total[nq + q : nq + q + 1]
            bn2[m, 2:3, at_q] = total[q : q + 1]
        back = nt_dot(dsb[...], pfull[...])
        for q in range(nc):
            piece = back[:, q * c1l : (q + 1) * c1l]
            da[m, q % 2, q // 2] = piece
            dab[m, q % 2, q // 2] = piece.astype(BF)
        remote(dab.at[m, 1 - k], sr.at[m], sr_s, sr_r.at[m], sibdev).start()
        pacc[...] += mm(at[m], dsb[...])

    def stage_e(m):
        remote(sr.at[m], sr.at[m], sr_s, sr_r.at[m], sibdev).wait_recv()
        es[m] = (da[m, k, 1 - y] + sr[m, 1 - y].astype(F32)).astype(BF)
        remote(es.at[m], er.at[m], er_s, er_r.at[m], oppdev).start()

    def stage_f(m):
        remote(es.at[m], er.at[m], er_s, er_r.at[m], oppdev).wait_recv()
        upstream = da[m, k, y] + sr[m, y].astype(F32) + er[m].astype(F32)
        normed = (hid[m] - bn1[m, 0:1, :]) * bn1[m, 1:2, :]
        shifted = n1[0:1, :] * normed + n1[1:2, :]
        sigma = sigmoid(shifted)
        upstream = upstream * mk[m] * (sigma * (1.0 + shifted * (1.0 - sigma)))
        du[m] = upstream
        st4[m, 0, 0:1, :] = jnp.sum(upstream, axis=0, keepdims=True)
        st4[m, 0, 1:2, :] = jnp.sum(upstream * normed, axis=0, keepdims=True)
        stats_send(st4.at[m], st_s.at[3, m], st_r.at[3, m])

    def stage_g(m):
        stats_wait(st4.at[m], st_s.at[3, m], st_r.at[3, m])
        total = stats_sum(st4.at[m])
        n = cntm[m]
        bn1[m, 2:3, :] = total[1:2]
        bn1[m, 3:4, :] = total[0:1]
        bn1[m, 4:5, :] = total[2:3]
        normed = (hid[m] - bn1[m, 0:1, :]) * bn1[m, 1:2, :]
        gain = n1[0:1, :] * bn1[m, 1:2, :]
        value = mk[m] * gain * (du[m] - (total[0:1] + normed * total[1:2]) / n)
        dhp[PAD : PAD + pm, :] = value.astype(BF).astype(F32)

        def shifted(t):
            ky, kx = t // 3, t % 3
            off = PAD - (ky - 1) * SIDE - (kx - 1)
            piece = dhp[off : off + pm, :]
            found = edges(2 - ky, 2 - kx)
            return (piece if found is None else piece * found).astype(BF)

        left = xt[m]
        for t in range(0, 9, 2):
            if t < 8:
                pair = mm(left, jnp.concatenate([shifted(t), shifted(t + 1)], axis=1))
                acc[t * c1 : (t + 1) * c1, :] += pair[:, :c1l]
                acc[(t + 1) * c1 : (t + 2) * c1, :] += pair[:, c1l:]
            else:
                acc[t * c1 : (t + 1) * c1, :] += mm(left, shifted(t))

    orders = [2, 3, 1, 0] if nz == 4 else list(range(nz))

    def scatter_pieces(rr):
        return (rr.shape[0] - 4) // nz

    def scatter_start(total, sbuf, xbuf, ss, rr, js=orders):
        height = sbuf.shape[1]
        size = height // scatter_pieces(rr)
        for j in js:
            u = flip(z, j) * 2 + 1 - x
            for h in range(height // size):
                at_h = pl.ds(h * size, size)
                first = pl.multiple_of(u * height + h * size, size)
                sbuf[j, at_h] = total[pl.ds(first, size), :].astype(BF)
                remote(
                    sbuf.at[j, at_h], xbuf.at[j, at_h], ss.at[0],
                    rr.at[4 + j * (height // size) + h], xdev,
                ).start()

    def scatter_middle(total, xbuf, zbuf, rbuf, ss, rr, js, keep):
        height = xbuf.shape[1]
        pieces = scatter_pieces(rr)
        size = height // pieces
        for j in js:
            u = flip(z, j) * 2 + x
            for h in range(pieces):
                at_h = pl.ds(h * size, size)
                got = xbuf.at[j, at_h]
                remote(got, got, ss.at[0], rr.at[4 + j * pieces + h], xdev).wait_recv()
                first = pl.multiple_of(u * height + h * size, size)
                found = total[pl.ds(first, size), :] + got[...].astype(F32)
                if j == 0:
                    keep(h * size, found)
                    continue
                mine = zbuf.at[j, at_h]
                if j == 2:
                    mine[...] = found.astype(BF)

                    @pl.when(outer > 0)
                    def out_in():
                        to = rbuf.at[2, at_h]
                        remote(mine, to, ss.at[1], rr.at[2], zdev(1)).start()

                    @pl.when(outer == 0)
                    def in_in():
                        to = rbuf.at[0, at_h]
                        remote(mine, to, ss.at[1], rr.at[0], zdev(3)).start()

                    continue
                slot = 2 if j == 3 else 0

                @pl.when(outer > 0)
                def plain():
                    mine[...] = found.astype(BF)

                @pl.when(outer == 0)
                def added():
                    if h == 0:
                        relay = rbuf.at[slot]
                        remote(relay, relay, ss.at[1], rr.at[slot], xdev).wait_recv()
                    mine[...] = (found + rbuf[slot, at_h].astype(F32)).astype(BF)

                remote(mine, rbuf.at[j, at_h], ss.at[1], rr.at[j], zdev(j)).start()

    def scatter_wait(rbuf, ss, rr):
        if nz == 4:
            for j in (3, 1):
                remote(rbuf.at[j], rbuf.at[j], ss.at[1], rr.at[j], xdev).wait_recv()

    def scatter_drain(sbuf, zbuf, ss, rr):
        remote(sbuf, sbuf, ss.at[0], rr.at[0], xdev).wait_send()
        if nz > 1:
            sent = zbuf.at[pl.ds(1, nz - 1)]
            remote(sent, sent, ss.at[1], rr.at[0], xdev).wait_send()

    def cls_rows(u):
        return pl.ds(pl.multiple_of(u * images, images), images)

    wide = dla.shape[1] - c2l

    def share_cls():
        mine = jnp.concatenate([dlm[q] for q in range(MICRO)], axis=0).astype(BF)
        dla[cls_rows(d), 0:classes] = mine
        if wide > classes:
            dla[cls_rows(d), classes:wide] = jnp.zeros((images, wide - classes), BF)
        mine = jnp.concatenate([pool[q] for q in range(MICRO)], axis=0).astype(BF)
        dla[cls_rows(d), wide:] = mine
        gather_across(dla, dl_s, dl_r)
        gather_along(dla, dl_s, dl_r)

    def start_proj(j):
        if j < nz:
            scatter_start(pacc, gps, gpx, gp_s, gp_r, [j])

    def middle_proj(js):
        def keep(first, value):
            for q in range(nq):
                row = r1 + q * rp + first
                gout[row : row + value.shape[0], :] = value[:, q * 128 : (q + 1) * 128]

        scatter_middle(pacc, gpx, gpz, gpr, gp_s, gp_r, js, keep)

    def finish_cls():
        gather_finish(cfull, kw_s, kw_r)

    offsets = dict(a=0, b=2, l=3, c=5, d=8, e=9, f=12, g=14)
    stages = dict(
        a=stage_a, b=stage_b, l=stage_l, c=stage_c, d=stage_d, e=stage_e, f=stage_f, g=stage_g
    )
    def at_a0():
        gather_step(cfull, kw_s, kw_r, 2, False)

    hooks = {
        (0, "a"): at_a0,
        (3, "a"): finish_cls,
        (8, "c"): share_cls,
        (10, "d"): lambda: gather_step(dla, dl_s, dl_r, 1),
        (11, "d"): lambda: start_proj(2),
        (12, "e"): lambda: gather_step(dla, dl_s, dl_r, 2),
        (12, "f"): lambda: start_proj(3),
        (13, "f"): lambda: start_proj(1),
        (14, "g"): lambda: gather_step(dla, dl_s, dl_r, 3),
        (14, "f"): lambda: start_proj(0),
        (16, "g"): lambda: middle_proj(orders[:1]),
    }

    def step(s, carry):
        for name in "alcbedgf":
            i = offsets[name]

            @pl.when((s >= i) & (s < i + MICRO))
            def run(name=name, i=i):
                stages[name](s - i)

            for (when, after), hook in hooks.items():
                if after == name:

                    @pl.when(s == when)
                    def extra(hook=hook):
                        hook()

        return carry

    lax.fori_loop(0, MICRO + offsets["g"], step, 0)

    scatter_start(acc, gcs, gcx, gc_s, gc_r)
    middle_proj(orders[1:])

    gather_finish(dla, dl_s, dl_r)
    plt[...] = dla[:, wide:].T
    left = plt[pl.ds(pl.multiple_of(d * rc, rc), rc), :]
    row = r1 + nq * rp
    share = mm(left, dla[:, 0:wide])
    for q in range(wide // 128):
        gout[row + q * rc : row + (q + 1) * rc, :] = share[:, q * 128 : (q + 1) * 128]
    row = row + wide // 128 * rc
    share = jnp.sum(dla[:, 0:wide].astype(F32), axis=0, keepdims=True)
    for q in range(wide // 128):
        gout[row + q : row + q + 1, :] = share[:, q * 128 : (q + 1) * 128]
    row = row + wide // 128
    share = bn2[0, 1:3, :] + bn2[1, 1:3, :] + bn2[2, 1:3, :] + bn2[3, 1:3, :]
    for q in range(nq):
        gout[row + 2 * q : row + 2 * q + 2, :] = share[:, q * 128 : (q + 1) * 128]
    row = row + 2 * nq
    gout[row : row + 2, :] = bn1[0, 2:4, :] + bn1[1, 2:4, :] + bn1[2, 2:4, :] + bn1[3, 2:4, :]
    loss = bn1[0, 4:5, :] + bn1[1, 4:5, :] + bn1[2, 4:5, :] + bn1[3, 4:5, :]
    gout[row + 2 : row + 3, :] = loss / total_images
    def keep_conv(first, value):
        gout[first : first + value.shape[0], :] = value

    def middle_conv(js):
        scatter_middle(acc, gcx, gcz, gcr, gc_s, gc_r, js, keep_conv)

    middle_conv(orders[:1])
    scatter_wait(gpr, gp_s, gp_r)
    if nz == 4:
        for q in range(nq):
            at_q = slice(q * 128, (q + 1) * 128)
            share = gpr[1, :, at_q].astype(F32) + gpr[3, :, at_q].astype(F32)
            gout[r1 + q * rp : r1 + (q + 1) * rp, :] += share
    middle_conv(orders[1:])
    scatter_wait(gcr, gc_s, gc_r)
    if nz == 4:
        gout[0:r1, :] += gcr[1].astype(F32) + gcr[3].astype(F32)

    gather_drain(wfull, cw_s, cw_r)
    gather_drain(pfull, pw_s, pw_r, True)
    gather_drain(cfull, kw_s, kw_r, True)
    gather_drain(dla, dl_s, dl_r)
    scatter_drain(gps, gpz, gp_s, gp_r)
    scatter_drain(gcs, gcz, gc_s, gc_r)
    sent = xv.at[:, pl.ds(0, 3 * c1l)]
    remote(sent, sent, fx_s, fx_r.at[0, 0], sibdev).wait_send()
    sent = af.at[:, pl.ds(0, 3 * c1l)]
    remote(sent, sent, af_s, af_r.at[0, 0], sibdev).wait_send()
    sent = lgt.at[pl.ds(0, nc - 1)]
    remote(sent, sent, lg_s, lg_r.at[0], sibdev).wait_send()
    remote(sr, sr, sr_s, sr_r.at[0], sibdev).wait_send()
    remote(es, es, er_s, er_r.at[0], oppdev).wait_send()

    def drain(m, carry):
        for i, buf in enumerate((st1, st2, st3, st4)):
            stats_drain(buf.at[m], st_s.at[i, m], st_r.at[i, m])
        return carry

    lax.fori_loop(0, MICRO, drain, 0)


def fused_gradients(
    features, shortcut, valid_masks, labels, w_conv, w_proj, w_cls, cls_bias, norm_one, norm_two
):
    nd, nc = lax.axis_size("dp"), lax.axis_size("chan")
    nz = nd // 2
    pixels, c1l = features.shape
    c2l = shortcut.shape[1]
    images = valid_masks.shape[0]
    imb, pm = images // MICRO, pixels // MICRO
    r1, rp, rc = w_conv.shape[0], w_proj.shape[0], w_cls.shape[0]
    classes = w_cls.shape[1]
    c1 = c1l * nc
    nq = c2l // 128
    wide = -(-classes // 128) * 128
    grad_rows = r1 + nq * rp + wide // 128 * (rc + 1) + 2 * nq + 3
    grad_rows = -(-grad_rows // 8) * 8
    dims = (nd, nc, pm, imb, c1l, c2l, r1, rp, rc, classes, images * nd)
    vmem = pltpu.VMEM
    dma = pltpu.SemaphoreType.DMA
    m4 = MICRO
    scratch = [
        vmem((r1, c1l), F32), vmem((rp, c2l), F32), vmem((rc, classes), F32),
        vmem((9 * c1, c1l), BF), vmem((c1, c2l), BF), vmem((c2l, classes), BF),
        vmem((pixels, c1), BF), vmem((pixels, c2l), BF),
        vmem((m4, pm, c1), BF), vmem((m4, c1, pm), BF),
        vmem((9, PAD + pm + PAD, c1l), F32), vmem((m4, pm, c1l), F32), vmem((m4, pm, 128), F32),
        vmem((4, pm, 128), F32), vmem((m4, 1, 128), F32), vmem((m4, imb, 128), F32),
        vmem((pixels, c1), BF), vmem((m4, c1, pm), BF),
        vmem((m4, pm, c2l), F32), vmem((m4, pm, c2l), F32),
        vmem((m4, 8, c1l), F32), vmem((m4, 8, c2l), F32),
        vmem((m4, 2, imb, c2l), F32), vmem((m4, imb, c2l), F32),
        vmem((m4, nc, imb, classes), F32), vmem((m4, imb, classes), F32), vmem((m4, imb, c2l), F32),
        vmem((pm, c2l), BF), vmem((m4, 2, 2, pm, c1l), F32), vmem((m4, 2, 2, pm, c1l), BF),
        vmem((m4, 2, pm, c1l), BF), vmem((m4, pm, c1l), BF), vmem((m4, pm, c1l), BF),
        vmem((m4, pm, c1l), F32), vmem((PAD + pm + PAD, c1l), F32),
        vmem((9 * c1, c1l), F32), vmem((c1, c2l), F32),
        vmem((m4, nd, 8, c1l), F32),
        vmem((m4, nd, 2 * nq, 128), F32), vmem((m4, nd, 2 * nq, 128), F32),
        vmem((m4, nd, 8, c1l), F32),
        vmem((nz, r1, c1l), BF), vmem((nz, r1, c1l), BF),
        vmem((nz, r1, c1l), BF), vmem((nz, r1, c1l), BF),
        vmem((nz, rp, c2l), BF), vmem((nz, rp, c2l), BF),
        vmem((nz, rp, c2l), BF), vmem((nz, rp, c2l), BF),
        vmem((nd * images, wide + c2l), BF), vmem((c2l, nd * images), BF),
        dma((5,)),
        dma((4,)), dma((nd, 3)), dma((4,)), dma((nd, 1)), dma((4,)), dma((nd, 2)),
        dma((4,)), dma((nd, 1)),
        dma, dma((nc, m4)), dma, dma((nc, m4)), dma((4, m4)), dma((4, m4)),
        dma, dma((m4,)), dma, dma((m4,)), dma, dma((m4,)),
        dma((2,)), dma((4 + 4 * nz,)), dma((2,)), dma((4 + nz,)),
    ]
    whole = pl.BlockSpec(memory_space=pltpu.VMEM)
    hbm = pl.BlockSpec(memory_space=pl.ANY)
    scalar = pl.BlockSpec(memory_space=pltpu.SMEM)
    shape = jax.ShapeDtypeStruct
    return pl.pallas_call(
        functools.partial(fused_kernel, dims),
        out_shape=shape((grad_rows, 128), F32),
        in_specs=[hbm, hbm, whole, scalar, hbm, hbm, hbm, whole, whole, whole],
        out_specs=whole,
        scratch_shapes=scratch,
        compiler_params=pltpu.CompilerParams(
            collective_id=0, has_side_effects=True, vmem_limit_bytes=58 * 1024 * 1024
        ),
    )(
        features, shortcut, valid_masks, labels, w_conv, w_proj, w_cls,
        cls_bias.reshape(1, classes), norm_one, norm_two,
    )


def adam_kernel(grads, *refs):
    states, outs = refs[:18], refs[18:]
    row = 0
    for i, (rate, decay) in enumerate(ADAM_RATES):
        weight, moment, second = states[3 * i : 3 * i + 3]
        height, width = weight.shape
        for start in range(0, width, 128):
            size = min(128, width - start)
            at_q = slice(start, start + size)
            found = adam_step(
                weight[:, at_q], moment[:, at_q], second[:, at_q],
                grads[row : row + height, 0:size], rate, decay,
            )
            row += height
            for out, value in zip(outs[3 * i : 3 * i + 3], found):
                out[:, at_q] = value
            if i < 3:
                outs[18 + i][:, at_q] = found[0].astype(BF)
    outs[21][...] = grads[row : row + 1, :]


ADAM_RATES = (
    (rate_matrix, weight_decay),
    (rate_matrix, weight_decay),
    (rate_matrix, weight_decay),
    (rate_small, 0.0),
    (rate_small, 0.0),
    (rate_small, 0.0),
)


def fused_device(
    features, shortcut, valid_masks, labels, w_conv, w_proj, w_cls, cls_bias, norm_one, norm_two,
    conv_moment, conv_second, proj_moment, proj_second, cls_moment, cls_second,
    bias_moment, bias_second, one_moment, one_second, two_moment, two_second,
):
    grads = fused_gradients(
        features, shortcut, valid_masks, labels, w_conv, w_proj, w_cls, cls_bias, norm_one, norm_two
    )
    states = (
        (w_conv, conv_moment, conv_second),
        (w_proj, proj_moment, proj_second),
        (w_cls, cls_moment, cls_second),
        (cls_bias.reshape(1, -1), bias_moment.reshape(1, -1), bias_second.reshape(1, -1)),
        (norm_two, two_moment, two_second),
        (norm_one, one_moment, one_second),
    )
    operands, outs = [], []
    for state in states:
        operands += list(state)
        outs += [jax.ShapeDtypeStruct(state[0].shape, F32)] * 3
    outs += [jax.ShapeDtypeStruct(state[0].shape, BF) for state in states[:3]]
    outs.append(jax.ShapeDtypeStruct((1, 128), F32))
    whole = pl.BlockSpec(memory_space=pltpu.VMEM)
    done = list(
        pl.pallas_call(
            adam_kernel,
            out_shape=tuple(outs),
            in_specs=[whole] * (len(operands) + 1),
            out_specs=(whole,) * len(outs),
            compiler_params=pltpu.CompilerParams(vmem_limit_bytes=40 * 1024 * 1024),
        )(grads, *operands)
    )
    biases = [done[i].reshape(-1) for i in (9, 10, 11)]
    return tuple(done[:9] + biases + done[15:18] + done[12:15] + done[18:21]) + (done[21][0, 0],)


def run_device(*args):
    features, shortcut, valid_masks = args[:3]
    w_cls = args[6]
    fits = (
        lax.axis_size("chan") == 4
        and lax.axis_size("dp") in (2, 8)
        and features.shape[1] == 128
        and shortcut.shape[1] % 128 == 0
        and w_cls.shape[0] % 16 == 0
        and valid_masks.shape[0] % (4 * MICRO) == 0
    )
    return (fused_device if fits else per_device)(*args)


def solution(mesh):
    placed = (
        P("dp", "chan"),
        P("dp", "chan"),
        P("dp", None),
        P("dp"),
        P("dp", "chan"),
        P("dp", "chan"),
        P(("chan", "dp"), None),
        P(),
        P(None, "chan"),
        P(None, "chan"),
        P("dp", "chan"),
        P("dp", "chan"),
        P("dp", "chan"),
        P("dp", "chan"),
        P(("chan", "dp"), None),
        P(("chan", "dp"), None),
        P(),
        P(),
        P(None, "chan"),
        P(None, "chan"),
        P(None, "chan"),
        P(None, "chan"),
    )
    return jax.shard_map(
        run_device,
        mesh=mesh,
        in_specs=placed,
        out_specs=(
            P("dp", "chan"),
            P("dp", "chan"),
            P("dp", "chan"),
            P("dp", "chan"),
            P("dp", "chan"),
            P("dp", "chan"),
            P(("chan", "dp"), None),
            P(("chan", "dp"), None),
            P(("chan", "dp"), None),
            P(),
            P(),
            P(),
            P(None, "chan"),
            P(None, "chan"),
            P(None, "chan"),
            P(None, "chan"),
            P(None, "chan"),
            P(None, "chan"),
            P("dp", "chan"),
            P("dp", "chan"),
            P(("chan", "dp"), None),
            P(),
        ),
        check_vma=False,
    )
```

```python
import functools

import jax
import jax.numpy as jnp
from jax import lax
from jax.experimental import pallas as pl
from jax.experimental.pallas import tpu as pltpu
from jax.sharding import PartitionSpec as P

SIDE = 10
MICRO = 4
STEP = 3


norm_eps = 1e-05
adam_eps = 1e-08
beta_decay = 0.5
rate_matrix = 0.02
rate_small = 0.5
weight_decay = 0.01


def tap_columns(flat, images):
    width = flat.shape[1]
    grid = flat.reshape(images, SIDE, SIDE, width)
    padded = jnp.pad(grid, ((0, 0), (1, 1), (1, 1), (0, 0)))
    pieces = [
        padded[:, down : down + SIDE, across : across + SIDE, :]
        for down in range(3)
        for across in range(3)
    ]
    return jnp.concatenate(pieces, axis=3).reshape(images * SIDE * SIDE, 9 * width)


def silu_slope(value):
    sigma = jax.nn.sigmoid(value)
    return sigma * (1.0 + value * (1.0 - sigma))


def norm_forward(hidden, weights, params):
    sums, squares, count = lax.psum(
        (
            jnp.sum(hidden * weights, axis=1),
            jnp.sum(hidden * hidden * weights, axis=1),
            jnp.sum(weights, axis=1),
        ),
        "dp",
    )
    center = sums / count
    scale = lax.rsqrt(squares / count - center * center + norm_eps)
    normed = (hidden - center[:, None]) * scale[:, None]
    return (params[0] * normed + params[1], normed, scale[:, None], count[:, None])


def norm_backward(upstream, normed, scale, count, weights, params):
    total, along = lax.psum((jnp.sum(upstream, axis=1), jnp.sum(upstream * normed, axis=1)), "dp")
    grad = (
        weights
        * params[0]
        * scale
        * (upstream - (total[:, None] + normed * along[:, None]) / count)
    )
    return (grad, jnp.stack([jnp.sum(along, axis=0), jnp.sum(total, axis=0)]))


def contract_rows(left, right):
    return lax.dot_general(
        left, right, (((0,), (0,)), ((), ())), preferred_element_type=jnp.float32
    )


def contract_cols(left, right):
    return lax.dot_general(
        left, right, (((1,), (1,)), ((), ())), preferred_element_type=jnp.float32
    )


def adam_step(weight, moment, second, grad, rate, decay):
    moment = beta_decay * moment + (1.0 - beta_decay) * grad
    second = beta_decay * second + (1.0 - beta_decay) * grad * grad
    correct = 1.0 - beta_decay**STEP
    weight = weight - rate * (
        moment / correct / (jnp.sqrt(second / correct) + adam_eps) + decay * weight
    )
    return (weight, moment, second)


def per_device(
    features,
    shortcut,
    valid_masks,
    labels,
    w_conv,
    w_proj,
    w_cls,
    cls_bias,
    norm_one,
    norm_two,
    conv_moment,
    conv_second,
    proj_moment,
    proj_second,
    cls_moment,
    cls_second,
    bias_moment,
    bias_second,
    one_moment,
    one_second,
    two_moment,
    two_second,
):
    images = valid_masks.shape[0]
    area = SIDE * SIDE
    pixels = images * area
    total_images = images * lax.axis_size("dp")
    classes = w_cls.shape[1]
    conv_full, proj_full, cls_full = (
        lax.all_gather(w_conv.astype(jnp.bfloat16), "dp", axis=0, tiled=True),
        lax.all_gather(w_proj.astype(jnp.bfloat16), "dp", axis=0, tiled=True),
        lax.all_gather(w_cls.astype(jnp.bfloat16), "dp", axis=0, tiled=True),
    )

    def split(flat):
        return flat.reshape((MICRO, -1) + flat.shape[1:])

    def join(parts):
        return parts.reshape((-1,) + parts.shape[2:])

    image_mask = valid_masks.astype(jnp.float32)
    pixel_counts = jnp.sum(image_mask, axis=1)
    weights = split(image_mask.reshape(pixels, 1))
    masked = features * join(weights).astype(jnp.bfloat16)
    gathered = lax.all_gather(masked, "chan", axis=1, tiled=True)
    columns = tap_columns(gathered, images)
    hidden = jnp.dot(columns, conv_full, preferred_element_type=jnp.float32)
    shifted, normed_one, scale_one, count = norm_forward(split(hidden), weights, norm_one)
    active = join((jax.nn.silu(shifted) * weights).astype(jnp.bfloat16))
    active_full = lax.all_gather(active, "chan", axis=1, tiled=True)
    second = jnp.dot(active_full, proj_full, preferred_element_type=jnp.float32)
    shifted_two, normed_two, scale_two, _ = norm_forward(split(second), weights, norm_two)
    summed = shifted_two + split(shortcut.astype(jnp.float32))
    output = jax.nn.silu(summed) * weights
    channels = shortcut.shape[1]
    pooled = (
        jnp.sum(output.reshape(images, area, channels), axis=1) / pixel_counts[:, None]
    ).astype(jnp.bfloat16)
    partial_value = jnp.dot(pooled, cls_full, preferred_element_type=jnp.float32)
    logits = lax.psum(partial_value, "chan") + cls_bias
    top = jnp.max(logits, axis=1, keepdims=True)
    expo = jnp.exp(logits - top)
    expo_sum = jnp.sum(expo, axis=1, keepdims=True)
    onehot = (labels[:, None] == jnp.arange(classes)[None, :]).astype(jnp.float32)
    picked = jnp.sum(logits * onehot, axis=1)
    loss_sum = jnp.sum(top[:, 0] + jnp.log(expo_sum[:, 0]) - picked)
    dlogits = ((expo / expo_sum - onehot) / total_images).astype(jnp.bfloat16)
    grad_bias = jnp.sum(dlogits.astype(jnp.float32), axis=0)
    local_cls = contract_rows(pooled, dlogits)
    grad_pool = contract_cols(dlogits, cls_full)
    spread_back = jnp.broadcast_to(
        (grad_pool / pixel_counts[:, None])[:, None, :], (images, area, channels)
    ).reshape(MICRO, -1, channels)
    upstream_two = spread_back * weights * silu_slope(summed)
    grad_second, grad_two = norm_backward(
        upstream_two, normed_two, scale_two, count, weights, norm_two
    )
    grad_second = join(grad_second.astype(jnp.bfloat16))
    local_proj = contract_rows(active_full, grad_second)
    partial_act = contract_cols(grad_second, proj_full)
    grad_active = lax.psum_scatter(
        partial_act.astype(jnp.bfloat16), "chan", scatter_dimension=1, tiled=True
    ).astype(jnp.float32)
    upstream_one = split(grad_active) * weights * silu_slope(shifted)
    grad_hidden, grad_one = norm_backward(
        upstream_one, normed_one, scale_one, count, weights, norm_one
    )
    local_conv = contract_rows(columns, join(grad_hidden.astype(jnp.bfloat16)))
    sum_conv, sum_proj, sum_cls = (
        lax.psum_scatter(
            local_conv.astype(jnp.bfloat16), "dp", scatter_dimension=0, tiled=True
        ).astype(jnp.float32),
        lax.psum_scatter(
            local_proj.astype(jnp.bfloat16), "dp", scatter_dimension=0, tiled=True
        ).astype(jnp.float32),
        lax.psum_scatter(
            local_cls.astype(jnp.bfloat16), "dp", scatter_dimension=0, tiled=True
        ).astype(jnp.float32),
    )
    loss_total, bias_total = lax.psum((loss_sum, grad_bias), "dp")
    train_loss = loss_total / total_images
    conv_w, conv_m, conv_v = adam_step(
        w_conv, conv_moment, conv_second, sum_conv, rate_matrix, weight_decay
    )
    proj_w, proj_m, proj_v = adam_step(
        w_proj, proj_moment, proj_second, sum_proj, rate_matrix, weight_decay
    )
    cls_w, cls_m, cls_v = adam_step(
        w_cls, cls_moment, cls_second, sum_cls, rate_matrix, weight_decay
    )
    bias_w, bias_m, bias_v = adam_step(
        cls_bias, bias_moment, bias_second, bias_total, rate_small, 0.0
    )
    one_w, one_m, one_v = adam_step(norm_one, one_moment, one_second, grad_one, rate_small, 0.0)
    two_w, two_m, two_v = adam_step(norm_two, two_moment, two_second, grad_two, rate_small, 0.0)
    return (
        conv_w,
        conv_m,
        conv_v,
        proj_w,
        proj_m,
        proj_v,
        cls_w,
        cls_m,
        cls_v,
        bias_w,
        bias_m,
        bias_v,
        one_w,
        one_m,
        one_v,
        two_w,
        two_m,
        two_v,
        conv_w.astype(jnp.bfloat16),
        proj_w.astype(jnp.bfloat16),
        cls_w.astype(jnp.bfloat16),
        train_loss,
    )


MESH = pl.DeviceIdType.MESH
AREA = SIDE * SIDE
PAD = 16
BF = jnp.bfloat16
F32 = jnp.float32


def flip(value, bits):
    bit = 1
    while bit <= bits:
        if bits & bit:
            value = value + bit - 2 * bit * (lax.div(value, bit) % 2)
        bit *= 2
    return value


def nt_dot(left, right):
    return lax.dot_general(left, right, (((1,), (1,)), ((), ())), preferred_element_type=F32)


def mm(left, right):
    return jnp.dot(left, right, preferred_element_type=F32)


def sigmoid(value):
    return 1.0 / (1.0 + jnp.exp(-value))


def row_iota(shape):
    return lax.broadcasted_iota(jnp.int32, shape, 0)


def lane_iota(shape):
    return lax.broadcasted_iota(jnp.int32, shape, 1)


def fused_kernel(dims, *refs):
    nd, nc, pm, imb, c1l, c2l, r1, rp, rc, classes, total_images = dims
    (
        feat, short, masks_in, labels, wconv, wproj, wcls, cbias_in, n1_in, n2_in, gout,
        masks, cbias, n1, n2, wf, pf, cf, wfull, pfull, cfull, xv, sv, xm, xt, yb, hid, mk, edge, cntm, cnti,
        af, at, sec, slp, bn1, bn2, tsum, pool, lgt, dlm, dpd, dsb, da, dab, sr, es, er,
        du, dhp, acc, pacc, st1, st2, st3, st4,
        gcs, gcx, gcz, gcr, gps, gpx, gpz, gpr, dla, plt,
        ld_s, cw_s, cw_r, pw_s, pw_r, kw_s, kw_r, dl_s, dl_r, fx_s, fx_r, af_s, af_r, st_s, st_r,
        lg_s, lg_r, sr_s, sr_r, er_s, er_r, gc_s, gc_r, gp_s, gp_r,
    ) = refs
    nz = nd // 2
    c1 = c1l * nc
    nq = c2l // 128
    d = lax.axis_index("dp")
    c = lax.axis_index("chan")
    z, x = lax.div(d, 2), d % 2
    y, k = lax.div(c, 2), c % 2
    sib = y * 2 + 1 - k
    opp = (1 - y) * 2 + k
    dia = (1 - y) * 2 + 1 - k
    xdev = (z * 2 + 1 - x, c)
    sibdev = (d, sib)
    oppdev = (d, opp)

    def zdev(j):
        return (flip(z, j) * 2 + x, c)

    def remote(src, dst, ssem, rsem, dev):
        return pltpu.make_async_remote_copy(
            src_ref=src, dst_ref=dst, send_sem=ssem, recv_sem=rsem,
            device_id=dev, device_id_type=MESH,
        )

    def unit(buf, u, rows):
        return buf.at[pl.ds(pl.multiple_of(u * rows, rows), rows)]

    leftdev = ((z + nz - 1) % nz * 2 + x, c)
    rightdev = ((z + 1) % nz * 2 + x, c)
    has_left = lax.div(z + nz - 1, nz)
    has_right = 1 - lax.div(z + 1, nz)

    def gather_pieces(buf, rr, u):
        pieces = rr.shape[1]
        size = buf.shape[0] // (nd * pieces)
        for h in range(pieces):
            first = pl.multiple_of(u * (size * pieces) + h * size, size)
            yield buf.at[pl.ds(first, size)], rr.at[lax.div(u, 2), h]

    def gather_across(buf, ss, rr):
        for mine, _ in gather_pieces(buf, rr, d):
            remote(mine, mine, ss.at[0], rr.at[nz, 0], xdev).start()

    def gather_along(buf, ss, rr):
        for mine, arrived in gather_pieces(buf, rr, d):
            @pl.when(has_left > 0)
            def go_left():
                remote(mine, mine, ss.at[1], arrived, leftdev).start()

            @pl.when(has_right > 0)
            def go_right():
                remote(mine, mine, ss.at[2], arrived, rightdev).start()

    outer = 1 - has_left * has_right

    def gather_far(buf, ss, rr):
        if nz == 4:
            for mine, arrived in gather_pieces(buf, rr, d):
                @pl.when(outer > 0)
                def go_far():
                    remote(mine, mine, ss.at[3], arrived, zdev(3)).start()

    def gather_step(buf, ss, rr, j, relay=True):
        if j >= nz:
            return

        def pass_on(got, arrived, onward, i, dev):
            remote(got, got, ss.at[0], arrived, xdev).wait_recv()
            remote(got, got, ss.at[0], rr.at[nz, 0], xdev).start()

            if relay:
                @pl.when(onward > 0)
                def go_on():
                    remote(got, got, ss.at[i], arrived, dev).start()

        from_left = gather_pieces(buf, rr, (z + nz - j) % nz * 2 + x)
        from_right = gather_pieces(buf, rr, (z + j) % nz * 2 + x)
        for one, two in zip(from_left, from_right):
            @pl.when(z >= j)
            def left():
                pass_on(*one, has_right, 2, rightdev)

            @pl.when(z + j < nz)
            def right():
                pass_on(*two, has_left, 1, leftdev)

    def gather_finish(buf, ss, rr):
        got = buf.at[pl.ds(0, buf.shape[0] // 2)]
        remote(got, got, ss.at[0], rr.at[nz, 0], xdev).wait_recv()

    def gather_drain(buf, ss, rr, far=False):
        def sent(i, units):
            some = buf.at[pl.ds(0, buf.shape[0] // nd * units)]
            remote(some, some, ss.at[i], rr.at[nz, 0], xdev).wait_send()

        sent(0, nz)
        for q in range(nz):
            @pl.when(z == q)
            def mine(q=q):
                if q > 0:
                    sent(1, min(nz - q, 2) if far else nz - q)
                if q < nz - 1:
                    sent(2, min(q + 1, 2) if far else q + 1)
                if far and nz == 4 and q in (0, nz - 1):
                    sent(3, 1)

    def stats_send(buf, ss, rr):
        for p in reversed(range(1, nd)):
            remote(buf.at[0], buf.at[p], ss, rr, (flip(d, p), c)).start()

    def stats_wait(buf, ss, rr):
        got = buf.at[pl.ds(1, nd - 1)]
        remote(got, got, ss, rr, xdev).wait_recv()

    def stats_sum(buf):
        total = buf[d]
        for u in range(1, nd):
            total = total + buf[flip(d, u)]
        return total

    def stats_drain(buf, ss, rr):
        sent = buf.at[:, pl.ds(1, nd - 1)]
        remote(sent, sent, ss, rr, xdev).wait_send()

    def rows(m):
        return pl.ds(pl.multiple_of(m * pm, pm), pm)

    def lanes(chunk):
        return pl.ds(pl.multiple_of(chunk * c1l, c1l), c1l)

    def part(buf, m, chunk):
        return buf.at[rows(m), lanes(chunk)]

    def local(src, dst, i):
        return pltpu.make_async_copy(src, dst, ld_s.at[i])

    loads = [
        local(wconv, wf, 0),
        local(wproj, pf, 1),
        local(wcls, cf, 2),
        local(feat, xv.at[:, lanes(c)], 3),
        local(short, sv, 4),
        local(masks_in, masks, 5),
        local(cbias_in, cbias, 6),
        local(n1_in, n1, 7),
        local(n2_in, n2, 8),
    ]
    loads[0].start()

    barrier = pltpu.get_barrier_semaphore()
    for dev in (sibdev, oppdev, xdev):
        pl.semaphore_signal(barrier, inc=1, device_id=dev, device_id_type=MESH)

    @pl.when(has_left > 0)
    def greet_left():
        pl.semaphore_signal(barrier, inc=1, device_id=leftdev, device_id_type=MESH)

    @pl.when(has_right > 0)
    def greet_right():
        pl.semaphore_signal(barrier, inc=1, device_id=rightdev, device_id_type=MESH)

    for i in (1, 2, 5, 3, 4, 6, 7, 8):
        loads[i].start()
    loads[0].wait()
    wfull[pl.ds(pl.multiple_of(d * r1, r1), r1), :] = wf[...].astype(BF)
    pl.semaphore_wait(barrier, 3 + has_left + has_right)

    gather_across(wfull, cw_s, cw_r)
    gather_along(wfull, cw_s, cw_r)
    for m in range(MICRO):
        src = feat.at[pl.ds(m * pm, pm)]
        remote(src, part(xv, m, c), fx_s, fx_r.at[0, m], oppdev).start()
        remote(src, part(xv, m, c), fx_s, fx_r.at[1, m], sibdev).start()

    loads[1].wait()
    pfull[pl.ds(pl.multiple_of(d * rp, rp), rp), :] = pf[...].astype(BF)
    gather_across(pfull, pw_s, pw_r)
    loads[2].wait()
    cfull[pl.ds(pl.multiple_of(d * rc, rc), rc), :] = cf[...].astype(BF)

    pixel = row_iota((pm, 128))
    image = jnp.zeros((pm, 128), jnp.int32)
    for i in range(1, imb):
        image = image + (pixel >= AREA * i).astype(jnp.int32)
    pixel = pixel - AREA * image
    line = jnp.zeros((pm, 128), jnp.int32)
    for i in range(1, SIDE):
        line = line + (pixel >= SIDE * i).astype(jnp.int32)
    across = pixel - SIDE * line
    edge[0] = (line > 0).astype(F32)
    edge[1] = (line < SIDE - 1).astype(F32)
    edge[2] = (across > 0).astype(F32)
    edge[3] = (across < SIDE - 1).astype(F32)
    loads[5].wait()
    mask_bf = masks[...].astype(F32).astype(BF)
    images = imb * MICRO
    chosen = (pixel[:, :AREA] == lane_iota((pm, AREA))).astype(F32)
    ones = jnp.ones((AREA, 128), BF)
    image_count = jnp.sum(masks[...].astype(F32), axis=1, keepdims=True)
    for m in range(MICRO):
        away = row_iota((pm, images)) - AREA * (lane_iota((pm, images)) - imb * m)
        owner = jnp.where((away >= 0) & (away < AREA), 1.0, 0.0).astype(BF)
        spread = mm((mm(owner, mask_bf) * chosen).astype(BF), ones)
        mk[m] = spread
        cntm[m] = jnp.sum(spread, axis=0, keepdims=True)
        cnti[m] = jnp.broadcast_to(image_count[m * imb : (m + 1) * imb], (imb, 128))
        st1[m, 0, 2:3, :] = cntm[m]

    yb[:, 0:PAD, :] = jnp.zeros((9, PAD, c1l), F32)
    yb[:, PAD + pm :, :] = jnp.zeros((9, PAD, c1l), F32)
    dhp[0:PAD, :] = jnp.zeros((PAD, c1l), F32)
    dhp[PAD + pm :, :] = jnp.zeros((PAD, c1l), F32)

    def pass_features(m):
        got = part(xv, m, opp)
        remote(got, got, fx_s, fx_r.at[0, m], sibdev).wait_recv()
        remote(got, got, fx_s, fx_r.at[1, m], sibdev).start()

    def take_features(m, carry):
        got = xv.at[rows(m), pl.ds(0, 2 * c1l)]
        remote(got, got, fx_s, fx_r.at[1, m], sibdev).wait_recv()
        flat_mask = mk[m].astype(BF)
        for q in range(nc):
            piece = xv[rows(m), q * c1l : (q + 1) * c1l] * flat_mask
            xm[m, :, q * c1l : (q + 1) * c1l] = piece
            xt[m, q * c1l : (q + 1) * c1l, :] = piece.T
        return carry

    gather_step(wfull, cw_s, cw_r, 1)
    pass_features(0)
    gather_step(wfull, cw_s, cw_r, 2)
    gather_along(pfull, pw_s, pw_r)
    gather_far(pfull, pw_s, pw_r)
    pass_features(1)
    pass_features(2)
    loads[3].wait()
    loads[7].wait()
    gather_step(wfull, cw_s, cw_r, 3)
    gather_step(pfull, pw_s, pw_r, 1)
    pass_features(3)
    lax.fori_loop(0, MICRO, take_features, 0)
    gather_finish(wfull, cw_s, cw_r)

    def tap(t):
        return wfull[t * c1 : (t + 1) * c1, :]

    def edges(ky, kx):
        found = None
        if ky == 0:
            found = edge[0]
        if ky == 2:
            found = edge[1]
        if kx == 0:
            found = edge[2] if found is None else found * edge[2]
        if kx == 2:
            found = edge[3] if found is None else found * edge[3]
        return found

    def conv(m, carry):
        inputs = xm[m]
        for t in range(0, 9, 2):
            if t < 8:
                pair = mm(inputs, jnp.concatenate([tap(t), tap(t + 1)], axis=1))
                yb[t, PAD : PAD + pm, :] = pair[:, :c1l]
                yb[t + 1, PAD : PAD + pm, :] = pair[:, c1l:]
            else:
                yb[t, PAD : PAD + pm, :] = mm(inputs, tap(t))
        hidden = None
        for kx in range(3):
            column = None
            for ky in range(3):
                off = PAD + (ky - 1) * SIDE + kx - 1
                value = yb[3 * ky + kx, off : off + pm, :]
                if ky != 1:
                    value = value * edge[0 if ky == 0 else 1]
                column = value if column is None else column + value
            if kx != 1:
                column = column * edge[2 if kx == 0 else 3]
            hidden = column if hidden is None else hidden + column
        hid[m] = hidden
        valid = hidden * mk[m]
        st1[m, 0, 0:1, :] = jnp.sum(valid, axis=0, keepdims=True)
        st1[m, 0, 1:2, :] = jnp.sum(valid * hidden, axis=0, keepdims=True)
        stats_send(st1.at[m], st_s.at[0], st_r.at[0, m])

        @pl.when(m == 2)
        def bulk_at_2():
            gather_step(pfull, pw_s, pw_r, 3)
            gather_step(pfull, pw_s, pw_r, 2, False)

        @pl.when(m == 3)
        def bulk_at_3():
            gather_along(cfull, kw_s, kw_r)
            gather_across(cfull, kw_s, kw_r)
            gather_far(cfull, kw_s, kw_r)

        return carry

    lax.fori_loop(0, MICRO, conv, 0)
    acc[...] = jnp.zeros_like(acc)
    pacc[...] = jnp.zeros_like(pacc)

    def activate(m, carry):
        stats_wait(st1.at[m], st_s.at[0], st_r.at[0, m])
        totals = stats_sum(st1.at[m])
        n = totals[2:3]
        cntm[m] = n
        center = totals[0:1] / n
        bn1[m, 0:1, :] = center
        bn1[m, 1:2, :] = lax.rsqrt(totals[1:2] / n - center * center + norm_eps)
        normed = (hid[m] - bn1[m, 0:1, :]) * bn1[m, 1:2, :]
        shifted = n1[0:1, :] * normed + n1[1:2, :]
        active = (shifted * sigmoid(shifted) * mk[m]).astype(BF)
        mine = part(af, m, c)
        mine[...] = active
        remote(mine, mine, af_s, af_r.at[0, m], oppdev).start()
        remote(mine, mine, af_s, af_r.at[1, m], sibdev).start()
        return carry

    activate(0, 0)
    lax.fori_loop(1, MICRO, activate, 0)
    gather_step(cfull, kw_s, kw_r, 1)
    gather_step(cfull, kw_s, kw_r, 3)
    gather_finish(pfull, pw_s, pw_r)
    loads[4].wait()
    loads[6].wait()
    loads[8].wait()

    def turn(m, chunk):
        at[m, lanes_sub(chunk), :] = part(af, m, chunk)[...].T

    def lanes_sub(chunk):
        return pl.ds(pl.multiple_of(chunk * c1l, c1l), c1l)

    def stage_a(m):
        got = part(af, m, opp)
        remote(got, got, af_s, af_r.at[0, m], sibdev).wait_recv()
        remote(got, got, af_s, af_r.at[1, m], sibdev).start()
        turn(m, c)
        turn(m, opp)
        got = af.at[rows(m), pl.ds(0, 2 * c1l)]
        remote(got, got, af_s, af_r.at[1, m], sibdev).wait_recv()
        turn(m, sib)
        turn(m, dia)
        second = mm(af[rows(m), :], pfull[...])
        sec[m] = second
        mask = mk[m]
        for q in range(nq):
            piece = second[:, q * 128 : (q + 1) * 128]
            valid = piece * mask
            st2[m, 0, q : q + 1, :] = jnp.sum(valid, axis=0, keepdims=True)
            st2[m, 0, nq + q : nq + q + 1, :] = jnp.sum(valid * piece, axis=0, keepdims=True)
        stats_send(st2.at[m], st_s.at[1], st_r.at[1, m])

    low_half = row_iota((2, 8, 128)) * 0 + lax.broadcasted_iota(jnp.int32, (2, 8, 128), 1)
    tiles = AREA // 4
    half = tiles // 2

    def image_sums(value):
        value = value.reshape(imb // 2, tiles, 8, 128)
        middle = value[:, half]
        first = jnp.sum(value[:, :half], axis=1) + jnp.where(low_half < 4, middle, 0.0)
        last = jnp.sum(value[:, half + 1 :], axis=1) + jnp.where(low_half < 4, 0.0, middle)
        first = jnp.sum(first, axis=1)
        last = jnp.sum(last, axis=1)
        found = []
        for i in range(imb // 2):
            found += [first[i : i + 1], last[i : i + 1]]
        return jnp.concatenate(found, axis=0)

    def image_spread(value):
        pieces = []
        for i in range(imb // 2):
            first = jnp.broadcast_to(value[2 * i : 2 * i + 1], (8, 128))
            last = jnp.broadcast_to(value[2 * i + 1 : 2 * i + 2], (8, 128))
            middle = jnp.where(low_half[0] < 4, first, last)
            pieces.append(jnp.broadcast_to(first[None], (half, 8, 128)))
            pieces.append(middle[None])
            pieces.append(jnp.broadcast_to(last[None], (half, 8, 128)))
        return jnp.concatenate(pieces, axis=0).reshape(pm, 128)

    def stage_b(m):
        stats_wait(st2.at[m], st_s.at[1], st_r.at[1, m])
        total = stats_sum(st2.at[m])
        n = cntm[m]
        mask = mk[m]
        for q in range(nq):
            at_q = slice(q * 128, (q + 1) * 128)
            center = total[q : q + 1] / n
            spread = total[nq + q : nq + q + 1] / n - center * center
            scale = lax.rsqrt(spread + norm_eps)
            bn2[m, 0:1, at_q] = scale
            normed = (sec[m, :, at_q] - center) * scale
            sec[m, :, at_q] = normed
            summed = n2[0:1, at_q] * normed + n2[1:2, at_q]
            summed = summed + sv[rows(m), at_q].astype(F32)
            sigma = sigmoid(summed)
            slope = sigma * (1.0 + summed * (1.0 - sigma)) * mask
            slp[m, :, at_q] = slope
            pool[m, :, at_q] = (image_sums(summed * sigma * mask) / cnti[m]).astype(BF).astype(F32)
            tsum[m, 0, :, at_q] = image_sums(slope)
            tsum[m, 1, :, at_q] = image_sums(slope * normed)

    def stage_l(m):
        lgt[m, c] = mm(pool[m].astype(BF), cfull[...])
        for dev in (oppdev, (d, dia), sibdev):
            remote(lgt.at[m, c], lgt.at[m, c], lg_s, lg_r.at[m], dev).start()

    def stage_c(m):
        got = lgt.at[m, pl.ds(0, nc - 1)]
        remote(got, got, lg_s, lg_r.at[m], sibdev).wait_recv()
        logits = lgt[m, 0]
        for q in range(1, nc):
            logits = logits + lgt[m, q]
        logits = logits + cbias[...]
        top = jnp.max(logits, axis=1, keepdims=True)
        expo = jnp.exp(logits - top)
        expo_sum = jnp.sum(expo, axis=1, keepdims=True)
        image_row = row_iota((imb, classes))
        target = jnp.zeros((imb, classes), jnp.int32)
        for i in range(imb):
            target = jnp.where(image_row == i, labels[m * imb + i], target)
        onehot = (target == lane_iota((imb, classes))).astype(F32)
        picked = jnp.sum(logits * onehot, axis=1, keepdims=True)
        loss = jnp.sum(top + jnp.log(expo_sum) - picked, axis=0, keepdims=True)
        st4[m, 0, 2:3, :] = jnp.broadcast_to(loss, (1, 128))
        dlogits = ((expo / expo_sum - onehot) / total_images).astype(BF)
        dlm[m] = dlogits.astype(F32)
        spread = nt_dot(dlogits, cfull[...])
        for q in range(nq):
            at_q = slice(q * 128, (q + 1) * 128)
            value = spread[:, at_q] / cnti[m]
            dpd[m, :, at_q] = value
            st3[m, 0, q : q + 1, :] = jnp.sum(value * tsum[m, 0, :, at_q], axis=0, keepdims=True)
            st3[m, 0, nq + q : nq + q + 1, :] = jnp.sum(
                value * tsum[m, 1, :, at_q], axis=0, keepdims=True
            )
        stats_send(st3.at[m], st_s.at[2], st_r.at[2, m])

    def stage_d(m):
        stats_wait(st3.at[m], st_s.at[2], st_r.at[2, m])
        total = stats_sum(st3.at[m])
        n = cntm[m]
        mask = mk[m]
        for q in range(nq):
            at_q = slice(q * 128, (q + 1) * 128)
            gain = n2[0:1, at_q] * bn2[m, 0:1, at_q]
            base = gain * total[q : q + 1] / n
            ramp = gain * total[nq + q : nq + q + 1] / n
            value = image_spread(gain * dpd[m, :, at_q]) * slp[m, :, at_q]
            value = value - mask * (base + ramp * sec[m, :, at_q])
            dsb[:, at_q] = value.astype(BF)
        for q in range(nq):
            at_q = slice(q * 128, (q + 1) * 128)
            bn2[m, 1:2, at_q] = total[nq + q : nq + q + 1]
            bn2[m, 2:3, at_q] = total[q : q + 1]
        back = nt_dot(dsb[...], pfull[...])
        for q in range(nc):
            piece = back[:, q * c1l : (q + 1) * c1l]
            da[m, q % 2, q // 2] = piece
            dab[m, q % 2, q // 2] = piece.astype(BF)
        remote(dab.at[m, 1 - k], sr.at[m], sr_s, sr_r.at[m], sibdev).start()
        pacc[...] += mm(at[m], dsb[...])

    def stage_e(m):
        remote(sr.at[m], sr.at[m], sr_s, sr_r.at[m], sibdev).wait_recv()
        es[m] = (da[m, k, 1 - y] + sr[m, 1 - y].astype(F32)).astype(BF)
        remote(es.at[m], er.at[m], er_s, er_r.at[m], oppdev).start()

    def stage_f(m):
        remote(es.at[m], er.at[m], er_s, er_r.at[m], oppdev).wait_recv()
        upstream = da[m, k, y] + sr[m, y].astype(F32) + er[m].astype(F32)
        normed = (hid[m] - bn1[m, 0:1, :]) * bn1[m, 1:2, :]
        shifted = n1[0:1, :] * normed + n1[1:2, :]
        sigma = sigmoid(shifted)
        upstream = upstream * mk[m] * (sigma * (1.0 + shifted * (1.0 - sigma)))
        du[m] = upstream
        st4[m, 0, 0:1, :] = jnp.sum(upstream, axis=0, keepdims=True)
        st4[m, 0, 1:2, :] = jnp.sum(upstream * normed, axis=0, keepdims=True)
        stats_send(st4.at[m], st_s.at[3], st_r.at[3, m])

    def stage_g(m):
        stats_wait(st4.at[m], st_s.at[3], st_r.at[3, m])
        total = stats_sum(st4.at[m])
        n = cntm[m]
        bn1[m, 2:3, :] = total[1:2]
        bn1[m, 3:4, :] = total[0:1]
        bn1[m, 4:5, :] = total[2:3]
        normed = (hid[m] - bn1[m, 0:1, :]) * bn1[m, 1:2, :]
        gain = n1[0:1, :] * bn1[m, 1:2, :]
        value = mk[m] * gain * (du[m] - (total[0:1] + normed * total[1:2]) / n)
        dhp[PAD : PAD + pm, :] = value.astype(BF).astype(F32)

        def shifted(t):
            ky, kx = t // 3, t % 3
            off = PAD - (ky - 1) * SIDE - (kx - 1)
            piece = dhp[off : off + pm, :]
            found = edges(2 - ky, 2 - kx)
            return (piece if found is None else piece * found).astype(BF)

        left = xt[m]
        for t in range(0, 9, 2):
            if t < 8:
                pair = mm(left, jnp.concatenate([shifted(t), shifted(t + 1)], axis=1))
                acc[t * c1 : (t + 1) * c1, :] += pair[:, :c1l]
                acc[(t + 1) * c1 : (t + 2) * c1, :] += pair[:, c1l:]
            else:
                acc[t * c1 : (t + 1) * c1, :] += mm(left, shifted(t))

    orders = [2, 3, 1, 0] if nz == 4 else list(range(nz))

    def scatter_pieces(rr):
        return (rr.shape[0] - 4) // nz

    def scatter_start(total, sbuf, xbuf, ss, rr, js=orders):
        height = sbuf.shape[1]
        size = height // scatter_pieces(rr)
        for j in js:
            u = flip(z, j) * 2 + 1 - x
            for h in range(height // size):
                at_h = pl.ds(h * size, size)
                first = pl.multiple_of(u * height + h * size, size)
                sbuf[j, at_h] = total[pl.ds(first, size), :].astype(BF)
                remote(
                    sbuf.at[j, at_h], xbuf.at[j, at_h], ss.at[0],
                    rr.at[4 + j * (height // size) + h], xdev,
                ).start()

    def scatter_middle(total, xbuf, zbuf, rbuf, ss, rr, js, keep):
        height = xbuf.shape[1]
        pieces = scatter_pieces(rr)
        size = height // pieces
        for j in js:
            u = flip(z, j) * 2 + x
            for h in range(pieces):
                at_h = pl.ds(h * size, size)
                got = xbuf.at[j, at_h]
                remote(got, got, ss.at[0], rr.at[4 + j * pieces + h], xdev).wait_recv()
                first = pl.multiple_of(u * height + h * size, size)
                found = total[pl.ds(first, size), :] + got[...].astype(F32)
                if j == 0:
                    keep(h * size, found)
                    continue
                mine = zbuf.at[j, at_h]
                if j == 2:
                    mine[...] = found.astype(BF)

                    @pl.when(outer > 0)
                    def out_in():
                        to = rbuf.at[2, at_h]
                        remote(mine, to, ss.at[1], rr.at[2], zdev(1)).start()

                    @pl.when(outer == 0)
                    def in_in():
                        to = rbuf.at[0, at_h]
                        remote(mine, to, ss.at[1], rr.at[0], zdev(3)).start()

                    continue
                slot = 2 if j == 3 else 0

                @pl.when(outer > 0)
                def plain():
                    mine[...] = found.astype(BF)

                @pl.when(outer == 0)
                def added():
                    if h == 0:
                        relay = rbuf.at[slot]
                        remote(relay, relay, ss.at[1], rr.at[slot], xdev).wait_recv()
                    mine[...] = (found + rbuf[slot, at_h].astype(F32)).astype(BF)

                remote(mine, rbuf.at[j, at_h], ss.at[1], rr.at[j], zdev(j)).start()

    def scatter_wait(rbuf, ss, rr):
        if nz == 4:
            for j in (3, 1):
                remote(rbuf.at[j], rbuf.at[j], ss.at[1], rr.at[j], xdev).wait_recv()

    def scatter_drain(sbuf, zbuf, ss, rr):
        remote(sbuf, sbuf, ss.at[0], rr.at[0], xdev).wait_send()
        if nz > 1:
            sent = zbuf.at[pl.ds(1, nz - 1)]
            remote(sent, sent, ss.at[1], rr.at[0], xdev).wait_send()

    def cls_rows(u):
        return pl.ds(pl.multiple_of(u * images, images), images)

    wide = dla.shape[1] - c2l

    def share_cls():
        mine = jnp.concatenate([dlm[q] for q in range(MICRO)], axis=0).astype(BF)
        dla[cls_rows(d), 0:classes] = mine
        if wide > classes:
            dla[cls_rows(d), classes:wide] = jnp.zeros((images, wide - classes), BF)
        mine = jnp.concatenate([pool[q] for q in range(MICRO)], axis=0).astype(BF)
        dla[cls_rows(d), wide:] = mine
        gather_across(dla, dl_s, dl_r)
        gather_along(dla, dl_s, dl_r)

    def start_proj(j):
        if j < nz:
            scatter_start(pacc, gps, gpx, gp_s, gp_r, [j])

    def middle_proj(js):
        def keep(first, value):
            for q in range(nq):
                row = r1 + q * rp + first
                gout[row : row + value.shape[0], :] = value[:, q * 128 : (q + 1) * 128]

        scatter_middle(pacc, gpx, gpz, gpr, gp_s, gp_r, js, keep)

    def finish_cls():
        gather_finish(cfull, kw_s, kw_r)

    offsets = dict(a=0, b=2, l=3, c=5, d=8, e=9, f=11, g=13)
    stages = dict(
        a=stage_a, b=stage_b, l=stage_l, c=stage_c, d=stage_d, e=stage_e, f=stage_f, g=stage_g
    )
    def at_a0():
        gather_step(cfull, kw_s, kw_r, 2, False)

    hooks = {
        (0, "a"): at_a0,
        (3, "a"): finish_cls,
        (8, "c"): share_cls,
        (10, "d"): lambda: gather_step(dla, dl_s, dl_r, 1),
        (11, "f"): lambda: start_proj(2),
        (12, "e"): lambda: gather_step(dla, dl_s, dl_r, 2),
        (12, "f"): lambda: start_proj(3),
        (13, "f"): lambda: start_proj(1),
        (14, "g"): lambda: gather_step(dla, dl_s, dl_r, 3),
        (14, "f"): lambda: start_proj(0),
        (16, "b"): lambda: middle_proj(orders[:1]),
    }

    def step(s, carry):
        for name in "alcbedfg":
            i = offsets[name]

            @pl.when((s >= i) & (s < i + MICRO))
            def run(name=name, i=i):
                stages[name](s - i)

            for (when, after), hook in hooks.items():
                if after == name:

                    @pl.when(s == when)
                    def extra(hook=hook):
                        hook()

        return carry

    lax.fori_loop(0, MICRO + offsets["g"], step, 0)

    scatter_start(acc, gcs, gcx, gc_s, gc_r)
    middle_proj(orders[1:])

    gather_finish(dla, dl_s, dl_r)
    plt[...] = dla[:, wide:].T
    left = plt[pl.ds(pl.multiple_of(d * rc, rc), rc), :]
    row = r1 + nq * rp
    share = mm(left, dla[:, 0:wide])
    for q in range(wide // 128):
        gout[row + q * rc : row + (q + 1) * rc, :] = share[:, q * 128 : (q + 1) * 128]
    row = row + wide // 128 * rc
    share = jnp.sum(dla[:, 0:wide].astype(F32), axis=0, keepdims=True)
    for q in range(wide // 128):
        gout[row + q : row + q + 1, :] = share[:, q * 128 : (q + 1) * 128]
    row = row + wide // 128
    share = bn2[0, 1:3, :] + bn2[1, 1:3, :] + bn2[2, 1:3, :] + bn2[3, 1:3, :]
    for q in range(nq):
        gout[row + 2 * q : row + 2 * q + 2, :] = share[:, q * 128 : (q + 1) * 128]
    row = row + 2 * nq
    gout[row : row + 2, :] = bn1[0, 2:4, :] + bn1[1, 2:4, :] + bn1[2, 2:4, :] + bn1[3, 2:4, :]
    loss = bn1[0, 4:5, :] + bn1[1, 4:5, :] + bn1[2, 4:5, :] + bn1[3, 4:5, :]
    gout[row + 2 : row + 3, :] = loss / total_images
    def keep_conv(first, value):
        gout[first : first + value.shape[0], :] = value

    def middle_conv(js):
        scatter_middle(acc, gcx, gcz, gcr, gc_s, gc_r, js, keep_conv)

    middle_conv(orders[:1])
    scatter_wait(gpr, gp_s, gp_r)
    if nz == 4:
        for q in range(nq):
            at_q = slice(q * 128, (q + 1) * 128)
            share = gpr[1, :, at_q].astype(F32) + gpr[3, :, at_q].astype(F32)
            gout[r1 + q * rp : r1 + (q + 1) * rp, :] += share
    middle_conv(orders[1:])
    scatter_wait(gcr, gc_s, gc_r)
    if nz == 4:
        gout[0:r1, :] += gcr[1].astype(F32) + gcr[3].astype(F32)

    gather_drain(wfull, cw_s, cw_r)
    gather_drain(pfull, pw_s, pw_r, True)
    gather_drain(cfull, kw_s, kw_r, True)
    gather_drain(dla, dl_s, dl_r)
    scatter_drain(gps, gpz, gp_s, gp_r)
    scatter_drain(gcs, gcz, gc_s, gc_r)
    sent = xv.at[:, pl.ds(0, 3 * c1l)]
    remote(sent, sent, fx_s, fx_r.at[0, 0], sibdev).wait_send()
    sent = af.at[:, pl.ds(0, 3 * c1l)]
    remote(sent, sent, af_s, af_r.at[0, 0], sibdev).wait_send()
    sent = lgt.at[pl.ds(0, nc - 1)]
    remote(sent, sent, lg_s, lg_r.at[0], sibdev).wait_send()
    remote(sr, sr, sr_s, sr_r.at[0], sibdev).wait_send()
    remote(es, es, er_s, er_r.at[0], oppdev).wait_send()

    for i, buf in enumerate((st1, st2, st3, st4)):
        stats_drain(buf, st_s.at[i], st_r.at[i, 0])


def fused_gradients(
    features, shortcut, valid_masks, labels, w_conv, w_proj, w_cls, cls_bias, norm_one, norm_two
):
    nd, nc = lax.axis_size("dp"), lax.axis_size("chan")
    nz = nd // 2
    pixels, c1l = features.shape
    c2l = shortcut.shape[1]
    images = valid_masks.shape[0]
    imb, pm = images // MICRO, pixels // MICRO
    r1, rp, rc = w_conv.shape[0], w_proj.shape[0], w_cls.shape[0]
    classes = w_cls.shape[1]
    c1 = c1l * nc
    nq = c2l // 128
    wide = -(-classes // 128) * 128
    grad_rows = r1 + nq * rp + wide // 128 * (rc + 1) + 2 * nq + 3
    grad_rows = -(-grad_rows // 8) * 8
    dims = (nd, nc, pm, imb, c1l, c2l, r1, rp, rc, classes, images * nd)
    vmem = pltpu.VMEM
    dma = pltpu.SemaphoreType.DMA
    m4 = MICRO
    scratch = [
        vmem((images, SIDE * SIDE), jnp.int32), vmem((1, classes), F32),
        vmem((2, c1l), F32), vmem((2, c2l), F32),
        vmem((r1, c1l), F32), vmem((rp, c2l), F32), vmem((rc, classes), F32),
        vmem((9 * c1, c1l), BF), vmem((c1, c2l), BF), vmem((c2l, classes), BF),
        vmem((pixels, c1), BF), vmem((pixels, c2l), BF),
        vmem((m4, pm, c1), BF), vmem((m4, c1, pm), BF),
        vmem((9, PAD + pm + PAD, c1l), F32), vmem((m4, pm, c1l), F32), vmem((m4, pm, 128), F32),
        vmem((4, pm, 128), F32), vmem((m4, 1, 128), F32), vmem((m4, imb, 128), F32),
        vmem((pixels, c1), BF), vmem((m4, c1, pm), BF),
        vmem((m4, pm, c2l), F32), vmem((m4, pm, c2l), F32),
        vmem((m4, 8, c1l), F32), vmem((m4, 8, c2l), F32),
        vmem((m4, 2, imb, c2l), F32), vmem((m4, imb, c2l), F32),
        vmem((m4, nc, imb, classes), F32), vmem((m4, imb, classes), F32), vmem((m4, imb, c2l), F32),
        vmem((pm, c2l), BF), vmem((m4, 2, 2, pm, c1l), F32), vmem((m4, 2, 2, pm, c1l), BF),
        vmem((m4, 2, pm, c1l), BF), vmem((m4, pm, c1l), BF), vmem((m4, pm, c1l), BF),
        vmem((m4, pm, c1l), F32), vmem((PAD + pm + PAD, c1l), F32),
        vmem((9 * c1, c1l), F32), vmem((c1, c2l), F32),
        vmem((m4, nd, 8, c1l), F32),
        vmem((m4, nd, 2 * nq, 128), F32), vmem((m4, nd, 2 * nq, 128), F32),
        vmem((m4, nd, 8, c1l), F32),
        vmem((nz, r1, c1l), BF), vmem((nz, r1, c1l), BF),
        vmem((nz, r1, c1l), BF), vmem((nz, r1, c1l), BF),
        vmem((nz, rp, c2l), BF), vmem((nz, rp, c2l), BF),
        vmem((nz, rp, c2l), BF), vmem((nz, rp, c2l), BF),
        vmem((nd * images, wide + c2l), BF), vmem((c2l, nd * images), BF),
        dma((9,)),
        dma((4,)), dma((nz + 1, 3)), dma((4,)), dma((nz + 1, 1)), dma((4,)), dma((nz + 1, 2)),
        dma((4,)), dma((nz + 1, 1)),
        dma, dma((2, m4)), dma, dma((2, m4)), dma((4,)), dma((4, m4)),
        dma, dma((m4,)), dma, dma((m4,)), dma, dma((m4,)),
        dma((2,)), dma((4 + 4 * nz,)), dma((2,)), dma((4 + nz,)),
    ]
    whole = pl.BlockSpec(memory_space=pltpu.VMEM)
    hbm = pl.BlockSpec(memory_space=pl.ANY)
    scalar = pl.BlockSpec(memory_space=pltpu.SMEM)
    shape = jax.ShapeDtypeStruct
    return pl.pallas_call(
        functools.partial(fused_kernel, dims),
        out_shape=shape((grad_rows, 128), F32),
        in_specs=[hbm, hbm, hbm, scalar, hbm, hbm, hbm, hbm, hbm, hbm],
        out_specs=whole,
        scratch_shapes=scratch,
        compiler_params=pltpu.CompilerParams(
            collective_id=0, has_side_effects=True, vmem_limit_bytes=58 * 1024 * 1024
        ),
    )(
        features, shortcut, valid_masks, labels, w_conv, w_proj, w_cls,
        cls_bias.reshape(1, classes), norm_one, norm_two,
    )


def adam_kernel(grads, *refs):
    states, outs = refs[:18], refs[18:]
    row = 0
    for i, (rate, decay) in enumerate(ADAM_RATES):
        weight, moment, second = states[3 * i : 3 * i + 3]
        height, width = weight.shape
        for start in range(0, width, 128):
            size = min(128, width - start)
            at_q = slice(start, start + size)
            found = adam_step(
                weight[:, at_q], moment[:, at_q], second[:, at_q],
                grads[row : row + height, 0:size], rate, decay,
            )
            row += height
            for out, value in zip(outs[3 * i : 3 * i + 3], found):
                out[:, at_q] = value
            if i < 3:
                outs[18 + i][:, at_q] = found[0].astype(BF)
    outs[21][...] = grads[row : row + 1, :]


ADAM_RATES = (
    (rate_matrix, weight_decay),
    (rate_matrix, weight_decay),
    (rate_matrix, weight_decay),
    (rate_small, 0.0),
    (rate_small, 0.0),
    (rate_small, 0.0),
)


def fused_device(
    features, shortcut, valid_masks, labels, w_conv, w_proj, w_cls, cls_bias, norm_one, norm_two,
    conv_moment, conv_second, proj_moment, proj_second, cls_moment, cls_second,
    bias_moment, bias_second, one_moment, one_second, two_moment, two_second,
):
    grads = fused_gradients(
        features, shortcut, valid_masks, labels, w_conv, w_proj, w_cls, cls_bias, norm_one, norm_two
    )
    states = (
        (w_conv, conv_moment, conv_second),
        (w_proj, proj_moment, proj_second),
        (w_cls, cls_moment, cls_second),
        (cls_bias.reshape(1, -1), bias_moment.reshape(1, -1), bias_second.reshape(1, -1)),
        (norm_two, two_moment, two_second),
        (norm_one, one_moment, one_second),
    )
    operands, outs = [], []
    for state in states:
        operands += list(state)
        outs += [jax.ShapeDtypeStruct(state[0].shape, F32)] * 3
    outs += [jax.ShapeDtypeStruct(state[0].shape, BF) for state in states[:3]]
    outs.append(jax.ShapeDtypeStruct((1, 128), F32))
    whole = pl.BlockSpec(memory_space=pltpu.VMEM)
    done = list(
        pl.pallas_call(
            adam_kernel,
            out_shape=tuple(outs),
            in_specs=[whole] * (len(operands) + 1),
            out_specs=(whole,) * len(outs),
            compiler_params=pltpu.CompilerParams(vmem_limit_bytes=40 * 1024 * 1024),
        )(grads, *operands)
    )
    biases = [done[i].reshape(-1) for i in (9, 10, 11)]
    return tuple(done[:9] + biases + done[15:18] + done[12:15] + done[18:21]) + (done[21][0, 0],)


def run_device(*args):
    features, shortcut, valid_masks = args[:3]
    w_cls = args[6]
    fits = (
        lax.axis_size("chan") == 4
        and lax.axis_size("dp") in (2, 8)
        and features.shape[1] == 128
        and shortcut.shape[1] % 128 == 0
        and w_cls.shape[0] % 16 == 0
        and valid_masks.shape[0] % (4 * MICRO) == 0
    )
    return (fused_device if fits else per_device)(*args)


def solution(mesh):
    placed = (
        P("dp", "chan"),
        P("dp", "chan"),
        P("dp", None),
        P("dp"),
        P("dp", "chan"),
        P("dp", "chan"),
        P(("chan", "dp"), None),
        P(),
        P(None, "chan"),
        P(None, "chan"),
        P("dp", "chan"),
        P("dp", "chan"),
        P("dp", "chan"),
        P("dp", "chan"),
        P(("chan", "dp"), None),
        P(("chan", "dp"), None),
        P(),
        P(),
        P(None, "chan"),
        P(None, "chan"),
        P(None, "chan"),
        P(None, "chan"),
    )
    return jax.shard_map(
        run_device,
        mesh=mesh,
        in_specs=placed,
        out_specs=(
            P("dp", "chan"),
            P("dp", "chan"),
            P("dp", "chan"),
            P("dp", "chan"),
            P("dp", "chan"),
            P("dp", "chan"),
            P(("chan", "dp"), None),
            P(("chan", "dp"), None),
            P(("chan", "dp"), None),
            P(),
            P(),
            P(),
            P(None, "chan"),
            P(None, "chan"),
            P(None, "chan"),
            P(None, "chan"),
            P(None, "chan"),
            P(None, "chan"),
            P("dp", "chan"),
            P("dp", "chan"),
            P(("chan", "dp"), None),
            P(),
        ),
        check_vma=False,
    )
```

```python
import functools

import jax
import jax.numpy as jnp
from jax import lax
from jax.experimental import pallas as pl
from jax.experimental.pallas import tpu as pltpu
from jax.sharding import PartitionSpec as P

SIDE = 10
MICRO = 4
STEP = 3


norm_eps = 1e-05
adam_eps = 1e-08
beta_decay = 0.5
rate_matrix = 0.02
rate_small = 0.5
weight_decay = 0.01


def tap_columns(flat, images):
    width = flat.shape[1]
    grid = flat.reshape(images, SIDE, SIDE, width)
    padded = jnp.pad(grid, ((0, 0), (1, 1), (1, 1), (0, 0)))
    pieces = [
        padded[:, down : down + SIDE, across : across + SIDE, :]
        for down in range(3)
        for across in range(3)
    ]
    return jnp.concatenate(pieces, axis=3).reshape(images * SIDE * SIDE, 9 * width)


def silu_slope(value):
    sigma = jax.nn.sigmoid(value)
    return sigma * (1.0 + value * (1.0 - sigma))


def norm_forward(hidden, weights, params):
    sums, squares, count = lax.psum(
        (
            jnp.sum(hidden * weights, axis=1),
            jnp.sum(hidden * hidden * weights, axis=1),
            jnp.sum(weights, axis=1),
        ),
        "dp",
    )
    center = sums / count
    scale = lax.rsqrt(squares / count - center * center + norm_eps)
    normed = (hidden - center[:, None]) * scale[:, None]
    return (params[0] * normed + params[1], normed, scale[:, None], count[:, None])


def norm_backward(upstream, normed, scale, count, weights, params):
    total, along = lax.psum((jnp.sum(upstream, axis=1), jnp.sum(upstream * normed, axis=1)), "dp")
    grad = (
        weights
        * params[0]
        * scale
        * (upstream - (total[:, None] + normed * along[:, None]) / count)
    )
    return (grad, jnp.stack([jnp.sum(along, axis=0), jnp.sum(total, axis=0)]))


def contract_rows(left, right):
    return lax.dot_general(
        left, right, (((0,), (0,)), ((), ())), preferred_element_type=jnp.float32
    )


def contract_cols(left, right):
    return lax.dot_general(
        left, right, (((1,), (1,)), ((), ())), preferred_element_type=jnp.float32
    )


def adam_step(weight, moment, second, grad, rate, decay):
    moment = beta_decay * moment + (1.0 - beta_decay) * grad
    second = beta_decay * second + (1.0 - beta_decay) * grad * grad
    correct = 1.0 - beta_decay**STEP
    weight = weight - rate * (
        moment / correct / (jnp.sqrt(second / correct) + adam_eps) + decay * weight
    )
    return (weight, moment, second)


def per_device(
    features,
    shortcut,
    valid_masks,
    labels,
    w_conv,
    w_proj,
    w_cls,
    cls_bias,
    norm_one,
    norm_two,
    conv_moment,
    conv_second,
    proj_moment,
    proj_second,
    cls_moment,
    cls_second,
    bias_moment,
    bias_second,
    one_moment,
    one_second,
    two_moment,
    two_second,
):
    images = valid_masks.shape[0]
    area = SIDE * SIDE
    pixels = images * area
    total_images = images * lax.axis_size("dp")
    classes = w_cls.shape[1]
    conv_full, proj_full, cls_full = (
        lax.all_gather(w_conv.astype(jnp.bfloat16), "dp", axis=0, tiled=True),
        lax.all_gather(w_proj.astype(jnp.bfloat16), "dp", axis=0, tiled=True),
        lax.all_gather(w_cls.astype(jnp.bfloat16), "dp", axis=0, tiled=True),
    )

    def split(flat):
        return flat.reshape((MICRO, -1) + flat.shape[1:])

    def join(parts):
        return parts.reshape((-1,) + parts.shape[2:])

    image_mask = valid_masks.astype(jnp.float32)
    pixel_counts = jnp.sum(image_mask, axis=1)
    weights = split(image_mask.reshape(pixels, 1))
    masked = features * join(weights).astype(jnp.bfloat16)
    gathered = lax.all_gather(masked, "chan", axis=1, tiled=True)
    columns = tap_columns(gathered, images)
    hidden = jnp.dot(columns, conv_full, preferred_element_type=jnp.float32)
    shifted, normed_one, scale_one, count = norm_forward(split(hidden), weights, norm_one)
    active = join((jax.nn.silu(shifted) * weights).astype(jnp.bfloat16))
    active_full = lax.all_gather(active, "chan", axis=1, tiled=True)
    second = jnp.dot(active_full, proj_full, preferred_element_type=jnp.float32)
    shifted_two, normed_two, scale_two, _ = norm_forward(split(second), weights, norm_two)
    summed = shifted_two + split(shortcut.astype(jnp.float32))
    output = jax.nn.silu(summed) * weights
    channels = shortcut.shape[1]
    pooled = (
        jnp.sum(output.reshape(images, area, channels), axis=1) / pixel_counts[:, None]
    ).astype(jnp.bfloat16)
    partial_value = jnp.dot(pooled, cls_full, preferred_element_type=jnp.float32)
    logits = lax.psum(partial_value, "chan") + cls_bias
    top = jnp.max(logits, axis=1, keepdims=True)
    expo = jnp.exp(logits - top)
    expo_sum = jnp.sum(expo, axis=1, keepdims=True)
    onehot = (labels[:, None] == jnp.arange(classes)[None, :]).astype(jnp.float32)
    picked = jnp.sum(logits * onehot, axis=1)
    loss_sum = jnp.sum(top[:, 0] + jnp.log(expo_sum[:, 0]) - picked)
    dlogits = ((expo / expo_sum - onehot) / total_images).astype(jnp.bfloat16)
    grad_bias = jnp.sum(dlogits.astype(jnp.float32), axis=0)
    local_cls = contract_rows(pooled, dlogits)
    grad_pool = contract_cols(dlogits, cls_full)
    spread_back = jnp.broadcast_to(
        (grad_pool / pixel_counts[:, None])[:, None, :], (images, area, channels)
    ).reshape(MICRO, -1, channels)
    upstream_two = spread_back * weights * silu_slope(summed)
    grad_second, grad_two = norm_backward(
        upstream_two, normed_two, scale_two, count, weights, norm_two
    )
    grad_second = join(grad_second.astype(jnp.bfloat16))
    local_proj = contract_rows(active_full, grad_second)
    partial_act = contract_cols(grad_second, proj_full)
    grad_active = lax.psum_scatter(
        partial_act.astype(jnp.bfloat16), "chan", scatter_dimension=1, tiled=True
    ).astype(jnp.float32)
    upstream_one = split(grad_active) * weights * silu_slope(shifted)
    grad_hidden, grad_one = norm_backward(
        upstream_one, normed_one, scale_one, count, weights, norm_one
    )
    local_conv = contract_rows(columns, join(grad_hidden.astype(jnp.bfloat16)))
    sum_conv, sum_proj, sum_cls = (
        lax.psum_scatter(
            local_conv.astype(jnp.bfloat16), "dp", scatter_dimension=0, tiled=True
        ).astype(jnp.float32),
        lax.psum_scatter(
            local_proj.astype(jnp.bfloat16), "dp", scatter_dimension=0, tiled=True
        ).astype(jnp.float32),
        lax.psum_scatter(
            local_cls.astype(jnp.bfloat16), "dp", scatter_dimension=0, tiled=True
        ).astype(jnp.float32),
    )
    loss_total, bias_total = lax.psum((loss_sum, grad_bias), "dp")
    train_loss = loss_total / total_images
    conv_w, conv_m, conv_v = adam_step(
        w_conv, conv_moment, conv_second, sum_conv, rate_matrix, weight_decay
    )
    proj_w, proj_m, proj_v = adam_step(
        w_proj, proj_moment, proj_second, sum_proj, rate_matrix, weight_decay
    )
    cls_w, cls_m, cls_v = adam_step(
        w_cls, cls_moment, cls_second, sum_cls, rate_matrix, weight_decay
    )
    bias_w, bias_m, bias_v = adam_step(
        cls_bias, bias_moment, bias_second, bias_total, rate_small, 0.0
    )
    one_w, one_m, one_v = adam_step(norm_one, one_moment, one_second, grad_one, rate_small, 0.0)
    two_w, two_m, two_v = adam_step(norm_two, two_moment, two_second, grad_two, rate_small, 0.0)
    return (
        conv_w,
        conv_m,
        conv_v,
        proj_w,
        proj_m,
        proj_v,
        cls_w,
        cls_m,
        cls_v,
        bias_w,
        bias_m,
        bias_v,
        one_w,
        one_m,
        one_v,
        two_w,
        two_m,
        two_v,
        conv_w.astype(jnp.bfloat16),
        proj_w.astype(jnp.bfloat16),
        cls_w.astype(jnp.bfloat16),
        train_loss,
    )


MESH = pl.DeviceIdType.MESH
AREA = SIDE * SIDE
PAD = 16
BF = jnp.bfloat16
F32 = jnp.float32


def flip(value, bits):
    bit = 1
    while bit <= bits:
        if bits & bit:
            value = value + bit - 2 * bit * (lax.div(value, bit) % 2)
        bit *= 2
    return value


def nt_dot(left, right):
    return lax.dot_general(left, right, (((1,), (1,)), ((), ())), preferred_element_type=F32)


def mm(left, right):
    return jnp.dot(left, right, preferred_element_type=F32)


def sigmoid(value):
    return 1.0 / (1.0 + jnp.exp(-value))


def row_iota(shape):
    return lax.broadcasted_iota(jnp.int32, shape, 0)


def lane_iota(shape):
    return lax.broadcasted_iota(jnp.int32, shape, 1)


def fused_kernel(dims, *refs):
    nd, nc, pm, imb, c1l, c2l, r1, rp, rc, classes, total_images = dims
    (
        feat, short, masks_in, labels, wconv, wproj, wcls, cbias_in, n1_in, n2_in, out,
        gout, masks, cbias, n1, n2, wf, pf, cf, wfull, pfull, cfull, xv, sv, xm, xt, yb, hid, mk, edge, cntm, cnti,
        af, at, sec, slp, bn1, bn2, tsum, pool, lgt, dlm, dpd, dsb, da, dab, sr, es, er,
        du, dhp, acc, pacc, st1, st2, st3, st4,
        gcs, gcx, gcz, gcr, gps, gpx, gpz, gpr, dla, plt,
        ld_s, cw_s, cw_r, pw_s, pw_r, kw_s, kw_r, dl_s, dl_r, fx_s, fx_r, af_s, af_r, st_s, st_r,
        lg_s, lg_r, sr_s, sr_r, er_s, er_r, gc_s, gc_r, gp_s, gp_r,
    ) = refs
    nz = nd // 2
    c1 = c1l * nc
    nq = c2l // 128
    d = lax.axis_index("dp")
    c = lax.axis_index("chan")
    z, x = lax.div(d, 2), d % 2
    y, k = lax.div(c, 2), c % 2
    sib = y * 2 + 1 - k
    opp = (1 - y) * 2 + k
    dia = (1 - y) * 2 + 1 - k
    xdev = (z * 2 + 1 - x, c)
    sibdev = (d, sib)
    oppdev = (d, opp)

    def zdev(j):
        return (flip(z, j) * 2 + x, c)

    def remote(src, dst, ssem, rsem, dev):
        return pltpu.make_async_remote_copy(
            src_ref=src, dst_ref=dst, send_sem=ssem, recv_sem=rsem,
            device_id=dev, device_id_type=MESH,
        )

    def unit(buf, u, rows):
        return buf.at[pl.ds(pl.multiple_of(u * rows, rows), rows)]

    leftdev = ((z + nz - 1) % nz * 2 + x, c)
    rightdev = ((z + 1) % nz * 2 + x, c)
    has_left = lax.div(z + nz - 1, nz)
    has_right = 1 - lax.div(z + 1, nz)

    def gather_pieces(buf, rr, u):
        pieces = rr.shape[1]
        size = buf.shape[0] // (nd * pieces)
        for h in range(pieces):
            first = pl.multiple_of(u * (size * pieces) + h * size, size)
            yield buf.at[pl.ds(first, size)], rr.at[lax.div(u, 2), h]

    def gather_across(buf, ss, rr):
        for mine, _ in gather_pieces(buf, rr, d):
            remote(mine, mine, ss.at[0], rr.at[nz, 0], xdev).start()

    def gather_along(buf, ss, rr):
        for mine, arrived in gather_pieces(buf, rr, d):
            @pl.when(has_left > 0)
            def go_left():
                remote(mine, mine, ss.at[1], arrived, leftdev).start()

            @pl.when(has_right > 0)
            def go_right():
                remote(mine, mine, ss.at[2], arrived, rightdev).start()

    outer = 1 - has_left * has_right

    def gather_far(buf, ss, rr):
        if nz == 4:
            for mine, arrived in gather_pieces(buf, rr, d):
                @pl.when(outer > 0)
                def go_far():
                    remote(mine, mine, ss.at[3], arrived, zdev(3)).start()

    def gather_step(buf, ss, rr, j, relay=True):
        if j >= nz:
            return

        def pass_on(got, arrived, onward, i, dev):
            remote(got, got, ss.at[0], arrived, xdev).wait_recv()
            remote(got, got, ss.at[0], rr.at[nz, 0], xdev).start()

            if relay:
                @pl.when(onward > 0)
                def go_on():
                    remote(got, got, ss.at[i], arrived, dev).start()

        from_left = gather_pieces(buf, rr, (z + nz - j) % nz * 2 + x)
        from_right = gather_pieces(buf, rr, (z + j) % nz * 2 + x)
        for one, two in zip(from_left, from_right):
            @pl.when(z >= j)
            def left():
                pass_on(*one, has_right, 2, rightdev)

            @pl.when(z + j < nz)
            def right():
                pass_on(*two, has_left, 1, leftdev)

    def gather_finish(buf, ss, rr):
        got = buf.at[pl.ds(0, buf.shape[0] // 2)]
        remote(got, got, ss.at[0], rr.at[nz, 0], xdev).wait_recv()

    def gather_drain(buf, ss, rr, far=False):
        def sent(i, units):
            some = buf.at[pl.ds(0, buf.shape[0] // nd * units)]
            remote(some, some, ss.at[i], rr.at[nz, 0], xdev).wait_send()

        sent(0, nz)
        for q in range(nz):
            @pl.when(z == q)
            def mine(q=q):
                if q > 0:
                    sent(1, min(nz - q, 2) if far else nz - q)
                if q < nz - 1:
                    sent(2, min(q + 1, 2) if far else q + 1)
                if far and nz == 4 and q in (0, nz - 1):
                    sent(3, 1)

    def stats_send(buf, ss, rr):
        for p in reversed(range(1, nd)):
            remote(buf.at[0], buf.at[p], ss, rr, (flip(d, p), c)).start()

    def stats_wait(buf, ss, rr):
        got = buf.at[pl.ds(1, nd - 1)]
        remote(got, got, ss, rr, xdev).wait_recv()

    def stats_sum(buf):
        total = buf[d]
        for u in range(1, nd):
            total = total + buf[flip(d, u)]
        return total

    def stats_drain(buf, ss, rr):
        sent = buf.at[:, pl.ds(1, nd - 1)]
        remote(sent, sent, ss, rr, xdev).wait_send()

    def rows(m):
        return pl.ds(pl.multiple_of(m * pm, pm), pm)

    def lanes(chunk):
        return pl.ds(pl.multiple_of(chunk * c1l, c1l), c1l)

    def part(buf, m, chunk):
        return buf.at[rows(m), lanes(chunk)]

    def local(src, dst, i):
        return pltpu.make_async_copy(src, dst, ld_s.at[i])

    loads = [
        local(wconv, wf, 0),
        local(wproj, pf, 1),
        local(wcls, cf, 2),
        local(feat, xv.at[:, lanes(c)], 3),
        local(short, sv, 4),
        local(masks_in, masks, 5),
        local(cbias_in, cbias, 6),
        local(n1_in, n1, 7),
        local(n2_in, n2, 8),
    ]
    loads[0].start()

    barrier = pltpu.get_barrier_semaphore()
    for dev in (sibdev, oppdev, xdev):
        pl.semaphore_signal(barrier, inc=1, device_id=dev, device_id_type=MESH)

    @pl.when(has_left > 0)
    def greet_left():
        pl.semaphore_signal(barrier, inc=1, device_id=leftdev, device_id_type=MESH)

    @pl.when(has_right > 0)
    def greet_right():
        pl.semaphore_signal(barrier, inc=1, device_id=rightdev, device_id_type=MESH)

    for i in (1, 2, 5, 3, 4, 6, 7, 8):
        loads[i].start()
    loads[0].wait()
    wfull[pl.ds(pl.multiple_of(d * r1, r1), r1), :] = wf[...].astype(BF)
    pl.semaphore_wait(barrier, 3 + has_left + has_right)

    gather_across(wfull, cw_s, cw_r)
    gather_along(wfull, cw_s, cw_r)
    for m in range(MICRO):
        src = feat.at[pl.ds(m * pm, pm)]
        remote(src, part(xv, m, c), fx_s, fx_r.at[0, m], oppdev).start()
        remote(src, part(xv, m, c), fx_s, fx_r.at[1, m], sibdev).start()

    loads[1].wait()
    pfull[pl.ds(pl.multiple_of(d * rp, rp), rp), :] = pf[...].astype(BF)
    gather_across(pfull, pw_s, pw_r)
    loads[2].wait()
    cfull[pl.ds(pl.multiple_of(d * rc, rc), rc), :] = cf[...].astype(BF)

    pixel = row_iota((pm, 128))
    image = jnp.zeros((pm, 128), jnp.int32)
    for i in range(1, imb):
        image = image + (pixel >= AREA * i).astype(jnp.int32)
    pixel = pixel - AREA * image
    line = jnp.zeros((pm, 128), jnp.int32)
    for i in range(1, SIDE):
        line = line + (pixel >= SIDE * i).astype(jnp.int32)
    across = pixel - SIDE * line
    edge[0] = (line > 0).astype(F32)
    edge[1] = (line < SIDE - 1).astype(F32)
    edge[2] = (across > 0).astype(F32)
    edge[3] = (across < SIDE - 1).astype(F32)
    loads[5].wait()
    mask_bf = masks[...].astype(F32).astype(BF)
    images = imb * MICRO
    chosen = (pixel[:, :AREA] == lane_iota((pm, AREA))).astype(F32)
    ones = jnp.ones((AREA, 128), BF)
    image_count = jnp.sum(masks[...].astype(F32), axis=1, keepdims=True)
    for m in range(MICRO):
        away = row_iota((pm, images)) - AREA * (lane_iota((pm, images)) - imb * m)
        owner = jnp.where((away >= 0) & (away < AREA), 1.0, 0.0).astype(BF)
        spread = mm((mm(owner, mask_bf) * chosen).astype(BF), ones)
        mk[m] = spread
        cntm[m] = jnp.sum(spread, axis=0, keepdims=True)
        cnti[m] = jnp.broadcast_to(image_count[m * imb : (m + 1) * imb], (imb, 128))
        st1[m, 0, 2:3, :] = cntm[m]

    yb[:, 0:PAD, :] = jnp.zeros((9, PAD, c1l), F32)
    yb[:, PAD + pm :, :] = jnp.zeros((9, PAD, c1l), F32)
    dhp[0:PAD, :] = jnp.zeros((PAD, c1l), F32)
    dhp[PAD + pm :, :] = jnp.zeros((PAD, c1l), F32)

    def pass_features(m):
        got = part(xv, m, opp)
        remote(got, got, fx_s, fx_r.at[0, m], sibdev).wait_recv()
        remote(got, got, fx_s, fx_r.at[1, m], sibdev).start()

    def take_features(m, carry):
        got = xv.at[rows(m), pl.ds(0, 2 * c1l)]
        remote(got, got, fx_s, fx_r.at[1, m], sibdev).wait_recv()
        flat_mask = mk[m].astype(BF)
        for q in range(nc):
            piece = xv[rows(m), q * c1l : (q + 1) * c1l] * flat_mask
            xm[m, :, q * c1l : (q + 1) * c1l] = piece
            xt[m, q * c1l : (q + 1) * c1l, :] = piece.T
        return carry

    gather_step(wfull, cw_s, cw_r, 1)
    pass_features(0)
    gather_step(wfull, cw_s, cw_r, 2)
    gather_along(pfull, pw_s, pw_r)
    gather_far(pfull, pw_s, pw_r)
    pass_features(1)
    pass_features(2)
    loads[3].wait()
    loads[7].wait()
    gather_step(wfull, cw_s, cw_r, 3)
    gather_step(pfull, pw_s, pw_r, 1)
    pass_features(3)
    lax.fori_loop(0, MICRO, take_features, 0)
    gather_finish(wfull, cw_s, cw_r)

    def tap(t):
        return wfull[t * c1 : (t + 1) * c1, :]

    def edges(ky, kx):
        found = None
        if ky == 0:
            found = edge[0]
        if ky == 2:
            found = edge[1]
        if kx == 0:
            found = edge[2] if found is None else found * edge[2]
        if kx == 2:
            found = edge[3] if found is None else found * edge[3]
        return found

    def conv(m, carry):
        inputs = xm[m]
        for t in range(0, 9, 2):
            if t < 8:
                pair = mm(inputs, jnp.concatenate([tap(t), tap(t + 1)], axis=1))
                yb[t, PAD : PAD + pm, :] = pair[:, :c1l]
                yb[t + 1, PAD : PAD + pm, :] = pair[:, c1l:]
            else:
                yb[t, PAD : PAD + pm, :] = mm(inputs, tap(t))
        hidden = None
        for kx in range(3):
            column = None
            for ky in range(3):
                off = PAD + (ky - 1) * SIDE + kx - 1
                value = yb[3 * ky + kx, off : off + pm, :]
                if ky != 1:
                    value = value * edge[0 if ky == 0 else 1]
                column = value if column is None else column + value
            if kx != 1:
                column = column * edge[2 if kx == 0 else 3]
            hidden = column if hidden is None else hidden + column
        hid[m] = hidden
        valid = hidden * mk[m]
        st1[m, 0, 0:1, :] = jnp.sum(valid, axis=0, keepdims=True)
        st1[m, 0, 1:2, :] = jnp.sum(valid * hidden, axis=0, keepdims=True)
        stats_send(st1.at[m], st_s.at[0], st_r.at[0, m])

        @pl.when(m == 2)
        def bulk_at_2():
            gather_step(pfull, pw_s, pw_r, 3)
            gather_step(pfull, pw_s, pw_r, 2, False)

        @pl.when(m == 3)
        def bulk_at_3():
            gather_along(cfull, kw_s, kw_r)
            gather_across(cfull, kw_s, kw_r)
            gather_far(cfull, kw_s, kw_r)

        return carry

    lax.fori_loop(0, MICRO, conv, 0)
    acc[...] = jnp.zeros_like(acc)
    pacc[...] = jnp.zeros_like(pacc)

    def activate(m, carry):
        stats_wait(st1.at[m], st_s.at[0], st_r.at[0, m])
        totals = stats_sum(st1.at[m])
        n = totals[2:3]
        cntm[m] = n
        center = totals[0:1] / n
        bn1[m, 0:1, :] = center
        bn1[m, 1:2, :] = lax.rsqrt(totals[1:2] / n - center * center + norm_eps)
        normed = (hid[m] - bn1[m, 0:1, :]) * bn1[m, 1:2, :]
        shifted = n1[0:1, :] * normed + n1[1:2, :]
        active = (shifted * sigmoid(shifted) * mk[m]).astype(BF)
        mine = part(af, m, c)
        mine[...] = active
        remote(mine, mine, af_s, af_r.at[0, m], oppdev).start()
        remote(mine, mine, af_s, af_r.at[1, m], sibdev).start()
        return carry

    activate(0, 0)
    lax.fori_loop(1, MICRO, activate, 0)
    gather_step(cfull, kw_s, kw_r, 1)
    gather_step(cfull, kw_s, kw_r, 3)
    gather_finish(pfull, pw_s, pw_r)
    loads[4].wait()
    loads[6].wait()
    loads[8].wait()

    def turn(m, chunk):
        at[m, lanes_sub(chunk), :] = part(af, m, chunk)[...].T

    def lanes_sub(chunk):
        return pl.ds(pl.multiple_of(chunk * c1l, c1l), c1l)

    def stage_a(m):
        got = part(af, m, opp)
        remote(got, got, af_s, af_r.at[0, m], sibdev).wait_recv()
        remote(got, got, af_s, af_r.at[1, m], sibdev).start()
        turn(m, c)
        turn(m, opp)
        got = af.at[rows(m), pl.ds(0, 2 * c1l)]
        remote(got, got, af_s, af_r.at[1, m], sibdev).wait_recv()
        turn(m, sib)
        turn(m, dia)
        second = mm(af[rows(m), :], pfull[...])
        sec[m] = second
        mask = mk[m]
        for q in range(nq):
            piece = second[:, q * 128 : (q + 1) * 128]
            valid = piece * mask
            st2[m, 0, q : q + 1, :] = jnp.sum(valid, axis=0, keepdims=True)
            st2[m, 0, nq + q : nq + q + 1, :] = jnp.sum(valid * piece, axis=0, keepdims=True)
        stats_send(st2.at[m], st_s.at[1], st_r.at[1, m])

    low_half = row_iota((2, 8, 128)) * 0 + lax.broadcasted_iota(jnp.int32, (2, 8, 128), 1)
    tiles = AREA // 4
    half = tiles // 2

    def image_sums(value):
        value = value.reshape(imb // 2, tiles, 8, 128)
        middle = value[:, half]
        first = jnp.sum(value[:, :half], axis=1) + jnp.where(low_half < 4, middle, 0.0)
        last = jnp.sum(value[:, half + 1 :], axis=1) + jnp.where(low_half < 4, 0.0, middle)
        first = jnp.sum(first, axis=1)
        last = jnp.sum(last, axis=1)
        found = []
        for i in range(imb // 2):
            found += [first[i : i + 1], last[i : i + 1]]
        return jnp.concatenate(found, axis=0)

    def image_spread(value):
        pieces = []
        for i in range(imb // 2):
            first = jnp.broadcast_to(value[2 * i : 2 * i + 1], (8, 128))
            last = jnp.broadcast_to(value[2 * i + 1 : 2 * i + 2], (8, 128))
            middle = jnp.where(low_half[0] < 4, first, last)
            pieces.append(jnp.broadcast_to(first[None], (half, 8, 128)))
            pieces.append(middle[None])
            pieces.append(jnp.broadcast_to(last[None], (half, 8, 128)))
        return jnp.concatenate(pieces, axis=0).reshape(pm, 128)

    def stage_b(m):
        stats_wait(st2.at[m], st_s.at[1], st_r.at[1, m])
        total = stats_sum(st2.at[m])
        n = cntm[m]
        mask = mk[m]
        for q in range(nq):
            at_q = slice(q * 128, (q + 1) * 128)
            center = total[q : q + 1] / n
            spread = total[nq + q : nq + q + 1] / n - center * center
            scale = lax.rsqrt(spread + norm_eps)
            bn2[m, 0:1, at_q] = scale
            normed = (sec[m, :, at_q] - center) * scale
            sec[m, :, at_q] = normed
            summed = n2[0:1, at_q] * normed + n2[1:2, at_q]
            summed = summed + sv[rows(m), at_q].astype(F32)
            sigma = sigmoid(summed)
            slope = sigma * (1.0 + summed * (1.0 - sigma)) * mask
            slp[m, :, at_q] = slope
            pool[m, :, at_q] = (image_sums(summed * sigma * mask) / cnti[m]).astype(BF).astype(F32)
            tsum[m, 0, :, at_q] = image_sums(slope)
            tsum[m, 1, :, at_q] = image_sums(slope * normed)

    def stage_l(m):
        lgt[m, c] = mm(pool[m].astype(BF), cfull[...])
        for dev in (oppdev, (d, dia), sibdev):
            remote(lgt.at[m, c], lgt.at[m, c], lg_s, lg_r.at[m], dev).start()

    def stage_c(m):
        got = lgt.at[m, pl.ds(0, nc - 1)]
        remote(got, got, lg_s, lg_r.at[m], sibdev).wait_recv()
        logits = lgt[m, 0]
        for q in range(1, nc):
            logits = logits + lgt[m, q]
        logits = logits + cbias[...]
        top = jnp.max(logits, axis=1, keepdims=True)
        expo = jnp.exp(logits - top)
        expo_sum = jnp.sum(expo, axis=1, keepdims=True)
        image_row = row_iota((imb, classes))
        target = jnp.zeros((imb, classes), jnp.int32)
        for i in range(imb):
            target = jnp.where(image_row == i, labels[m * imb + i], target)
        onehot = (target == lane_iota((imb, classes))).astype(F32)
        picked = jnp.sum(logits * onehot, axis=1, keepdims=True)
        loss = jnp.sum(top + jnp.log(expo_sum) - picked, axis=0, keepdims=True)
        st4[m, 0, 2:3, :] = jnp.broadcast_to(loss, (1, 128))
        dlogits = ((expo / expo_sum - onehot) / total_images).astype(BF)
        dlm[m] = dlogits.astype(F32)
        spread = nt_dot(dlogits, cfull[...])
        for q in range(nq):
            at_q = slice(q * 128, (q + 1) * 128)
            value = spread[:, at_q] / cnti[m]
            dpd[m, :, at_q] = value
            st3[m, 0, q : q + 1, :] = jnp.sum(value * tsum[m, 0, :, at_q], axis=0, keepdims=True)
            st3[m, 0, nq + q : nq + q + 1, :] = jnp.sum(
                value * tsum[m, 1, :, at_q], axis=0, keepdims=True
            )
        stats_send(st3.at[m], st_s.at[2], st_r.at[2, m])

    def stage_d(m):
        stats_wait(st3.at[m], st_s.at[2], st_r.at[2, m])
        total = stats_sum(st3.at[m])
        n = cntm[m]
        mask = mk[m]
        for q in range(nq):
            at_q = slice(q * 128, (q + 1) * 128)
            gain = n2[0:1, at_q] * bn2[m, 0:1, at_q]
            base = gain * total[q : q + 1] / n
            ramp = gain * total[nq + q : nq + q + 1] / n
            value = image_spread(gain * dpd[m, :, at_q]) * slp[m, :, at_q]
            value = value - mask * (base + ramp * sec[m, :, at_q])
            dsb[:, at_q] = value.astype(BF)
        for q in range(nq):
            at_q = slice(q * 128, (q + 1) * 128)
            bn2[m, 1:2, at_q] = total[nq + q : nq + q + 1]
            bn2[m, 2:3, at_q] = total[q : q + 1]
        back = nt_dot(dsb[...], pfull[...])
        for q in range(nc):
            piece = back[:, q * c1l : (q + 1) * c1l]
            da[m, q % 2, q // 2] = piece
            dab[m, q % 2, q // 2] = piece.astype(BF)
        remote(dab.at[m, 1 - k], sr.at[m], sr_s, sr_r.at[m], sibdev).start()
        pacc[...] += mm(at[m], dsb[...])

    def stage_e(m):
        remote(sr.at[m], sr.at[m], sr_s, sr_r.at[m], sibdev).wait_recv()
        es[m] = (da[m, k, 1 - y] + sr[m, 1 - y].astype(F32)).astype(BF)
        remote(es.at[m], er.at[m], er_s, er_r.at[m], oppdev).start()

    def stage_f(m):
        remote(es.at[m], er.at[m], er_s, er_r.at[m], oppdev).wait_recv()
        upstream = da[m, k, y] + sr[m, y].astype(F32) + er[m].astype(F32)
        normed = (hid[m] - bn1[m, 0:1, :]) * bn1[m, 1:2, :]
        shifted = n1[0:1, :] * normed + n1[1:2, :]
        sigma = sigmoid(shifted)
        upstream = upstream * mk[m] * (sigma * (1.0 + shifted * (1.0 - sigma)))
        du[m] = upstream
        st4[m, 0, 0:1, :] = jnp.sum(upstream, axis=0, keepdims=True)
        st4[m, 0, 1:2, :] = jnp.sum(upstream * normed, axis=0, keepdims=True)
        stats_send(st4.at[m], st_s.at[3], st_r.at[3, m])

    def stage_g(m):
        stats_wait(st4.at[m], st_s.at[3], st_r.at[3, m])
        total = stats_sum(st4.at[m])
        n = cntm[m]
        bn1[m, 2:3, :] = total[1:2]
        bn1[m, 3:4, :] = total[0:1]
        bn1[m, 4:5, :] = total[2:3]
        normed = (hid[m] - bn1[m, 0:1, :]) * bn1[m, 1:2, :]
        gain = n1[0:1, :] * bn1[m, 1:2, :]
        value = mk[m] * gain * (du[m] - (total[0:1] + normed * total[1:2]) / n)
        dhp[PAD : PAD + pm, :] = value.astype(BF).astype(F32)

        def shifted(t):
            ky, kx = t // 3, t % 3
            off = PAD - (ky - 1) * SIDE - (kx - 1)
            piece = dhp[off : off + pm, :]
            found = edges(2 - ky, 2 - kx)
            return (piece if found is None else piece * found).astype(BF)

        left = xt[m]
        for t in range(0, 9, 2):
            if t < 8:
                pair = mm(left, jnp.concatenate([shifted(t), shifted(t + 1)], axis=1))
                acc[t * c1 : (t + 1) * c1, :] += pair[:, :c1l]
                acc[(t + 1) * c1 : (t + 2) * c1, :] += pair[:, c1l:]
            else:
                acc[t * c1 : (t + 1) * c1, :] += mm(left, shifted(t))

    orders = [2, 3, 1, 0] if nz == 4 else list(range(nz))

    def scatter_pieces(rr):
        return (rr.shape[0] - 4) // nz

    def scatter_start(total, sbuf, xbuf, ss, rr, js=orders):
        height = sbuf.shape[1]
        size = height // scatter_pieces(rr)
        for j in js:
            u = flip(z, j) * 2 + 1 - x
            for h in range(height // size):
                at_h = pl.ds(h * size, size)
                first = pl.multiple_of(u * height + h * size, size)
                sbuf[j, at_h] = total[pl.ds(first, size), :].astype(BF)
                remote(
                    sbuf.at[j, at_h], xbuf.at[j, at_h], ss.at[0],
                    rr.at[4 + j * (height // size) + h], xdev,
                ).start()

    def scatter_middle(total, xbuf, zbuf, rbuf, ss, rr, js, keep):
        height = xbuf.shape[1]
        pieces = scatter_pieces(rr)
        size = height // pieces
        for j in js:
            u = flip(z, j) * 2 + x
            for h in range(pieces):
                at_h = pl.ds(h * size, size)
                got = xbuf.at[j, at_h]
                remote(got, got, ss.at[0], rr.at[4 + j * pieces + h], xdev).wait_recv()
                first = pl.multiple_of(u * height + h * size, size)
                found = total[pl.ds(first, size), :] + got[...].astype(F32)
                if j == 0:
                    keep(h * size, found)
                    continue
                mine = zbuf.at[j, at_h]
                if j == 2:
                    mine[...] = found.astype(BF)

                    @pl.when(outer > 0)
                    def out_in():
                        to = rbuf.at[2, at_h]
                        remote(mine, to, ss.at[1], rr.at[2], zdev(1)).start()

                    @pl.when(outer == 0)
                    def in_in():
                        to = rbuf.at[0, at_h]
                        remote(mine, to, ss.at[1], rr.at[0], zdev(3)).start()

                    continue
                slot = 2 if j == 3 else 0

                @pl.when(outer > 0)
                def plain():
                    mine[...] = found.astype(BF)

                @pl.when(outer == 0)
                def added():
                    if h == 0:
                        relay = rbuf.at[slot]
                        remote(relay, relay, ss.at[1], rr.at[slot], xdev).wait_recv()
                    mine[...] = (found + rbuf[slot, at_h].astype(F32)).astype(BF)

                remote(mine, rbuf.at[j, at_h], ss.at[1], rr.at[j], zdev(j)).start()

    def scatter_wait(rbuf, ss, rr):
        if nz == 4:
            for j in (3, 1):
                remote(rbuf.at[j], rbuf.at[j], ss.at[1], rr.at[j], xdev).wait_recv()

    def scatter_drain(sbuf, zbuf, ss, rr):
        remote(sbuf, sbuf, ss.at[0], rr.at[0], xdev).wait_send()
        if nz > 1:
            sent = zbuf.at[pl.ds(1, nz - 1)]
            remote(sent, sent, ss.at[1], rr.at[0], xdev).wait_send()

    def cls_rows(u):
        return pl.ds(pl.multiple_of(u * images, images), images)

    wide = dla.shape[1] - c2l

    def share_cls():
        mine = jnp.concatenate([dlm[q] for q in range(MICRO)], axis=0).astype(BF)
        dla[cls_rows(d), 0:classes] = mine
        if wide > classes:
            dla[cls_rows(d), classes:wide] = jnp.zeros((images, wide - classes), BF)
        mine = jnp.concatenate([pool[q] for q in range(MICRO)], axis=0).astype(BF)
        dla[cls_rows(d), wide:] = mine
        gather_across(dla, dl_s, dl_r)
        gather_along(dla, dl_s, dl_r)

    def start_proj(j):
        if j < nz:
            scatter_start(pacc, gps, gpx, gp_s, gp_r, [j])

    def middle_proj(js):
        def keep(first, value):
            for q in range(nq):
                row = r1 + q * rp + first
                gout[row : row + value.shape[0], :] = value[:, q * 128 : (q + 1) * 128]

        scatter_middle(pacc, gpx, gpz, gpr, gp_s, gp_r, js, keep)

    def finish_cls():
        gather_finish(cfull, kw_s, kw_r)

    offsets = dict(a=0, b=2, l=3, c=5, d=8, e=9, f=11, g=13)
    stages = dict(
        a=stage_a, b=stage_b, l=stage_l, c=stage_c, d=stage_d, e=stage_e, f=stage_f, g=stage_g
    )
    def at_a0():
        gather_step(cfull, kw_s, kw_r, 2, False)

    hooks = {
        (0, "a"): at_a0,
        (3, "a"): finish_cls,
        (8, "c"): share_cls,
        (10, "d"): lambda: gather_step(dla, dl_s, dl_r, 1),
        (11, "f"): lambda: start_proj(2),
        (12, "e"): lambda: gather_step(dla, dl_s, dl_r, 2),
        (12, "f"): lambda: start_proj(3),
        (13, "f"): lambda: start_proj(1),
        (14, "g"): lambda: gather_step(dla, dl_s, dl_r, 3),
        (14, "f"): lambda: start_proj(0),
        (16, "b"): lambda: middle_proj(orders[:1]),
    }

    def step(s, carry):
        for name in "alcbedfg":
            i = offsets[name]

            @pl.when((s >= i) & (s < i + MICRO))
            def run(name=name, i=i):
                stages[name](s - i)

            for (when, after), hook in hooks.items():
                if after == name:

                    @pl.when(s == when)
                    def extra(hook=hook):
                        hook()

        return carry

    lax.fori_loop(0, MICRO + offsets["g"], step, 0)

    scatter_start(acc, gcs, gcx, gc_s, gc_r)
    middle_proj(orders[1:])

    gather_finish(dla, dl_s, dl_r)
    plt[...] = dla[:, wide:].T
    left = plt[pl.ds(pl.multiple_of(d * rc, rc), rc), :]
    row = r1 + nq * rp
    share = mm(left, dla[:, 0:wide])
    for q in range(wide // 128):
        gout[row + q * rc : row + (q + 1) * rc, :] = share[:, q * 128 : (q + 1) * 128]
    row = row + wide // 128 * rc
    share = jnp.sum(dla[:, 0:wide].astype(F32), axis=0, keepdims=True)
    for q in range(wide // 128):
        gout[row + q : row + q + 1, :] = share[:, q * 128 : (q + 1) * 128]
    row = row + wide // 128
    share = bn2[0, 1:3, :] + bn2[1, 1:3, :] + bn2[2, 1:3, :] + bn2[3, 1:3, :]
    for q in range(nq):
        gout[row + 2 * q : row + 2 * q + 2, :] = share[:, q * 128 : (q + 1) * 128]
    row = row + 2 * nq
    gout[row : row + 2, :] = bn1[0, 2:4, :] + bn1[1, 2:4, :] + bn1[2, 2:4, :] + bn1[3, 2:4, :]
    loss = bn1[0, 4:5, :] + bn1[1, 4:5, :] + bn1[2, 4:5, :] + bn1[3, 4:5, :]
    gout[row + 2 : row + 3, :] = loss / total_images
    row = row + 3
    if row < gout.shape[0]:
        gout[row:, :] = jnp.zeros((gout.shape[0] - row, 128), F32)
    def keep_conv(first, value):
        gout[first : first + value.shape[0], :] = value

    def middle_conv(js):
        scatter_middle(acc, gcx, gcz, gcr, gc_s, gc_r, js, keep_conv)

    middle_conv(orders[:1])
    scatter_wait(gpr, gp_s, gp_r)
    if nz == 4:
        for q in range(nq):
            at_q = slice(q * 128, (q + 1) * 128)
            share = gpr[1, :, at_q].astype(F32) + gpr[3, :, at_q].astype(F32)
            gout[r1 + q * rp : r1 + (q + 1) * rp, :] += share
    rest = gout.shape[0] - r1
    small_out = local(gout.at[pl.ds(r1, rest)], out.at[pl.ds(r1, rest)], 9)
    small_out.start()
    middle_conv(orders[1:])
    scatter_wait(gcr, gc_s, gc_r)
    if nz == 4:
        gout[0:r1, :] += gcr[1].astype(F32) + gcr[3].astype(F32)

    conv_out = local(gout.at[pl.ds(0, r1)], out.at[pl.ds(0, r1)], 10)
    conv_out.start()
    gather_drain(wfull, cw_s, cw_r)
    gather_drain(pfull, pw_s, pw_r, True)
    gather_drain(cfull, kw_s, kw_r, True)
    gather_drain(dla, dl_s, dl_r)
    scatter_drain(gps, gpz, gp_s, gp_r)
    scatter_drain(gcs, gcz, gc_s, gc_r)
    sent = xv.at[:, pl.ds(0, 3 * c1l)]
    remote(sent, sent, fx_s, fx_r.at[0, 0], sibdev).wait_send()
    sent = af.at[:, pl.ds(0, 3 * c1l)]
    remote(sent, sent, af_s, af_r.at[0, 0], sibdev).wait_send()
    sent = lgt.at[pl.ds(0, nc - 1)]
    remote(sent, sent, lg_s, lg_r.at[0], sibdev).wait_send()
    remote(sr, sr, sr_s, sr_r.at[0], sibdev).wait_send()
    remote(es, es, er_s, er_r.at[0], oppdev).wait_send()

    for i, buf in enumerate((st1, st2, st3, st4)):
        stats_drain(buf, st_s.at[i], st_r.at[i, 0])
    small_out.wait()
    conv_out.wait()


def fused_gradients(
    features, shortcut, valid_masks, labels, w_conv, w_proj, w_cls, cls_bias, norm_one, norm_two
):
    nd, nc = lax.axis_size("dp"), lax.axis_size("chan")
    nz = nd // 2
    pixels, c1l = features.shape
    c2l = shortcut.shape[1]
    images = valid_masks.shape[0]
    imb, pm = images // MICRO, pixels // MICRO
    r1, rp, rc = w_conv.shape[0], w_proj.shape[0], w_cls.shape[0]
    classes = w_cls.shape[1]
    c1 = c1l * nc
    nq = c2l // 128
    wide = -(-classes // 128) * 128
    grad_rows = r1 + nq * rp + wide // 128 * (rc + 1) + 2 * nq + 3
    grad_rows = -(-grad_rows // 8) * 8
    dims = (nd, nc, pm, imb, c1l, c2l, r1, rp, rc, classes, images * nd)
    vmem = pltpu.VMEM
    dma = pltpu.SemaphoreType.DMA
    m4 = MICRO
    scratch = [
        vmem((grad_rows, 128), F32),
        vmem((images, SIDE * SIDE), jnp.int32), vmem((1, classes), F32),
        vmem((2, c1l), F32), vmem((2, c2l), F32),
        vmem((r1, c1l), F32), vmem((rp, c2l), F32), vmem((rc, classes), F32),
        vmem((9 * c1, c1l), BF), vmem((c1, c2l), BF), vmem((c2l, classes), BF),
        vmem((pixels, c1), BF), vmem((pixels, c2l), BF),
        vmem((m4, pm, c1), BF), vmem((m4, c1, pm), BF),
        vmem((9, PAD + pm + PAD, c1l), F32), vmem((m4, pm, c1l), F32), vmem((m4, pm, 128), F32),
        vmem((4, pm, 128), F32), vmem((m4, 1, 128), F32), vmem((m4, imb, 128), F32),
        vmem((pixels, c1), BF), vmem((m4, c1, pm), BF),
        vmem((m4, pm, c2l), F32), vmem((m4, pm, c2l), F32),
        vmem((m4, 8, c1l), F32), vmem((m4, 8, c2l), F32),
        vmem((m4, 2, imb, c2l), F32), vmem((m4, imb, c2l), F32),
        vmem((m4, nc, imb, classes), F32), vmem((m4, imb, classes), F32), vmem((m4, imb, c2l), F32),
        vmem((pm, c2l), BF), vmem((m4, 2, 2, pm, c1l), F32), vmem((m4, 2, 2, pm, c1l), BF),
        vmem((m4, 2, pm, c1l), BF), vmem((m4, pm, c1l), BF), vmem((m4, pm, c1l), BF),
        vmem((m4, pm, c1l), F32), vmem((PAD + pm + PAD, c1l), F32),
        vmem((9 * c1, c1l), F32), vmem((c1, c2l), F32),
        vmem((m4, nd, 8, c1l), F32),
        vmem((m4, nd, 2 * nq, 128), F32), vmem((m4, nd, 2 * nq, 128), F32),
        vmem((m4, nd, 8, c1l), F32),
        vmem((nz, r1, c1l), BF), vmem((nz, r1, c1l), BF),
        vmem((nz, r1, c1l), BF), vmem((nz, r1, c1l), BF),
        vmem((nz, rp, c2l), BF), vmem((nz, rp, c2l), BF),
        vmem((nz, rp, c2l), BF), vmem((nz, rp, c2l), BF),
        vmem((nd * images, wide + c2l), BF), vmem((c2l, nd * images), BF),
        dma((11,)),
        dma((4,)), dma((nz + 1, 3)), dma((4,)), dma((nz + 1, 1)), dma((4,)), dma((nz + 1, 2)),
        dma((4,)), dma((nz + 1, 1)),
        dma, dma((2, m4)), dma, dma((2, m4)), dma((4,)), dma((4, m4)),
        dma, dma((m4,)), dma, dma((m4,)), dma, dma((m4,)),
        dma((2,)), dma((4 + 4 * nz,)), dma((2,)), dma((4 + nz,)),
    ]
    whole = pl.BlockSpec(memory_space=pltpu.VMEM)
    hbm = pl.BlockSpec(memory_space=pl.ANY)
    scalar = pl.BlockSpec(memory_space=pltpu.SMEM)
    shape = jax.ShapeDtypeStruct
    return pl.pallas_call(
        functools.partial(fused_kernel, dims),
        out_shape=shape((grad_rows, 128), F32),
        in_specs=[hbm, hbm, hbm, scalar, hbm, hbm, hbm, hbm, hbm, hbm],
        out_specs=hbm,
        scratch_shapes=scratch,
        compiler_params=pltpu.CompilerParams(
            collective_id=0, has_side_effects=True, vmem_limit_bytes=58 * 1024 * 1024
        ),
    )(
        features, shortcut, valid_masks, labels, w_conv, w_proj, w_cls,
        cls_bias.reshape(1, classes), norm_one, norm_two,
    )


def adam_kernel(grads, *refs):
    states, results, outs, sent = refs[:18], refs[18:40], refs[40:62], refs[62]
    copies = []

    def send(i):
        copies.append(pltpu.make_async_copy(outs[i], results[i], sent.at[i]))
        copies[-1].start()

    row = 0
    for i, (rate, decay) in enumerate(ADAM_RATES):
        weight, moment, second = states[3 * i : 3 * i + 3]
        height, width = weight.shape
        for start in range(0, width, 128):
            size = min(128, width - start)
            at_q = slice(start, start + size)
            found = adam_step(
                weight[:, at_q], moment[:, at_q], second[:, at_q],
                grads[row : row + height, 0:size], rate, decay,
            )
            row += height
            for out, value in zip(outs[3 * i : 3 * i + 3], found):
                out[:, at_q] = value
            if i < 3:
                outs[18 + i][:, at_q] = found[0].astype(BF)
        for q in range(3 * i, 3 * i + 3):
            send(q)
        if i < 3:
            send(18 + i)
    outs[21][...] = grads[row : row + 1, :]
    send(21)
    for copy in copies:
        copy.wait()


ADAM_RATES = (
    (rate_matrix, weight_decay),
    (rate_matrix, weight_decay),
    (rate_matrix, weight_decay),
    (rate_small, 0.0),
    (rate_small, 0.0),
    (rate_small, 0.0),
)


def fused_device(
    features, shortcut, valid_masks, labels, w_conv, w_proj, w_cls, cls_bias, norm_one, norm_two,
    conv_moment, conv_second, proj_moment, proj_second, cls_moment, cls_second,
    bias_moment, bias_second, one_moment, one_second, two_moment, two_second,
):
    grads = fused_gradients(
        features, shortcut, valid_masks, labels, w_conv, w_proj, w_cls, cls_bias, norm_one, norm_two
    )
    states = (
        (w_conv, conv_moment, conv_second),
        (w_proj, proj_moment, proj_second),
        (w_cls, cls_moment, cls_second),
        (cls_bias.reshape(1, -1), bias_moment.reshape(1, -1), bias_second.reshape(1, -1)),
        (norm_two, two_moment, two_second),
        (norm_one, one_moment, one_second),
    )
    operands, outs = [], []
    for state in states:
        operands += list(state)
        outs += [jax.ShapeDtypeStruct(state[0].shape, F32)] * 3
    outs += [jax.ShapeDtypeStruct(state[0].shape, BF) for state in states[:3]]
    outs.append(jax.ShapeDtypeStruct((1, 128), F32))
    whole = pl.BlockSpec(memory_space=pltpu.VMEM)
    done = list(
        pl.pallas_call(
            adam_kernel,
            out_shape=tuple(outs),
            in_specs=[whole] * (len(operands) + 1),
            out_specs=(pl.BlockSpec(memory_space=pl.ANY),) * len(outs),
            scratch_shapes=[pltpu.VMEM(o.shape, o.dtype) for o in outs]
            + [pltpu.SemaphoreType.DMA((len(outs),))],
            compiler_params=pltpu.CompilerParams(vmem_limit_bytes=40 * 1024 * 1024),
        )(grads, *operands)
    )
    biases = [done[i].reshape(-1) for i in (9, 10, 11)]
    return tuple(done[:9] + biases + done[15:18] + done[12:15] + done[18:21]) + (done[21][0, 0],)


def run_device(*args):
    features, shortcut, valid_masks = args[:3]
    w_cls = args[6]
    fits = (
        lax.axis_size("chan") == 4
        and lax.axis_size("dp") in (2, 8)
        and features.shape[1] == 128
        and shortcut.shape[1] % 128 == 0
        and w_cls.shape[0] % 16 == 0
        and valid_masks.shape[0] % (4 * MICRO) == 0
    )
    return (fused_device if fits else per_device)(*args)


def solution(mesh):
    placed = (
        P("dp", "chan"),
        P("dp", "chan"),
        P("dp", None),
        P("dp"),
        P("dp", "chan"),
        P("dp", "chan"),
        P(("chan", "dp"), None),
        P(),
        P(None, "chan"),
        P(None, "chan"),
        P("dp", "chan"),
        P("dp", "chan"),
        P("dp", "chan"),
        P("dp", "chan"),
        P(("chan", "dp"), None),
        P(("chan", "dp"), None),
        P(),
        P(),
        P(None, "chan"),
        P(None, "chan"),
        P(None, "chan"),
        P(None, "chan"),
    )
    return jax.shard_map(
        run_device,
        mesh=mesh,
        in_specs=placed,
        out_specs=(
            P("dp", "chan"),
            P("dp", "chan"),
            P("dp", "chan"),
            P("dp", "chan"),
            P("dp", "chan"),
            P("dp", "chan"),
            P(("chan", "dp"), None),
            P(("chan", "dp"), None),
            P(("chan", "dp"), None),
            P(),
            P(),
            P(),
            P(None, "chan"),
            P(None, "chan"),
            P(None, "chan"),
            P(None, "chan"),
            P(None, "chan"),
            P(None, "chan"),
            P("dp", "chan"),
            P("dp", "chan"),
            P(("chan", "dp"), None),
            P(),
        ),
        check_vma=False,
    )
```
